32 devices in a mesh: section: 2 (over core), dp: 8 (over z, y), mp: 2 (over x).
Axes of the slice: x: 2, y: 2, z: 4, core: 2. Of those that a mesh axis runs over, the one named last changes fastest.
Arguments:
- block_input: bfloat16 [2, 1024, 768], P(None, ('dp', 'mp')), may hold values from -6 to 6
- out_cotangent: bfloat16 [2, 1024, 768], P(None, ('dp', 'mp')), may hold values from -6 to 6
- seq_starts: int32 [2, 8, 2], P(None, 'dp'), may hold values from 0 to 128, as said below
- seq_lengths: int32 [2, 8, 2], P(None, 'dp'), may hold values from 0 to 128, as said below
- mixer_gain: float32 [2, 768], P('section'), may hold values from 0.5 to 1.5
- qkv_weight: bfloat16 [2, 3, 768, 768], P('section', None, None, 'mp'), may hold values from -0.21875 to 0.21875
- feature_weight: bfloat16 [2, 12, 64, 64], P('section', 'mp'), may hold values from -1.5 to 1.5
- mixer_weight: bfloat16 [2, 768, 768], P('section', 'mp'), may hold values from -1.75 to 1.75
- ffn_gain: float32 [2, 768], P('section'), may hold values from 0.5 to 1.5
- up_weight: bfloat16 [2, 768, 3072], P('section', None, 'mp'), may hold values from -0.21875 to 0.21875
- down_weight: bfloat16 [2, 3072, 768], P('section', 'mp'), may hold values from -0.109375 to 0.109375
Outputs:
- activations: bfloat16 [2, 2, 1024, 768], P('section', None, ('dp', 'mp'))
- input_grads: bfloat16 [2, 2, 1024, 768], P('section', None, ('dp', 'mp'))
- mixer_gain_grad: float32 [2, 768], P('section')
- qkv_weight_grad: float32 [2, 3, 768, 768], P('section', None, None, 'mp')
- feature_weight_grad: float32 [2, 12, 64, 64], P('section', 'mp')
- mixer_weight_grad: float32 [2, 768, 768], P('section', 'mp')
- ffn_gain_grad: float32 [2, 768], P('section')
- up_weight_grad: float32 [2, 768, 3072], P('section', None, 'mp')
- down_weight_grad: float32 [2, 3072, 768], P('section', 'mp')
The draws below stay inside these ranges and needn't reach their ends.
Inputs may be any that keep to these rules, and one draw needn't show every extreme that they name: `seq_starts`: in each buffer the offsets rise, are multiples of 64, the first is 0, and slots after the last sequence hold 128; a sequence's span runs to the next offset or to the buffer's end. In every buffer one sequence begins in the first 64 rows and ends in the last 64 rows. `seq_lengths`: A sequence's length lies within the last 64 positions of its span; in every buffer the longest sequence fills its span of 128 tokens. Unused slots, and a trailing span that holds no sequence, have length 0.
All inputs are finite; a program needn't handle non-finite values.
Results may differ from the reference program's by a relative error of at most 0.03.
Values may be sent and summed in bfloat16 or wider, within the bound.
A program may use at most 128 MiB of HBM per device.

```python
import jax
import jax.numpy as jnp
from jax import lax

D = 768
H = 12
HD = 64
FF = 3072
STRETCH = 64
MB = 2
TOK_DEV = 128
ROWS_MP = 64
TOKENS = 1024
SLOTS = 2
N_SECTION = 2


def buffer_layout(key):
    nblock = TOK_DEV // STRETCH
    quarter = ROWS_MP // STRETCH
    subkeys = jax.random.split(key, 4)
    longest = nblock - quarter + 1
    before = jax.random.randint(subkeys[1], (), 0, nblock - longest + 1)
    remain = nblock - longest - before
    trailing = jax.random.randint(subkeys[2], (), 0, remain + 1)
    coin_flips = jax.random.randint(subkeys[3], (nblock,), 0, 2)
    block_order = jnp.arange(nblock, dtype=jnp.int32)
    inner = (block_order > 0) & (block_order < before) | (block_order > before + longest) & (block_order < nblock - trailing)
    flagged = (block_order == 0) | (block_order == before) | (block_order == before + longest) & (remain > 0)
    flagged = flagged | (block_order == nblock - trailing) & (trailing > 0) | inner & (coin_flips == 1)
    ranked = jnp.sort(jnp.where(flagged, block_order, nblock + block_order))
    starts = jnp.where(ranked < nblock, ranked * STRETCH, TOK_DEV).astype(jnp.int32)
    return (starts, (before * STRETCH).astype(jnp.int32), ((nblock - trailing) * STRETCH).astype(jnp.int32), trailing > 0)


def all_layouts(key):
    buffer_keys = jax.random.split(key, MB * (TOKENS // TOK_DEV))
    return jax.vmap(buffer_layout)(buffer_keys)


def draw_seq_starts(key, part):
    starts, long_start, tail_start, has_tail = all_layouts(key)
    return starts.reshape(MB, TOKENS // TOK_DEV, SLOTS)


def draw_seq_lengths(key, part):
    starts, long_start, tail_start, has_tail = all_layouts(key)
    key = jax.random.fold_in(key, 5)
    following = jnp.concatenate([starts[:, 1:], jnp.full((starts.shape[0], 1), TOK_DEV, jnp.int32)], axis=1)
    span_len = following - starts
    padding = jax.random.randint(key, starts.shape, 0, STRETCH)
    trimmed = jnp.where(starts == long_start[:, None], span_len, span_len - padding)
    empty = (span_len == 0) | has_tail[:, None] & (starts == tail_start[:, None])
    return jnp.where(empty, 0, trimmed).astype(jnp.int32).reshape(MB, TOKENS // TOK_DEV, SLOTS)


def block_levels(key, dims, shards, smallest, top_value):
    def one(axis_at, parts):
        draws = jax.random.uniform(jax.random.fold_in(jax.random.fold_in(key, 6), axis_at), (parts,), jnp.float32, smallest / len(shards), top_value / len(shards))
        return jnp.repeat(jnp.exp(draws), dims[axis_at] // parts).reshape((-1,) + (1,) * (len(dims) - axis_at - 1))

    factor_of = one(*shards[0])
    for cut in shards[1:]:
        factor_of = factor_of * one(*cut)
    return factor_of


def bell_draw(own_key, shape, scale, most, cuts=(), kind=jnp.bfloat16):
    array = jax.random.normal(own_key, shape, jnp.float32) * scale
    if len(cuts) > 0:
        array = block_levels(own_key, shape, cuts, -0.22, 0.18) * array
    return jnp.clip(array, min=-most, max=most).astype(kind)


def setup_inputs(seed: int = 0) -> dict:
    key_list = jax.random.split(jax.random.key(seed), 12)
    block_input = bell_draw(key_list[0], (MB, TOKENS, D), 1.0, 6.0, ((1, 16),))
    out_cotangent = bell_draw(key_list[1], (MB, TOKENS, D), 1.0, 6.0, ((1, 16),))
    seq_starts = draw_seq_starts(jax.random.fold_in(key_list[11], 71), 0)
    seq_lengths = draw_seq_lengths(jax.random.fold_in(key_list[11], 71), 0)
    mixer_gain = jnp.clip(1.0 + 0.1 * jax.random.normal(key_list[4], (N_SECTION, D), jnp.float32), 0.5, 1.5)
    qkv_weight = bell_draw(key_list[5], (N_SECTION, 3, D, D), D ** -0.5, 0.21875, ((0, 2), (3, 2)))
    feature_weight = bell_draw(key_list[6], (N_SECTION, H, HD, HD), (HD // 4) ** -0.5, 1.5, ((0, 2), (1, 2)))
    mixer_weight = bell_draw(key_list[7], (N_SECTION, D, D), (D // 64) ** -0.5, 1.75, ((0, 2), (1, 2)))
    ffn_gain = jnp.clip(1.0 + 0.1 * jax.random.normal(key_list[8], (N_SECTION, D), jnp.float32), 0.5, 1.5)
    up_weight = bell_draw(key_list[9], (N_SECTION, D, FF), D ** -0.5, 0.21875, ((0, 2), (2, 2)))
    down_weight = bell_draw(key_list[10], (N_SECTION, FF, D), FF ** -0.5, 0.109375, ((0, 2), (1, 2)))
    return dict(block_input=block_input, out_cotangent=out_cotangent, seq_starts=seq_starts, seq_lengths=seq_lengths, mixer_gain=mixer_gain, qkv_weight=qkv_weight, feature_weight=feature_weight, mixer_weight=mixer_weight, ffn_gain=ffn_gain, up_weight=up_weight, down_weight=down_weight)


@jax.custom_vjp
def reduced_precision(v):
    return lax.optimization_barrier(v.astype(jnp.bfloat16)).astype(jnp.float32)

@jax.custom_vjp
def reduced_backward(v):
    return v

def low_keep(v):
    return (reduced_precision(v), None)

def low_pass(kept, grad):
    return (grad,)

def back_keep(v):
    return (v, None)

def back_low(kept, grad):
    return (reduced_precision(grad),)
reduced_precision.defvjp(low_keep, low_pass)
reduced_backward.defvjp(back_keep, back_low)
EXACT_PRECISION = lax.Precision.HIGHEST

def layer_norm(residual, gain):
    row_mean = lax.optimization_barrier(jnp.mean(residual, axis=-1, keepdims=True))
    centered = residual - row_mean
    row_var = lax.optimization_barrier(jnp.mean(centered * centered, axis=-1, keepdims=True))
    return centered * lax.rsqrt(row_var + 1e-05) * gain

def hedgehog(logits):
    return jnp.concatenate([jax.nn.softmax(logits, axis=-1), jax.nn.softmax(-logits, axis=-1)], axis=-1)

def linear_mix(q_feat, k_feat, values, same_doc):
    row_total, head_count, feat_count = q_feat.shape
    value_width = values.shape[2]
    blocks = same_doc.shape[0]
    block_size = row_total // blocks
    q_blocks = q_feat.reshape(blocks, block_size, head_count, feat_count)
    k_blocks = k_feat.reshape(blocks, block_size, head_count, feat_count)
    v_blocks = values.reshape(blocks, block_size, head_count, value_width)
    lower_mask = (jnp.arange(block_size)[:, None] >= jnp.arange(block_size)[None, :]).astype(jnp.float32)
    scores = jnp.einsum('cihf,cjhf->chij', q_blocks, k_blocks, precision=EXACT_PRECISION) * lower_mask
    numerator = jnp.einsum('chij,cjhe->cihe', scores, v_blocks, precision=EXACT_PRECISION)
    denominator = jnp.transpose(lax.optimization_barrier(jnp.sum(scores, axis=3)), (0, 2, 1))
    block_kv = jnp.einsum('cjhf,cjhe->chfe', k_blocks, v_blocks, precision=EXACT_PRECISION)
    block_keys = lax.optimization_barrier(jnp.sum(k_blocks, axis=1))
    carried = jnp.einsum('cd,dhfe->chfe', same_doc, block_kv, precision=EXACT_PRECISION)
    carried_keys = jnp.einsum('cd,dhf->chf', same_doc, block_keys, precision=EXACT_PRECISION)
    numerator = numerator + jnp.einsum('cihf,chfe->cihe', q_blocks, carried, precision=EXACT_PRECISION)
    denominator = denominator + jnp.einsum('cihf,chf->cih', q_blocks, carried_keys, precision=EXACT_PRECISION)
    return (numerator / denominator[..., None]).reshape(row_total, head_count * value_width)

def doc_tables(starts, lengths, row_total, block_size, row_offset, row_count):
    blocks = row_total // block_size
    block_pos = jnp.arange(blocks, dtype=jnp.int32) * block_size
    block_doc = lax.optimization_barrier(jnp.sum((starts[None, :] <= block_pos[:, None]).astype(jnp.int32), axis=1))
    block_order = jnp.arange(blocks, dtype=jnp.int32)
    same_doc = ((block_doc[:, None] == block_doc[None, :]) & (block_order[None, :] < block_order[:, None])).astype(jnp.float32)
    positions = row_offset + jnp.arange(row_count, dtype=jnp.int32)
    doc_begin = lax.optimization_barrier(jnp.max(jnp.where(starts[None, :] <= positions[:, None], starts[None, :], 0), axis=1))
    length_of = lax.optimization_barrier(jnp.sum(jnp.where(starts[None, :] == doc_begin[:, None], lengths[None, :], 0), axis=1))
    live_rows = (positions - doc_begin < length_of).astype(jnp.float32)
    return (same_doc, live_rows)

def block_layer(weights, residual, same_doc):
    first_gain, query_key_value_matrix, feature_map, out_matrix, second_gain, up_matrix, down_matrix = weights
    row_total = residual.shape[0]
    normalized_rows = reduced_precision(layer_norm(residual, first_gain))
    projected_rows = reduced_precision(reduced_backward(jnp.einsum('my,qyt->qmt', normalized_rows, query_key_value_matrix, precision=EXACT_PRECISION)))
    by_head = projected_rows.reshape(3, row_total, H, HD)
    q_logit = reduced_backward(jnp.einsum('nhd,hde->nhe', by_head[0], feature_map, precision=EXACT_PRECISION))
    k_logit = reduced_backward(jnp.einsum('nhd,hde->nhe', by_head[1], feature_map, precision=EXACT_PRECISION))
    q_feat = reduced_precision(hedgehog(q_logit))
    k_feat = reduced_precision(hedgehog(k_logit))
    mixed = reduced_precision(reduced_backward(linear_mix(q_feat, k_feat, by_head[2], same_doc)))
    resid_mid = residual + reduced_backward(jnp.dot(mixed, out_matrix, precision=EXACT_PRECISION))
    normed_mid = reduced_precision(layer_norm(resid_mid, second_gain))
    hidden = reduced_precision(jax.nn.gelu(reduced_backward(jnp.dot(normed_mid, up_matrix, precision=EXACT_PRECISION))))
    return resid_mid + reduced_backward(jnp.dot(hidden, down_matrix, precision=EXACT_PRECISION))

def table_one(starts, lengths):
    return doc_tables(starts, lengths, TOK_DEV, STRETCH, 0, TOK_DEV)

def reference(block_input, out_cotangent, seq_starts, seq_lengths, mixer_gain, qkv_weight, feature_weight, mixer_weight, ffn_gain, up_weight, down_weight):
    groups = TOKENS // TOK_DEV
    buffers = MB * groups
    starts_all = seq_starts.reshape(buffers, SLOTS)
    lengths_all = seq_lengths.reshape(buffers, SLOTS)
    same_all, live_all = jax.vmap(table_one)(starts_all, lengths_all)
    inputs = block_input.astype(jnp.float32).reshape(buffers, TOK_DEV, D)
    cotangent = out_cotangent.astype(jnp.float32).reshape(buffers, TOK_DEV, D) * live_all[:, :, None]
    params = tuple((weight.astype(jnp.float32) for weight in (mixer_gain, qkv_weight, feature_weight, mixer_weight, ffn_gain, up_weight, down_weight)))
    shifts = jnp.zeros_like(inputs)

    def whole_block(params, inputs, shifts):

        def buffer_step(unused_carry, pieces):
            rows_in, shift_rows, same_doc = pieces
            first_layer = tuple((weight[0] for weight in params))
            second_layer = tuple((weight[1] for weight in params))
            middle = reduced_precision(reduced_backward(block_layer(first_layer, rows_in, same_doc) + shift_rows))
            return (unused_carry, (middle, block_layer(second_layer, middle, same_doc)))
        _, results = lax.scan(jax.checkpoint(buffer_step), jnp.zeros((), jnp.float32), (inputs, shifts, same_all))
        return results
    (middle, top), pullback = jax.vjp(whole_block, params, inputs, shifts)
    param_grads, input_grad, shift_grad = pullback((jnp.zeros_like(middle), cotangent))
    activations = jnp.stack([middle, top]).reshape(2, MB, TOKENS, D).astype(jnp.bfloat16)
    input_grads = jnp.stack([input_grad, shift_grad]).reshape(2, MB, TOKENS, D).astype(jnp.bfloat16)
    return (activations, input_grads, param_grads[0], param_grads[1], param_grads[2], param_grads[3], param_grads[4], param_grads[5], param_grads[6])
```

```python
import functools

import jax
import jax.numpy as jnp
from jax import lax
from jax.experimental import pallas as pl
from jax.experimental.pallas import tpu as pltpu
from jax.sharding import PartitionSpec as P

STRETCH = 64
GROUP = 8
LINE = 4
MESH = pl.DeviceIdType.MESH
BF = jnp.bfloat16
F32 = jnp.float32
ANY = pl.BlockSpec(memory_space=pl.ANY)
VM = pl.BlockSpec(memory_space=pltpu.VMEM)
SM = pl.BlockSpec(memory_space=pltpu.SMEM)


def dot(a, b, ca=1, cb=0):
    return lax.dot_general(a, b, (((ca,), (cb,)), ((), ())), preferred_element_type=F32)


def normed(v):
    mean = jnp.mean(v, axis=1, keepdims=True)
    c = v - mean
    rstd = lax.rsqrt(jnp.mean(c * c, axis=1, keepdims=True) + 1e-05)
    return c * rstd, rstd


def norm_back(grad, gain, xhat, rstd):
    t = grad * gain
    mean_t = jnp.mean(t, axis=1, keepdims=True)
    mean_tx = jnp.mean(t * xhat, axis=1, keepdims=True)
    return rstd * (t - mean_t - xhat * mean_tx)


def gelu_both(x):
    k = 0.7978845608028654
    x2 = x * x
    t = jnp.tanh(x * (k + (k * 0.044715) * x2))
    half = 0.5 * (1.0 + t)
    slope = half + 0.5 * x * (1.0 - t * t) * (k + (3.0 * k * 0.044715) * x2)
    return x * half, slope


def both_softmax(logit):
    up = jnp.exp(logit - jnp.max(logit, axis=0, keepdims=True))
    down = jnp.exp(jnp.min(logit, axis=0, keepdims=True) - logit)
    up = up * (1.0 / jnp.sum(up, axis=0, keepdims=True))
    down = down * (1.0 / jnp.sum(down, axis=0, keepdims=True))
    return jnp.concatenate([up.astype(BF), down.astype(BF)], axis=0)


def softmax_back(grad, feat):
    n = grad.shape[0] // 2
    g = grad * feat.astype(F32)
    p = feat.astype(F32)
    one = g[:n] - p[:n] * jnp.sum(g[:n], axis=0, keepdims=True)
    two = g[n:] - p[n:] * jnp.sum(g[n:], axis=0, keepdims=True)
    return one - two


def kernel(
    x_in, cot, starts, lengths, gain1, wqkv_h, fmap, wmix_h, gain2, up_h, down_h,
    act_o, ig_o, qkv_o, mix_o, small_o, up_o, down_o,
    wqkv, wmix, wup, wdown, rin, gin, mask,
    nrm, nrm_t, pt, vnat, qf, kf, st, mt, mtb, den_s, rmid, nm_all, gd_all, gp, rout, act, igv,
    pk3, gmid, gbr, gqk, gpt, pk4, gacc, sbuf, rbuf, pay, ybuf, zbuf, fin, ups, downs, acc_u, acc_d,
    lsem, xs, xr, cs, cr, gs, gr, ars, arr, osem,
):
    s = lax.axis_index("section")
    d = lax.axis_index("dp")
    xi = lax.axis_index("mp")
    micro, half, width = x_in.shape
    rows = 2 * half
    heads, hs = fmap.shape[1], fmap.shape[2]
    hw = heads * hs
    ff = up_h.shape[2]
    g = lax.rem(d, GROUP)
    base = d - g
    pos = lax.div(g, 2)
    par = lax.rem(g, 2)
    to_x = (s, d, 1 - xi)
    to_c = (1 - s, d, xi)
    to_y = (s, base + pos * 2 + 1 - par, xi)

    def line_pos(k):
        return lax.rem(pos + k, LINE)

    def to_line(k):
        return (s, base + line_pos(k) * 2 + par, xi)

    partners = [to_x, to_c, to_y] + [to_line(k) for k in range(1, LINE)]

    def local(src, dst, i):
        return pltpu.make_async_copy(src, dst, lsem.at[i])

    def remote(src, dst, ss, rs, to):
        return pltpu.make_async_remote_copy(
            src_ref=src, dst_ref=dst, send_sem=ss, recv_sem=rs, device_id=to, device_id_type=MESH
        )

    loads = [
        local(wqkv_h.at[0], wqkv, 0),
        local(wmix_h.at[0], wmix, 1),
        local(up_h.at[0], wup, 2),
        local(down_h.at[0], wdown, 3),
    ]
    own_x = local(x_in, rin.at[:, pl.ds(0, half)], 4)
    own_c = local(cot, gin.at[:, pl.ds(0, half)], 5)

    @pl.when(s == 0)
    def _():
        own_x.start()

    @pl.when(s == 1)
    def _():
        own_c.start()

    for c in loads:
        c.start()

    barrier = pltpu.get_barrier_semaphore()
    for to in partners:
        pl.semaphore_signal(barrier, inc=1, device_id=to, device_id_type=MESH)
    pl.semaphore_wait(barrier, len(partners))

    first_x = remote(x_in, rin.at[:, pl.ds(half, half)], xs.at[0], xr.at[0], to_x)
    first_c = remote(cot, gin.at[:, pl.ds(half, half)], xs.at[0], xr.at[0], to_x)

    @pl.when(s == 0)
    def _():
        first_x.start()

    @pl.when(s == 1)
    def _():
        first_c.start()

    jj = lax.broadcasted_iota(jnp.int32, (rows, rows), 0)
    ii = lax.broadcasted_iota(jnp.int32, (rows, rows), 1)
    j_own, i_own = jj < half, ii < half
    inside = ((j_own == i_own) & (jj <= ii)).astype(F32)
    own_first = jnp.where(xi == 0, 1.0, 0.0)
    across = jnp.where(j_own & ~i_own, own_first, jnp.where(i_own & ~j_own, 1.0 - own_first, 0.0))
    slots = starts.shape[2]
    for m in range(micro):
        n0 = jnp.int32(0)
        n1 = jnp.int32(0)
        for j in range(slots):
            n0 += jnp.where(starts[m, 0, j] <= 0, 1, 0)
            n1 += jnp.where(starts[m, 0, j] <= STRETCH, 1, 0)
        same = jnp.where(n0 == n1, 1.0, 0.0)
        mask[m] = inside + across * same

    def live_of(m, part):
        block = xi if part == 0 else 1 - xi
        begin = jnp.int32(0)
        for j in range(slots):
            begin = jnp.where(starts[m, 0, j] <= block * STRETCH, jnp.maximum(begin, starts[m, 0, j]), begin)
        length = jnp.int32(0)
        for j in range(slots):
            length += jnp.where(starts[m, 0, j] == begin, lengths[m, 0, j], 0)
        row = block * STRETCH + lax.broadcasted_iota(jnp.int32, (half, width), 0)
        return (row - begin < length).astype(F32)

    def x_swap(e, m):
        i = 1 + e * micro + m
        return remote(sbuf.at[e, m], rbuf.at[e, m], xs.at[i], xr.at[i], to_x)

    def give(e, m, part):
        part = part.astype(BF)
        sbuf[e, m, pl.ds(0, half)] = part[half:]
        sbuf[e, m, pl.ds(half, half)] = part[:half]
        x_swap(e, m).start()

    def c_copy(e, m):
        i = e * micro + m
        src, dst = ((act, rin), (igv, gin))[e]
        return remote(src.at[m], dst.at[m], cs.at[i], cr.at[i], to_c)

    def mixer_forward(m):
        if m == 0:
            @pl.when(s == 0)
            def _():
                own_x.wait()
                first_x.wait_recv()

        @pl.when(s == 1)
        def _():
            c_copy(0, m).wait_recv()

        if m == 0:
            loads[0].wait()
        r = rin[m].astype(F32)
        n = (normed(r)[0] * gain1[...]).astype(BF)
        nrm[m] = n
        for q in range(3):
            p = dot(n, wqkv[q]).astype(BF)
            if q == 2:
                vnat[m] = p
            pt[m, q] = p.T
        for h in range(heads):
            hr = pl.ds(h * hs, hs)
            w = fmap[0, h]
            qfh = both_softmax(dot(w, pt[m, 0, hr], 0, 0))
            kfh = both_softmax(dot(w, pt[m, 1, hr], 0, 0))
            qf[m, h] = qfh
            kf[m, h] = kfh
            sc = dot(kfh, qfh, 0, 0) * mask[m]
            den = 1.0 / jnp.sum(sc, axis=0, keepdims=True)
            scb = sc.astype(BF)
            st[m, h] = scb
            den_s[m, h] = jnp.broadcast_to(den, (8, rows))
            mx = dot(pt[m, 2, hr], scb) * den
            mt[m, hr] = mx
            mtb[m, hr] = mx.astype(BF)
        if m == 0:
            loads[1].wait()
        part = dot(mtb[m].T, wmix[...])
        give(0, m, part)
        rmid[m] = r + part

    def ffn_forward(m):
        x_swap(0, m).wait_recv()
        r = rmid[m] + rbuf[0, m].astype(F32)
        rmid[m] = r
        n = (normed(r)[0] * gain2[...]).astype(BF)
        nm_all[g, :, pl.ds(m * rows, rows)] = n.T
        if m == 0:
            loads[2].wait()
        h, slope = gelu_both(dot(n, wup[...]))
        h = h.astype(BF)
        gp[m] = slope.astype(BF)
        if m == 0:
            loads[3].wait()
        part = dot(h, wdown[...])
        give(1, m, part)
        rout[m] = r + part

    def end_forward(m):
        x_swap(1, m).wait_recv()
        act[m] = (rout[m] + rbuf[1, m].astype(F32)).astype(BF)

        @pl.when(s == 0)
        def _():
            c_copy(0, m).start()

        pltpu.make_async_copy(act.at[m, pl.ds(0, half)], act_o.at[0, m], osem.at[m]).start()

    gathered = (nm_all, gd_all)

    def spread(kind, k):
        ref = gathered[kind].at[g]
        i = kind * 7 + k
        return remote(ref, ref, gs.at[i], gr.at[i], to_y if k == 0 else to_line(k))

    def relay(kind, k):
        slot = lax.rem(pos - k + LINE, LINE) * 2 + par
        ref = gathered[kind].at[slot]
        i = kind * 7 + LINE - 1 + k
        return remote(ref, ref, gs.at[i], gr.at[i], to_y)

    for m in range(micro):
        mixer_forward(m)
    for m in range(micro):
        ffn_forward(m)
    for k in range(LINE):
        spread(0, k).start()
    for m in range(micro):
        end_forward(m)

    def relay_all(kind):
        for k in range(1, LINE):
            spread(kind, k).wait_recv()
            relay(kind, k).start()

    @pl.when(s == 0)
    def _():
        relay_all(0)

    def ffn_back(m):
        if m == 0:
            @pl.when(s == 1)
            def _():
                own_c.wait()
                first_c.wait_recv()

        @pl.when(s == 0)
        def _():
            c_copy(1, m).wait_recv()

        for part in range(2):
            keep = jnp.where(s == 1, live_of(m, part), 1.0)
            pr = pl.ds(part * half, half)
            gd_all[g, pl.ds(m * rows + part * half, half)] = (gin[m, pr].astype(F32) * keep).astype(BF)
        gd = gd_all[g, pl.ds(m * rows, rows)]
        gpre = (dot(gd, wdown[...], 1, 1) * gp[m].astype(F32)).astype(BF)
        part = dot(gpre, wup[...], 1, 1)
        give(2, m, part)
        pk3[m] = part

    def mixer_back(m):
        x_swap(2, m).wait_recv()
        gn = pk3[m] + rbuf[2, m].astype(F32)
        xhat, rstd = normed(rmid[m])
        gacc[1, m] = jnp.broadcast_to(jnp.sum(gn * xhat, axis=0, keepdims=True), (8, width))
        gm = gd_all[g, pl.ds(m * rows, rows)].astype(F32) + norm_back(gn, gain2[...], xhat, rstd)
        gmid[m] = gm
        gb = gm.astype(BF)
        gbr[m] = gb
        gmt = dot(wmix[...], gb, 1, 1).astype(BF)
        for h in range(heads):
            hr = pl.ds(h * hs, hs)
            den = den_s[m, h, pl.ds(0, 1)]
            go = gmt[h * hs : (h + 1) * hs].astype(F32)
            gden = -jnp.sum(go * mt[m, hr], axis=0, keepdims=True) * den
            gnum = (go * den).astype(BF)
            pad = jnp.zeros_like(gnum)
            wide = jnp.concatenate([gnum, pad] if h % 2 == 0 else [pad, gnum], axis=0)
            gst = ((dot(vnat[m, :, pl.ds((h // 2) * 2 * hs, 2 * hs)], wide) + gden) * mask[m]).astype(BF)
            qfh = qf[m, h]
            kfh = kf[m, h]
            gql = softmax_back(dot(kfh, gst), qfh).astype(BF)
            gkl = softmax_back(dot(qfh, gst, 1, 1), kfh).astype(BF)
            gv = dot(gnum, st[m, h], 1, 1).astype(BF)
            gqk[0, m, hr] = gql
            gqk[1, m, hr] = gkl
            w = fmap[0, h]
            gpt[m, 0, hr] = dot(w, gql).astype(BF)
            gpt[m, 1, hr] = dot(w, gkl).astype(BF)
            gpt[m, 2, hr] = gv
        gnt = dot(wqkv[0], gpt[m, 0]) + dot(wqkv[1], gpt[m, 1]) + dot(wqkv[2], gpt[m, 2])
        part = gnt.T
        give(3, m, part)
        pk4[m] = part
        nrm_t[m] = nrm[m].T

    def end_back(m):
        x_swap(3, m).wait_recv()
        gn = pk4[m] + rbuf[3, m].astype(F32)
        xhat, rstd = normed(rin[m].astype(F32))
        gacc[0, m] = jnp.broadcast_to(jnp.sum(gn * xhat, axis=0, keepdims=True), (8, width))
        igv[m] = (gmid[m] + norm_back(gn, gain1[...], xhat, rstd)).astype(BF)

        @pl.when(s == 1)
        def _():
            c_copy(1, m).start()

        pltpu.make_async_copy(igv.at[m, pl.ds(0, half)], ig_o.at[0, m], osem.at[micro + m]).start()

    for m in range(micro):
        ffn_back(m)
    for k in range(LINE):
        spread(1, k).start()
    for m in range(micro):
        mixer_back(m)

    for q in range(3):
        tot = dot(nrm_t[0], gpt[0, q], 1, 1)
        for m in range(1, micro):
            tot += dot(nrm_t[m], gpt[m, q], 1, 1)
        pay[pl.ds(q * width, width)] = tot.astype(BF)
    tot = dot(mtb[0], gbr[0])
    for m in range(1, micro):
        tot += dot(mtb[m], gbr[m])
    tot = tot.astype(BF)
    base_row = 3 * width
    for c in range(width // hw):
        pay[pl.ds(base_row + c * hw, hw)] = tot[:, c * hw : (c + 1) * hw]
    base_row += (width // hw) * hw
    left = lax.broadcasted_iota(jnp.int32, (hs, 2 * hs), 1) < hs
    for p in range(heads // 2):
        pr = pl.ds(p * 2 * hs, 2 * hs)
        tot = jnp.zeros((2 * hs, 2 * hs), F32)
        for m in range(micro):
            tot += dot(pt[m, 0, pr], gqk[0, m, pr], 1, 1) + dot(pt[m, 1, pr], gqk[1, m, pr], 1, 1)
        pay[pl.ds(base_row, hs), pl.ds(p * 2 * hs, 2 * hs)] = jnp.where(left, tot[:hs], tot[hs:]).astype(BF)

    for m in range(micro):
        end_back(m)

    base_row += hs
    tail = pay.shape[0] - base_row
    row = lax.broadcasted_iota(jnp.int32, (tail, hw), 0)
    block = jnp.zeros((tail, hw), F32)
    for e in range(2):
        tot = gacc[e, 0, pl.ds(0, 1)]
        for m in range(1, micro):
            tot += gacc[e, m, pl.ds(0, 1)]
        for c in range(width // hw):
            block = jnp.where(row == e * (width // hw) + c, tot[:, c * hw : (c + 1) * hw], block)
    pay[pl.ds(base_row, tail)] = block.astype(BF)

    side = pay.shape[0] // 2
    chunk = side // LINE

    def mine(c):
        return pl.ds(pl.multiple_of(par * side + c * chunk, 16), chunk)

    def other(c):
        return pl.ds(pl.multiple_of((1 - par) * side + c * chunk, 16), chunk)

    def ar_pair(k):
        c = line_pos(k)
        return remote(
            pay.at[other(c)], ybuf.at[pl.ds(pl.multiple_of(c * chunk, 16), chunk)], ars.at[k], arr.at[k], to_y
        )

    def ar_line(k):
        return remote(pay.at[mine(line_pos(k))], zbuf.at[k - 1], ars.at[3 + k], arr.at[3 + k], to_line(k))

    def ar_spread(k):
        ref = fin.at[mine(pos)]
        return remote(ref, ref, ars.at[6 + k], arr.at[6 + k], to_line(k))

    def ar_back(k):
        ref = fin.at[mine(lax.rem(pos - k + LINE, LINE))]
        return remote(ref, ref, ars.at[10 + k], arr.at[10 + k], to_y)

    order = [1, 2, 3, 0]
    for k in order:
        ar_pair(k).start()

    @pl.when(s == 1)
    def _():
        relay_all(0)

    for k in order:
        ar_pair(k).wait_recv()
        c = line_pos(k)
        yr = pl.ds(pl.multiple_of(c * chunk, 16), chunk)
        pay[mine(c)] = (pay[mine(c)].astype(F32) + ybuf[yr].astype(F32)).astype(BF)
        if k > 0:
            ar_line(k).start()

    relay_all(1)
    for kind in range(2):
        spread(kind, 0).wait_recv()
        for k in range(1, LINE):
            relay(kind, k).wait_recv()


    def ffn_grads(tile, t):
        hr = pl.ds(pl.multiple_of(t * tile, tile), tile)
        wu = wup[:, hr].T
        wd = wdown[hr]
        for i in range(GROUP):
            h, slope = gelu_both(dot(wu, nm_all[i]))
            gpre = (dot(wd, gd_all[i], 1, 1) * slope).astype(BF)
            a = dot(nm_all[i], gpre, 1, 1)
            b = dot(h.astype(BF), gd_all[i])
            if i == 0:
                acc_u[...] = a
                acc_d[...] = b
            else:
                acc_u[...] += a
                acc_d[...] += b
        ups[:, hr] = acc_u[...].astype(BF)
        downs[hr] = acc_d[...].astype(BF)

    tile = 256
    steps = ff // tile

    def some(lo, hi):
        lax.fori_loop(lo, hi, lambda t, _: (ffn_grads(tile, t), 0)[1], 0)

    some(0, steps // 2)

    mrow = mine(pos)
    tot = pay[mrow].astype(F32)
    for k in range(1, LINE):
        ar_line(k).wait_recv()
        tot += zbuf[k - 1].astype(F32)
    fin[mrow] = tot.astype(BF)
    for k in range(1, LINE):
        ar_spread(k).start()
    ar_back(0).start()

    some(steps // 2, steps)
    outs = [
        pltpu.make_async_copy(ups, up_o, osem.at[2 * micro]),
        pltpu.make_async_copy(downs, down_o, osem.at[2 * micro + 1]),
    ]
    for c in outs:
        c.start()

    for k in range(1, LINE):
        ar_spread(k).wait_recv()
        ar_back(k).start()
    for k in range(LINE):
        ar_back(k).wait_recv()

    tail_out = [pltpu.make_async_copy(fin.at[pl.ds(0, 3 * width)], qkv_o, osem.at[2 * micro + 2])]
    for c in range(width // hw):
        tail_out.append(
            pltpu.make_async_copy(
                fin.at[pl.ds(3 * width + c * hw, hw)], mix_o.at[:, pl.ds(c * hw, hw)], osem.at[2 * micro + 3 + c]
            )
        )
    n_out = 2 * micro + 3 + width // hw
    small = 3 * width + (width // hw) * hw
    tail_out.append(
        pltpu.make_async_copy(fin.at[pl.ds(small, small_o.shape[0])], small_o, osem.at[n_out])
    )
    for c in tail_out:
        c.start()

    @pl.when(s == 0)
    def _():
        first_x.wait_send()
        for m in range(micro):
            c_copy(0, m).wait_send()

    @pl.when(s == 1)
    def _():
        first_c.wait_send()
        for m in range(micro):
            c_copy(1, m).wait_send()

    for e in range(4):
        for m in range(micro):
            x_swap(e, m).wait_send()
    for kind in range(2):
        for k in range(LINE):
            spread(kind, k).wait_send()
        for k in range(1, LINE):
            relay(kind, k).wait_send()
    for k in range(LINE):
        ar_pair(k).wait_send()
        ar_back(k).wait_send()
    for k in range(1, LINE):
        ar_line(k).wait_send()
        ar_spread(k).wait_send()
    for m in range(micro):
        pltpu.make_async_copy(act.at[m, pl.ds(0, half)], act_o.at[0, m], osem.at[m]).wait()
        pltpu.make_async_copy(igv.at[m, pl.ds(0, half)], ig_o.at[0, m], osem.at[micro + m]).wait()
    for c in outs + tail_out:
        c.wait()


def on_device(x, cot, starts, lengths, gain1, wqkv, fmap, wmix, gain2, wup, wdown):
    micro, half, width = x.shape
    rows = 2 * half
    heads, hs = fmap.shape[1], fmap.shape[2]
    hw = heads * hs
    ff = wup.shape[2]
    cut = width // hw
    used = 3 * width + cut * hw + hs + 2 * cut
    unit = 2 * LINE * 16
    pay_rows = -(-used // unit) * unit
    small_rows = -(-(hs + 2 * cut) // 16) * 16
    f, b = F32, BF
    vm = pltpu.VMEM
    dma = pltpu.SemaphoreType.DMA
    out = lambda shape: jax.ShapeDtypeStruct(shape, b)
    act, ig, qkv, mix, small, up, down = pl.pallas_call(
        kernel,
        out_shape=[
            out((1, micro, half, width)),
            out((1, micro, half, width)),
            out((3 * width, hw)),
            out((hw, width)),
            out((small_rows, hw)),
            out((width, ff)),
            out((ff, width)),
        ],
        in_specs=[ANY, ANY, SM, SM, VM, ANY, VM, ANY, VM, ANY, ANY],
        out_specs=[ANY] * 7,
        scratch_shapes=[
            vm((3, width, hw), b),
            vm((hw, width), b),
            vm((width, ff), b),
            vm((ff, width), b),
            vm((micro, rows, width), b),
            vm((micro, rows, width), b),
            vm((micro, rows, rows), f),
            vm((micro, rows, width), b),
            vm((micro, width, rows), b),
            vm((micro, 3, hw, rows), b),
            vm((micro, rows, hw), b),
            vm((micro, heads, 2 * hs, rows), b),
            vm((micro, heads, 2 * hs, rows), b),
            vm((micro, heads, rows, rows), b),
            vm((micro, hw, rows), f),
            vm((micro, hw, rows), b),
            vm((micro, heads, 8, rows), f),
            vm((micro, rows, width), f),
            vm((GROUP, width, micro * rows), b),
            vm((GROUP, micro * rows, width), b),
            vm((micro, rows, ff), b),
            vm((micro, rows, width), f),
            vm((micro, rows, width), b),
            vm((micro, rows, width), b),
            vm((micro, rows, width), f),
            vm((micro, rows, width), f),
            vm((micro, rows, width), b),
            vm((2, micro, hw, rows), b),
            vm((micro, 3, hw, rows), b),
            vm((micro, rows, width), f),
            vm((2, micro, 8, width), f),
            vm((4, micro, rows, width), b),
            vm((4, micro, rows, width), b),
            vm((pay_rows, hw), b),
            vm((pay_rows // 2, hw), b),
            vm((LINE - 1, pay_rows // 2 // LINE, hw), b),
            vm((pay_rows, hw), b),
            vm((width, ff), b),
            vm((ff, width), b),
            vm((width, 256), f),
            vm((256, width), f),
            dma((6,)),
            dma((1 + 4 * micro,)),
            dma((1 + 4 * micro,)),
            dma((2 * micro,)),
            dma((2 * micro,)),
            dma((14,)),
            dma((14,)),
            dma((14,)),
            dma((14,)),
            dma((2 * micro + 4 + cut,)),
        ],
        compiler_params=pltpu.CompilerParams(
            collective_id=0, has_side_effects=True, vmem_limit_bytes=56 * 1024 * 1024
        ),
    )(x, cot, starts, lengths, gain1, wqkv, fmap, wmix, gain2, wup, wdown)

    n = lax.axis_size("dp")
    if n > GROUP:
        same_place = [[i + j * GROUP for j in range(n // GROUP)] for i in range(GROUP)]
        qkv, mix, small, up, down = lax.psum(
            tuple(v.astype(f) for v in (qkv, mix, small, up, down)), "dp", axis_index_groups=same_place
        )
    features = jnp.swapaxes(small[:hs].astype(f).reshape(hs, heads, hs), 0, 1)
    gains = small[hs : hs + 2 * cut].astype(f).reshape(2, width)
    return (
        act,
        ig,
        gains[None, 0],
        qkv.astype(f).reshape(1, 3, width, hw),
        features[None],
        mix.astype(f)[None],
        gains[None, 1],
        up.astype(f)[None],
        down.astype(f)[None],
    )


def solution(mesh):
    in_specs = (
        P(None, ("dp", "mp"), None),
        P(None, ("dp", "mp"), None),
        P(None, "dp", None),
        P(None, "dp", None),
        P("section", None),
        P("section", None, None, "mp"),
        P("section", "mp", None, None),
        P("section", "mp", None),
        P("section", None),
        P("section", None, "mp"),
        P("section", "mp", None),
    )
    out_specs = (
        P("section", None, ("dp", "mp"), None),
        P("section", None, ("dp", "mp"), None),
        P("section", None),
        P("section", None, None, "mp"),
        P("section", "mp", None, None),
        P("section", "mp", None),
        P("section", None),
        P("section", None, "mp"),
        P("section", "mp", None),
    )
    return jax.shard_map(
        on_device, mesh=mesh, in_specs=in_specs, out_specs=out_specs, check_vma=False
    )
```

```python
import functools

import functools

import jax
import jax.numpy as jnp
from jax import lax
from jax.experimental import pallas as pl
from jax.experimental.pallas import tpu as pltpu
from jax.sharding import PartitionSpec as P

STRETCH = 64
GROUP = 8
LINE = 4
MESH = pl.DeviceIdType.MESH
BF = jnp.bfloat16
F32 = jnp.float32
ANY = pl.BlockSpec(memory_space=pl.ANY)
VM = pl.BlockSpec(memory_space=pltpu.VMEM)
SM = pl.BlockSpec(memory_space=pltpu.SMEM)


def dot(a, b, ca=1, cb=0):
    return lax.dot_general(a, b, (((ca,), (cb,)), ((), ())), preferred_element_type=F32)


def normed(v):
    mean = jnp.mean(v, axis=1, keepdims=True)
    c = v - mean
    rstd = lax.rsqrt(jnp.mean(c * c, axis=1, keepdims=True) + 1e-05)
    return c * rstd, rstd


def norm_back(grad, gain, xhat, rstd):
    t = grad * gain
    mean_t = jnp.mean(t, axis=1, keepdims=True)
    mean_tx = jnp.mean(t * xhat, axis=1, keepdims=True)
    return rstd * (t - mean_t - xhat * mean_tx)


def gelu_both(x):
    k = 0.7978845608028654
    x2 = x * x
    t = jnp.tanh(x * (k + (k * 0.044715) * x2))
    half = 0.5 * (1.0 + t)
    slope = half + 0.5 * x * (1.0 - t * t) * (k + (3.0 * k * 0.044715) * x2)
    return x * half, slope


def both_softmax(logit):
    up = jnp.exp(logit - jnp.max(logit, axis=0, keepdims=True))
    down = jnp.exp(jnp.min(logit, axis=0, keepdims=True) - logit)
    up = up * (1.0 / jnp.sum(up, axis=0, keepdims=True))
    down = down * (1.0 / jnp.sum(down, axis=0, keepdims=True))
    return jnp.concatenate([up.astype(BF), down.astype(BF)], axis=0)


def softmax_back(grad, feat):
    n = grad.shape[0] // 2
    g = grad * feat.astype(F32)
    p = feat.astype(F32)
    one = g[:n] - p[:n] * jnp.sum(g[:n], axis=0, keepdims=True)
    two = g[n:] - p[n:] * jnp.sum(g[n:], axis=0, keepdims=True)
    return one - two


def kernel(
    x_in, cot, starts, lengths, gain1, wqkv_h, fmap, wmix_h, gain2, up_h, down_h,
    act_o, ig_o, qkv_o, mix_o, small_o, up_o, down_o,
    wqkv, wmix, wup, wdown, wupt, rin, gin, mask,
    nrm_t, pt, vnat, qf, kf, st, mt, mtb, den_s, rmid, nm_all, nm_cat, gd_all, hb, gb, gp, part_f, act, igv,
    gbr, gqk, gpt, gacc, sbuf, rbuf,
    ynrm, ymtb, ygpt, ygbr, sb, ysb, hp, fin, from_out, from_opp, from_pair, hnm, hgd,
    lsem, xs, xr, cs, cr, la, ha, fs, us, ys, yr, ars, arr, osem, turn,
):
    s = lax.axis_index("section")
    d = lax.axis_index("dp")
    xi = lax.axis_index("mp")
    micro, half, width = x_in.shape
    rows = 2 * half
    span = micro * rows
    heads, hs = fmap.shape[1], fmap.shape[2]
    hw = heads * hs
    ff = up_h.shape[2]
    g = lax.rem(d, GROUP)
    base = d - g
    pos = lax.div(g, 2)
    par = lax.rem(g, 2)
    to_x = (s, d, 1 - xi)
    to_c = (1 - s, d, xi)
    to_y = (s, base + pos * 2 + 1 - par, xi)
    outer = (pos == 0) | (pos == LINE - 1)
    inner = (pos > 0) & (pos < LINE - 1)
    side = lax.div(pos, 2)
    to_mate = (s, base + (side * 4 + 1 - pos) * 2 + par, xi)
    to_opp = (s, base + (LINE - 1 - pos) * 2 + par, xi)

    def other_core(to):
        return (1 - s,) + to[1:]

    def other_core(to):
        return (1 - s,) + to[1:]

    def at(core, p, q):
        return (core, base + p * 2 + q, xi)

    def greet(act):
        for to in (to_x, to_c, to_y, other_core(to_y)):
            act(to)
        pl.when(pos < LINE - 1)(lambda: act(at(s, pos + 1, par)))
        pl.when(pos > 0)(lambda: act(at(s, pos - 1, par)))

    def local(src, dst, sem):
        return pltpu.make_async_copy(src, dst, sem)

    def remote(src, dst, ss, rs, to):
        return pltpu.make_async_remote_copy(
            src_ref=src, dst_ref=dst, send_sem=ss, recv_sem=rs, device_id=to, device_id_type=MESH
        )

    def cols(m):
        return pl.ds(m * rows, rows)

    def slot(i):
        return pl.ds(pl.multiple_of(i * span, span), span)

    own_x = local(x_in, rin.at[:, pl.ds(0, half)], lsem.at[4])
    own_c = local(cot, gin.at[:, pl.ds(0, half)], lsem.at[4])
    loads = [
        local(wqkv_h.at[0], wqkv, lsem.at[0]),
        local(wmix_h.at[0], wmix, lsem.at[1]),
        local(up_h.at[0], wup, lsem.at[2]),
        local(down_h.at[0], wdown, lsem.at[3]),
    ]

    def first_x(m):
        return remote(rin.at[m, pl.ds(0, half)], rin.at[m, pl.ds(half, half)], xs.at[m], xr.at[m], to_x)

    def first_c(m):
        return remote(gin.at[m, pl.ds(0, half)], gin.at[m, pl.ds(half, half)], xs.at[m], xr.at[m], to_x)

    @pl.when(s == 0)
    def _():
        own_x.start()

    @pl.when(s == 1)
    def _():
        own_c.start()

    for c in loads:
        c.start()

    barrier = pltpu.get_barrier_semaphore()
    greet(lambda to: pl.semaphore_signal(barrier, inc=1, device_id=to, device_id_type=MESH))
    pl.semaphore_wait(barrier, jnp.where(inner, 6, 5))

    @pl.when(s == 0)
    def _():
        own_x.wait()
        first_x(0).start()

    jj = lax.broadcasted_iota(jnp.int32, (rows, rows), 0)
    ii = lax.broadcasted_iota(jnp.int32, (rows, rows), 1)
    j_own, i_own = jj < half, ii < half
    inside = ((j_own == i_own) & (jj <= ii)).astype(F32)
    own_first = jnp.where(xi == 0, 1.0, 0.0)
    across = jnp.where(j_own & ~i_own, own_first, jnp.where(i_own & ~j_own, 1.0 - own_first, 0.0))
    slots = starts.shape[2]
    for m in range(micro):
        n0 = jnp.int32(0)
        n1 = jnp.int32(0)
        for j in range(slots):
            n0 += jnp.where(starts[m, 0, j] <= 0, 1, 0)
            n1 += jnp.where(starts[m, 0, j] <= STRETCH, 1, 0)
        same = jnp.where(n0 == n1, 1.0, 0.0)
        mask[m] = inside + across * same

    def live_of(m, part):
        block = xi if part == 0 else 1 - xi
        begin = jnp.int32(0)
        for j in range(slots):
            begin = jnp.where(starts[m, 0, j] <= block * STRETCH, jnp.maximum(begin, starts[m, 0, j]), begin)
        length = jnp.int32(0)
        for j in range(slots):
            length += jnp.where(starts[m, 0, j] == begin, lengths[m, 0, j], 0)
        row = block * STRETCH + lax.broadcasted_iota(jnp.int32, (half, width), 0)
        return (row - begin < length).astype(F32)

    def block_of(kind, p, q):
        i = p * 2 + q
        return nm_all.at[i] if kind == 0 else gd_all.at[slot(i)]

    class Gather:
        def __init__(self, kind, layer):
            self.kind, self.layer = kind, layer
            self.core = kind
            self.same = layer == kind

        def held(self, p):
            if self.same:
                return block_of(self.kind, p, par)
            return (hnm, hgd)[self.kind].at[p]

        def arrival(self, p):
            return la.at[self.kind, p * 2 + par] if self.same else ha.at[p]

        def send(self, i):
            return fs.at[0 if self.same else 1, i]

        def to(self, core, p, q):
            return (core, base + p * 2 + q, xi)

        def up(self):
            return remote(block_of(self.kind, pos, par), self.held(pos), us.at[0], ha.at[pos], to_c)

        def step(self, i, p, q, ref):
            return remote(ref, self.held(p), self.send(i), self.arrival(p), self.to(self.core, q, par))

        def pair(self, i, p, ref):
            return remote(
                ref, block_of(self.kind, p, par), self.send(i), la.at[self.kind, p * 2 + par], self.to(self.layer, pos, 1 - par)
            )

        def home(self, i, p, ref):
            return remote(
                ref, block_of(self.kind, p, par), self.send(i), la.at[self.kind, p * 2 + par], self.to(self.layer, pos, par)
            )

        def moves(self, way, j):
            p = pos - j if way == 0 else pos + j
            ref = self.held(p)
            i = 3 + (way * (LINE - 1) + j - 1) * 3
            if j == 0:
                return [
                    (self.step(0, p, pos + 1, ref), pos < LINE - 1),
                    (self.step(1, p, pos - 1, ref), pos > 0),
                    (self.pair(2, p, ref), None),
                ]
            came = (p >= 0) if way == 0 else (p < LINE)
            q = pos + 1 if way == 0 else pos - 1
            goes = (q < LINE) if way == 0 else (q >= 0)
            out = [(self.step(i, p, q, ref), came & goes), (self.pair(i + 1, p, ref), came)]
            if not self.same:
                out.append((self.home(i + 2, p, ref), came))
            return out

        def each(self, way, j, what):
            for copy, when in self.moves(way, j):
                if when is None:
                    what(copy)
                else:
                    pl.when(when)(functools.partial(what, copy))

        def own(self):
            if not self.same:
                self.up().wait_recv()
            self.each(0, 0, lambda c: c.start())

        def pass_on(self, j):
            for way in range(2):
                p = pos - j if way == 0 else pos + j

                @pl.when((p >= 0) if way == 0 else (p < LINE))
                def _():
                    self.step(0, p, pos, self.held(p)).wait_recv()

                self.each(way, j, lambda c: c.start())

        def sent(self):
            self.each(0, 0, lambda c: c.wait_send())
            for way in range(2):
                for j in range(1, LINE):
                    self.each(way, j, lambda c: c.wait_send())

        def complete(self):
            for k in range(LINE):
                p = lax.rem(pos + k, LINE)
                ref = block_of(self.kind, p, 1 - par)
                remote(ref, ref, fs.at[0, 0], la.at[self.kind, p * 2 + 1 - par], to_y).wait_recv()
                if k > 0 and not self.same:
                    ref = block_of(self.kind, p, par)
                    remote(ref, ref, fs.at[0, 0], la.at[self.kind, p * 2 + par], to_c).wait_recv()

    nm0, nm1, gd0, gd1 = Gather(0, 0), Gather(0, 1), Gather(1, 0), Gather(1, 1)

    def grad_rows(m):
        return pl.ds(pl.multiple_of(g * span + m * rows, rows), rows)

    @pl.when(s == 0)
    def _():
        first_x(0).wait_recv()
        for m in range(1, micro):
            first_x(m).start()
        pl.semaphore_signal(turn, inc=1, device_id=to_c, device_id_type=MESH)

    @pl.when(s == 1)
    def _():
        for c in loads:
            c.wait()
        wupt[...] = wup[...].T
        own_c.wait()
        pl.semaphore_wait(turn, 1)
        for m in range(micro):
            first_c(m).start()
        for m in range(micro):
            first_c(m).wait_recv()
        for m in range(micro):
            for part in range(2):
                pr = pl.ds(part * half, half)
                to = pl.ds(pl.multiple_of(g * span + m * rows + part * half, half), half)
                gd_all[to] = (gin[m, pr].astype(F32) * live_of(m, part)).astype(BF)
        gd1.own()
        gd1.pass_on(1)

    def x_swap(e, m):
        i = (1 + e) * micro + m
        return remote(sbuf.at[e, m], rbuf.at[e, m], xs.at[i], xr.at[i], to_x)

    def give(e, m, part):
        part = part.astype(BF)
        sbuf[e, m, pl.ds(0, half)] = part[half:]
        sbuf[e, m, pl.ds(half, half)] = part[:half]
        x_swap(e, m).start()

    def c_copy(e, m):
        i = e * micro + m
        src, dst = ((act, rin), (igv, gin))[e]
        return remote(src.at[m], dst.at[m], cs.at[i], cr.at[i], to_c)

    def y_copies(when):
        out = []
        if when == 0:
            pairs = [(nrm_t, ynrm), (mtb, ymtb)]
        else:
            pairs = [
                (gpt.at[1 - par], ygpt.at[0]),
                (gpt.at[2], ygpt.at[1]),
                (gbr.at[:, pl.ds(pl.multiple_of((1 - par) * hw, 128), hw)], ygbr),
                (sb.at[1 - par], ysb),
            ]
        for i, (src, dst) in enumerate(pairs):
            j = 2 * when + i
            out.append(remote(src, dst, ys.at[j], yr.at[j], to_y))
        return out

    def mixer_forward(m):
        @pl.when(s == 0)
        def _():
            if m > 0:
                first_x(m).wait_recv()

        @pl.when(s == 1)
        def _():
            c_copy(0, m).wait_recv()

        if m == 0:
            @pl.when(s == 0)
            def _():
                loads[0].wait()
        r = rin[m].astype(F32)
        n = (normed(r)[0] * gain1[...]).astype(BF)
        nrm_t[:, cols(m)] = n.T
        for q in range(3):
            p = dot(n, wqkv[q]).astype(BF)
            if q == 2:
                vnat[m] = p
            pt[q, :, cols(m)] = p.T
        for h in range(heads):
            hr = pl.ds(h * hs, hs)
            w = fmap[0, h]
            qfh = both_softmax(dot(w, pt[0, hr, cols(m)], 0, 0))
            kfh = both_softmax(dot(w, pt[1, hr, cols(m)], 0, 0))
            qf[m, h] = qfh
            kf[m, h] = kfh
            sc = dot(kfh, qfh, 0, 0) * mask[m]
            den = 1.0 / jnp.sum(sc, axis=0, keepdims=True)
            scb = sc.astype(BF)
            st[m, h] = scb
            den_s[m, h] = jnp.broadcast_to(den, (8, rows))
            mx = dot(pt[2, hr, cols(m)], scb) * den
            mt[m, hr] = mx
            mtb[hr, cols(m)] = mx.astype(BF)
        if m == 0:
            @pl.when(s == 0)
            def _():
                loads[1].wait()
        part = dot(mtb[:, cols(m)].T, wmix[...])
        give(0, m, part)
        rmid[m] = r + part

    def ffn_forward(m):
        x_swap(0, m).wait_recv()
        r = rmid[m] + rbuf[0, m].astype(F32)
        rmid[m] = r
        n = (normed(r)[0] * gain2[...]).astype(BF)
        nm_all[g, :, cols(m)] = n.T
        if m == 0:
            @pl.when(s == 0)
            def _():
                loads[2].wait()
                loads[3].wait()
        h, slope = gelu_both(dot(n, wup[...]))
        h = h.astype(BF)
        gp[m] = slope.astype(BF)
        part = dot(h, wdown[...])
        give(1, m, part)
        part_f[m] = r + part

    def act_copy(m):
        return local(act.at[m, pl.ds(0, half)], act_o.at[0, m], osem.at[m])

    def ig_copy(m):
        return local(igv.at[m, pl.ds(0, half)], ig_o.at[0, m], osem.at[micro + m])

    def end_forward(m):
        x_swap(1, m).wait_recv()
        act[m] = (part_f[m] + rbuf[1, m].astype(F32)).astype(BF)

        @pl.when(s == 0)
        def _():
            c_copy(0, m).start()

        act_copy(m).start()

    for m in range(micro):
        mixer_forward(m)
    @pl.when(s == 1)
    def _():
        gd1.pass_on(2)

    @pl.when(s == 0)
    def _():
        for c in y_copies(0):
            c.start()

    for m in range(micro):
        ffn_forward(m)

    @pl.when(s == 0)
    def _():
        nm0.own()

    @pl.when(s == 1)
    def _():
        nm1.up().start()
        gd1.pass_on(3)

    for m in range(micro):
        end_forward(m)

    tile = 512
    tiles = ff // tile

    def hid_rows(t):
        return pl.ds(pl.multiple_of(t * tile, tile), tile)

    def hidden_ahead(lo, hi, which):
        def one(k, carry):
            i = which(k)
            for t in range(tiles):
                h, slope = gelu_both(dot(wupt[hid_rows(t)], nm_all[i]))
                hb[hid_rows(t), slot(i)] = h.astype(BF)
                gb[hid_rows(t), slot(i)] = slope.astype(BF)
            return carry

        lax.fori_loop(lo, hi, one, 0)

    @pl.when(s == 0)
    def _():
        wupt[...] = wup[...].T
        nm0.pass_on(1)
        hidden_ahead(0, 1, lambda k: g)
        nm0.pass_on(2)
        nm1.own()
        nm0.pass_on(3)
        nm1.pass_on(1)
        hidden_ahead(1, LINE, lambda k: lax.rem(pos + k, LINE) * 2 + par)
        nm1.pass_on(2)
        nm1.pass_on(3)

    def ffn_back(m):
        @pl.when(s == 0)
        def _():
            c_copy(1, m).wait_recv()
            gd_all[grad_rows(m)] = gin[m]

        gd = gd_all[grad_rows(m)]
        gpre = (dot(gd, wdown[...], 1, 1) * gp[m].astype(F32)).astype(BF)
        part = dot(gpre, wup[...], 1, 1)
        give(2, m, part)
        part_f[m] = part

    def mixer_back(m):
        x_swap(2, m).wait_recv()
        gn = part_f[m] + rbuf[2, m].astype(F32)
        xhat, rstd = normed(rmid[m])
        gacc[1, m] = jnp.broadcast_to(jnp.sum(gn * xhat, axis=0, keepdims=True), (8, width))
        gm = gd_all[grad_rows(m)].astype(F32) + norm_back(gn, gain2[...], xhat, rstd)
        rmid[m] = gm
        gb_ = gm.astype(BF)
        gbr[cols(m)] = gb_
        gmt = dot(wmix[...], gb_, 1, 1).astype(BF)
        for h in range(heads):
            hr = pl.ds(h * hs, hs)
            den = den_s[m, h, pl.ds(0, 1)]
            go = gmt[h * hs : (h + 1) * hs].astype(F32)
            gden = -jnp.sum(go * mt[m, hr], axis=0, keepdims=True) * den
            gnum = (go * den).astype(BF)
            pad = jnp.zeros_like(gnum)
            wide = jnp.concatenate([gnum, pad] if h % 2 == 0 else [pad, gnum], axis=0)
            gst = ((dot(vnat[m, :, pl.ds((h // 2) * 2 * hs, 2 * hs)], wide) + gden) * mask[m]).astype(BF)
            qfh = qf[m, h]
            kfh = kf[m, h]
            gql = softmax_back(dot(kfh, gst), qfh).astype(BF)
            gkl = softmax_back(dot(qfh, gst, 1, 1), kfh).astype(BF)
            gv = dot(gnum, st[m, h], 1, 1).astype(BF)
            gqk[0, hr, cols(m)] = gql
            gqk[1, hr, cols(m)] = gkl
            w = fmap[0, h]
            gpt[0, hr, cols(m)] = dot(w, gql).astype(BF)
            gpt[1, hr, cols(m)] = dot(w, gkl).astype(BF)
            gpt[2, hr, cols(m)] = gv
        gnt = dot(wqkv[0], gpt[0, :, cols(m)]) + dot(wqkv[1], gpt[1, :, cols(m)]) + dot(wqkv[2], gpt[2, :, cols(m)])
        part = gnt.T
        give(3, m, part)
        part_f[m] = part

    def end_back(m):
        x_swap(3, m).wait_recv()
        gn = part_f[m] + rbuf[3, m].astype(F32)
        xhat, rstd = normed(rin[m].astype(F32))
        gacc[0, m] = jnp.broadcast_to(jnp.sum(gn * xhat, axis=0, keepdims=True), (8, width))
        igv[m] = (rmid[m] + norm_back(gn, gain1[...], xhat, rstd)).astype(BF)

        @pl.when(s == 1)
        def _():
            c_copy(1, m).start()

        ig_copy(m).start()

    for m in range(micro):
        ffn_back(m)

    @pl.when(s == 0)
    def _():
        gd0.up().start()

    for m in range(micro):
        mixer_back(m)
    late = y_copies(1)

    @pl.when(s == 0)
    def _():
        for c in late[:3]:
            c.start()

    cut = width // hw
    q_rows = pl.ds(0, width)
    v_rows = pl.ds(width, width // 2)
    m_rows = pl.ds(width + width // 2, hw)
    s_rows = pl.ds(width + width // 2 + hw, hs)
    v_part = pl.ds(pl.multiple_of(par * (width // 2), 16), width // 2)
    m_part = pl.ds(pl.multiple_of(par * hw, 128), hw)

    left = lax.broadcasted_iota(jnp.int32, (hs, 2 * hs), 1) < hs
    for p in range(heads // 2):
        pr = pl.ds(p * 2 * hs, 2 * hs)
        tot = dot(pt[0, pr], gqk[0, pr], 1, 1) + dot(pt[1, pr], gqk[1, pr], 1, 1)
        sb[0, :, pr] = jnp.where(left, tot[:hs], tot[hs:]).astype(BF)

    for m in range(micro):
        end_back(m)

    row = lax.broadcasted_iota(jnp.int32, (hs, hw), 0)
    block = jnp.zeros((hs, hw), F32)
    for e in range(2):
        tot = gacc[e, 0, pl.ds(0, 1)]
        for m in range(1, micro):
            tot += gacc[e, m, pl.ds(0, 1)]
        for c in range(cut):
            block = jnp.where(row == e * cut + c, tot[:, c * hw : (c + 1) * hw], block)
    sb[1] = block.astype(BF)

    part_rows = hp.shape[0] // 2
    chunk = part_rows // 4

    class Line:
        def __init__(self, n):
            self.n = n

        def piece(self, near, j):
            group = side if near else 1 - side
            return pl.ds(pl.multiple_of((group * self.n + j) * chunk, 16), chunk)

        def final(self, near, j):
            if self.n == 4:
                return fin.at[self.piece(near, j)]
            group = side if near else 1 - side
            return fin.at[pl.ds(pl.multiple_of(par * part_rows + (group * self.n + j) * chunk, 16), chunk)]

        def send_in(self, near, j):
            i = 4 * near + j
            return remote(hp.at[self.piece(near, j)], from_out.at[i], ars.at[i], arr.at[i], to_mate)

        def send_over(self, j):
            return remote(hp.at[self.piece(0, j)], from_opp.at[j], ars.at[8 + j], arr.at[8 + j], to_opp)

        def total_over(self, j):
            ref = self.final(1, j)
            return remote(ref, ref, ars.at[12 + j], arr.at[12 + j], to_opp)

        def total_out(self, near, j):
            i = 16 + 4 * near + j
            ref = self.final(near, j)
            return remote(ref, ref, ars.at[i], arr.at[i], to_mate)

        def total_pair(self, near, j):
            i = 24 + 4 * near + j
            ref = self.final(near, j)
            return remote(ref, ref, ars.at[i], arr.at[i], to_y)

        def trade(self, j):
            return remote(hp.at[self.piece(1, j)], from_pair.at[j], ars.at[24 + j], arr.at[24 + j], to_y)

        def start(self):
            @pl.when(outer)
            def _():
                for near in range(2):
                    for j in range(self.n):
                        self.send_in(near, j).start()

        def collect(self, j):
            @pl.when(inner)
            def _():
                self.send_in(0, j).wait_recv()
                p = self.piece(0, j)
                hp[p] = (hp[p].astype(F32) + from_out[j].astype(F32)).astype(BF)
                self.send_over(j).start()

        def total(self, j):
            @pl.when(inner)
            def _():
                self.send_in(1, j).wait_recv()
                self.send_over(j).wait_recv()
                p = self.piece(1, j)
                tot = hp[p].astype(F32) + from_out[4 + j].astype(F32) + from_opp[j].astype(F32)
                if self.n == 4:
                    hp[p] = tot.astype(BF)
                    self.trade(j).start()
                else:
                    self.final(1, j)[...] = tot.astype(BF)
                    self.total_out(1, j).start()
                    self.total_over(j).start()

            if self.n == 2:
                @pl.when(outer)
                def _():
                    self.total_out(1, j).wait_recv()

                self.total_pair(1, j).start()

        def settle(self, j):
            @pl.when(inner)
            def _():
                self.trade(j).wait_recv()
                tot = hp[self.piece(1, j)].astype(F32) + from_pair[j].astype(F32)
                self.final(1, j)[...] = tot.astype(BF)
                self.total_out(1, j).start()
                self.total_over(j).start()

            @pl.when(outer)
            def _():
                self.total_out(1, j).wait_recv()

        def passed(self, j):
            @pl.when(inner)
            def _():
                self.total_over(j).wait_recv()
                self.total_out(0, j).start()

            @pl.when(outer)
            def _():
                self.total_out(0, j).wait_recv()

            if self.n == 2:
                self.total_pair(0, j).start()

        def finish(self):
            for j in range(self.n):
                @pl.when(outer)
                def _():
                    self.send_in(0, j).wait_send()
                    self.send_in(1, j).wait_send()

                @pl.when(inner)
                def _():
                    self.send_over(j).wait_send()
                    self.total_over(j).wait_send()
                    self.total_out(0, j).wait_send()
                    self.total_out(1, j).wait_send()
                    if self.n == 4:
                        self.trade(j).wait_send()

                if self.n == 2:
                    self.total_pair(0, j).wait_send()
                    self.total_pair(1, j).wait_send()

    first, second = Line(2), Line(4)

    def joined():
        for i in range(GROUP):
            nm_cat[:, pl.ds(i * span, span)] = nm_all[i]

    def grads_in(t):
        def one(i, carry):
            hr, sl = hid_rows(t), slot(i)
            gb[hr, sl] = (dot(wdown[hr], gd_all[sl], 1, 1) * gb[hr, sl].astype(F32)).astype(BF)
            return carry

        lax.fori_loop(0, GROUP, one, 0, unroll=2)

    def up_copy(t):
        return local(wup.at[:, hid_rows(t)], up_o.at[:, hid_rows(t)], osem.at[2 * micro + 10 + t])

    def down_copy(t):
        return local(wdown.at[hid_rows(t)], down_o.at[hid_rows(t)], osem.at[2 * micro + 10 + tiles + t])

    def grads_up(t):
        wup[:, hid_rows(t)] = dot(nm_cat[...], gb[hid_rows(t)], 1, 1).astype(BF)
        up_copy(t).start()

    def grads_down(t):
        wdown[hid_rows(t)] = dot(hb[hid_rows(t)], gd_all[...]).astype(BF)
        down_copy(t).start()

    @pl.when(s == 0)
    def _():
        late[3].start()
        for c in y_copies(0) + late:
            c.wait_recv()
        hp[q_rows] = (dot(nrm_t[...], gpt[par], 1, 1) + dot(ynrm[...], ygpt[0], 1, 1)).astype(BF)
        hp[v_rows] = (dot(nrm_t[v_part], gpt[2], 1, 1) + dot(ynrm[v_part], ygpt[1], 1, 1)).astype(BF)
        hp[m_rows] = (dot(mtb[...], gbr[:, m_part]) + dot(ymtb[...], ygbr[...])).astype(BF)
        hp[s_rows] = (sb[par].astype(F32) + ysb[...].astype(F32)).astype(BF)
        first.start()
        nm0.complete()

    @pl.when(s == 1)
    def _():
        gd0.own()
        for q in range(3):
            hp[pl.ds(q * width, width)] = dot(nrm_t[...], gpt[q], 1, 1).astype(BF)
        tot = dot(mtb[...], gbr[...]).astype(BF)
        for c in range(cut):
            hp[pl.ds(3 * width + c * hw, hw)] = tot[:, c * hw : (c + 1) * hw]
        for e in range(2):
            hp[pl.ds(3 * width + cut * hw + e * hs, hs)] = sb[e]
        second.start()
        gd0.pass_on(1)
        second.collect(0)
        gd0.pass_on(2)
        second.collect(1)
        nm1.complete()
        gd1.complete()

    hidden_ahead(0, jnp.where(s == 0, LINE, GROUP), lambda k: lax.rem(g + jnp.where(s == 0, 2 * k + 1 - 2 * par, k) + GROUP, GROUP))
    joined()

    @pl.when(s == 0)
    def _():
        first.collect(0)
        first.collect(1)
        gd0.complete()

    @pl.when(s == 1)
    def _():
        gd0.pass_on(3)

    plan = {
        (0, 0): ([], [("collect", 2)]),
        (0, 1): ([("total", 0)], [("collect", 3)]),
        (0, 2): ([], []),
        (1, 0): ([("total", 1)], []),
        (1, 1): ([("passed", 0)], [("total", 0)]),
        (1, 2): ([], [("total", 1)]),
        (2, 0): ([("passed", 1)], [("settle", 0)]),
        (2, 1): ([], [("total", 2), ("settle", 1)]),
        (2, 2): ([], [("total", 3)]),
    }

    def between(t, part):
        for (at_t, at_part), steps in plan.items():
            for layer, line in enumerate((first, second)):
                if at_part == part and steps[layer]:
                    @pl.when((s == layer) & (t == at_t))
                    def _():
                        for name, j in steps[layer]:
                            getattr(line, name)(j)

    def one_tile(t, carry):
        grads_in(t)
        between(t, 0)
        grads_up(t)
        between(t, 1)
        grads_down(t)
        between(t, 2)
        return carry

    lax.fori_loop(0, tiles, one_tile, 0)

    @pl.when(s == 0)
    def _():
        for near in range(2):
            for j in range(2):
                first.total_pair(near, j).wait_recv()

    @pl.when(s == 1)
    def _():
        second.settle(2)
        second.settle(3)
        for j in range(4):
            second.passed(j)

    def outs_of(layer, out_copy):
        if layer == 1:
            out_copy(fin.at[pl.ds(0, 3 * width)], qkv_o)
            for c in range(cut):
                out_copy(fin.at[pl.ds(3 * width + c * hw, hw)], mix_o.at[:, pl.ds(c * hw, hw)])
            for e in range(2):
                out_copy(fin.at[pl.ds(3 * width + cut * hw + e * hs, hs)], small_o.at[e])
            return
        for e in range(2):
            at = e * part_rows
            out_copy(fin.at[pl.ds(at, width)], qkv_o.at[pl.ds(e * width, width)])
            at += width
            out_copy(fin.at[pl.ds(at, width // 2)], qkv_o.at[pl.ds(2 * width + e * (width // 2), width // 2)])
            at += width // 2
            out_copy(fin.at[pl.ds(at, hw)], mix_o.at[:, pl.ds(e * hw, hw)])
            at += hw
            out_copy(fin.at[pl.ds(at, hs)], small_o.at[e])

    def ended(layer):
        mine = []

        def keep(src, dst):
            c = local(src, dst, osem.at[2 * micro + 2 + len(mine)])
            c.start()
            mine.append(c)

        outs_of(layer, keep)
        for c in mine:
            c.wait()

    for t in range(tiles):
        up_copy(t).wait()
        down_copy(t).wait()

    @pl.when(s == 0)
    def _():
        ended(0)

    @pl.when(s == 1)
    def _():
        ended(1)

    @pl.when(s == 0)
    def _():
        for m in range(micro):
            first_x(m).wait_send()
            c_copy(0, m).wait_send()

    @pl.when(s == 1)
    def _():
        for m in range(micro):
            first_c(m).wait_send()
            c_copy(1, m).wait_send()

    for e in range(4):
        for m in range(micro):
            x_swap(e, m).wait_send()
    @pl.when(s == 0)
    def _():
        nm0.sent()
        nm1.sent()
        gd0.up().wait_send()

    @pl.when(s == 1)
    def _():
        gd1.sent()
        gd0.sent()
        nm1.up().wait_send()

    @pl.when(s == 0)
    def _():
        for c in y_copies(0) + y_copies(1):
            c.wait_send()
        first.finish()

    @pl.when(s == 1)
    def _():
        second.finish()

    for m in range(micro):
        act_copy(m).wait()
        ig_copy(m).wait()


def widen(qkv, mix, small, up, down, qkv_o, mix_o, feat_o, g1_o, g2_o, up_o, down_o, sem_in, sem_out, *bufs):
    hs = feat_o.shape[2]
    hw = mix.shape[0]
    cut = mix.shape[1] // hw
    blocks = []
    for src, dst, step in ((up, up_o, 192), (down, down_o, 384), (qkv, qkv_o, 768), (mix, mix_o, 192)):
        for lo in range(0, src.shape[0], step):
            if dst is qkv_o:
                blocks.append((src.at[pl.ds(lo, step)], dst.at[0, lo // step]))
            else:
                blocks.append((src.at[pl.ds(lo, step)], dst.at[0, pl.ds(lo, step)]))
    half = len(blocks)
    narrow, wide = bufs[:half], bufs[half : 2 * half]
    small_v, feat_v, g1_v, g2_v = bufs[2 * half :]
    first = pltpu.make_async_copy(small, small_v, sem_in.at[half])
    first.start()
    loads = [pltpu.make_async_copy(b[0], n, sem_in.at[i]) for i, (b, n) in enumerate(zip(blocks, narrow))]
    for c in loads:
        c.start()
    outs = []

    def put(src, dst, i):
        c = pltpu.make_async_copy(src, dst, sem_out.at[i])
        c.start()
        outs.append(c)

    first.wait()
    for h in range(feat_v.shape[1]):
        feat_v[0, h] = small_v[0, pl.ds(0, hs), pl.ds(h * hs, hs)].astype(F32)
    for c in range(cut):
        cs = pl.ds(c * hw, hw)
        g1_v[:, cs] = small_v[1, pl.ds(0, 16)].astype(F32)[c : c + 1]
        g2_v[:, cs] = small_v[1, pl.ds(0, 16)].astype(F32)[cut + c : cut + c + 1]
    put(feat_v, feat_o, half)
    put(g1_v, g1_o, half + 1)
    put(g2_v, g2_o, half + 2)
    for i, (b, n, w) in enumerate(zip(blocks, narrow, wide)):
        loads[i].wait()
        w[...] = n[...].astype(F32)
        put(w, b[1], i)
    for c in outs:
        c.wait()


def on_device(x, cot, starts, lengths, gain1, wqkv, fmap, wmix, gain2, wup, wdown):
    micro, half, width = x.shape
    rows = 2 * half
    span = micro * rows
    heads, hs = fmap.shape[1], fmap.shape[2]
    hw = heads * hs
    ff = wup.shape[2]
    cut = width // hw
    part_rows = width + width // 2 + hw + hs
    f, b = F32, BF
    vm = pltpu.VMEM
    dma = pltpu.SemaphoreType.DMA
    out = lambda shape, t=b: jax.ShapeDtypeStruct(shape, t)
    act, ig, qkv, mix, small, up, down = pl.pallas_call(
        kernel,
        out_shape=[
            out((1, micro, half, width)),
            out((1, micro, half, width)),
            out((3 * width, hw)),
            out((hw, width)),
            out((2, hs, hw)),
            out((width, ff)),
            out((ff, width)),
        ],
        in_specs=[ANY, ANY, SM, SM, VM, ANY, VM, ANY, VM, ANY, ANY],
        out_specs=[ANY] * 7,
        scratch_shapes=[
            vm((3, width, hw), b),
            vm((hw, width), b),
            vm((width, ff), b),
            vm((ff, width), b),
            vm((ff, width), b),
            vm((micro, rows, width), b),
            vm((micro, rows, width), b),
            vm((micro, rows, rows), f),
            vm((width, span), b),
            vm((3, hw, span), b),
            vm((micro, rows, hw), b),
            vm((micro, heads, 2 * hs, rows), b),
            vm((micro, heads, 2 * hs, rows), b),
            vm((micro, heads, rows, rows), b),
            vm((micro, hw, rows), f),
            vm((hw, span), b),
            vm((micro, heads, 8, rows), f),
            vm((micro, rows, width), f),
            vm((GROUP, width, span), b),
            vm((width, GROUP * span), b),
            vm((GROUP * span, width), b),
            vm((ff, GROUP * span), b),
            vm((ff, GROUP * span), b),
            vm((micro, rows, ff), b),
            vm((micro, rows, width), f),
            vm((micro, rows, width), b),
            vm((micro, rows, width), b),
            vm((span, width), b),
            vm((2, hw, span), b),
            vm((3, hw, span), b),
            vm((2, micro, 8, width), f),
            vm((4, micro, rows, width), b),
            vm((4, micro, rows, width), b),
            vm((width, span), b),
            vm((hw, span), b),
            vm((2, hw, span), b),
            vm((span, hw), b),
            vm((2, hs, hw), b),
            vm((hs, hw), b),
            vm((2 * part_rows, hw), b),
            vm((2 * part_rows, hw), b),
            vm((8, part_rows // 4, hw), b),
            vm((4, part_rows // 4, hw), b),
            vm((4, part_rows // 4, hw), b),
            vm((LINE, width, span), b),
            vm((LINE, span, width), b),
            dma((5,)),
            dma((5 * micro,)),
            dma((5 * micro,)),
            dma((2 * micro,)),
            dma((2 * micro,)),
            dma((2, GROUP)),
            dma((LINE,)),
            dma((2, 21)),
            dma((1,)),
            dma((6,)),
            dma((6,)),
            dma((32,)),
            dma((32,)),
            dma((2 * micro + 16,)),
            pltpu.SemaphoreType.REGULAR,
        ],
        compiler_params=pltpu.CompilerParams(
            collective_id=0, has_side_effects=True, vmem_limit_bytes=60 * 1024 * 1024
        ),
    )(x, cot, starts, lengths, gain1, wqkv, fmap, wmix, gain2, wup, wdown)

    n = lax.axis_size("dp")
    if n > GROUP:
        same_place = [[i + j * GROUP for j in range(n // GROUP)] for i in range(GROUP)]
        qkv, mix, small, up, down = lax.psum((qkv, mix, small, up, down), "dp", axis_index_groups=same_place)

    shapes = []
    for a, step in ((up, 192), (down, 384), (qkv, 768), (mix, 192)):
        shapes += [(step, a.shape[1])] * (a.shape[0] // step)
    outs = [(1, 3, width, hw), (1, hw, width), (1, heads, hs, hs), (1, width), (1, width), (1, width, ff), (1, ff, width)]
    qkv, mix, features, g1, g2, up, down = pl.pallas_call(
        widen,
        out_shape=[out(o, f) for o in outs],
        in_specs=[ANY] * 5,
        out_specs=[ANY] * 7,
        scratch_shapes=[dma((len(shapes) + 1,)), dma((len(shapes) + 3,))]
        + [vm(o, b) for o in shapes]
        + [vm(o, f) for o in shapes]
        + [vm(small.shape, b), vm(outs[2], f), vm(outs[3], f), vm(outs[4], f)],
        compiler_params=pltpu.CompilerParams(vmem_limit_bytes=60 * 1024 * 1024),
    )(qkv, mix, small, up, down)
    return act, ig, g1, qkv, features, mix, g2, up, down


def solution(mesh):
    in_specs = (
        P(None, ("dp", "mp"), None),
        P(None, ("dp", "mp"), None),
        P(None, "dp", None),
        P(None, "dp", None),
        P("section", None),
        P("section", None, None, "mp"),
        P("section", "mp", None, None),
        P("section", "mp", None),
        P("section", None),
        P("section", None, "mp"),
        P("section", "mp", None),
    )
    out_specs = (
        P("section", None, ("dp", "mp"), None),
        P("section", None, ("dp", "mp"), None),
        P("section", None),
        P("section", None, None, "mp"),
        P("section", "mp", None, None),
        P("section", "mp", None),
        P("section", None),
        P("section", None, "mp"),
        P("section", "mp", None),
    )
    return jax.shard_map(
        on_device, mesh=mesh, in_specs=in_specs, out_specs=out_specs, check_vma=False
    )
```

```python
import functools

import functools

import jax
import jax.numpy as jnp
from jax import lax
from jax.experimental import pallas as pl
from jax.experimental.pallas import tpu as pltpu
from jax.sharding import PartitionSpec as P

STRETCH = 64
GROUP = 8
LINE = 4
MESH = pl.DeviceIdType.MESH
BF = jnp.bfloat16
F32 = jnp.float32
ANY = pl.BlockSpec(memory_space=pl.ANY)
VM = pl.BlockSpec(memory_space=pltpu.VMEM)
SM = pl.BlockSpec(memory_space=pltpu.SMEM)


def dot(a, b, ca=1, cb=0):
    return lax.dot_general(a, b, (((ca,), (cb,)), ((), ())), preferred_element_type=F32)


def normed(v):
    mean = jnp.mean(v, axis=1, keepdims=True)
    c = v - mean
    rstd = lax.rsqrt(jnp.mean(c * c, axis=1, keepdims=True) + 1e-05)
    return c * rstd, rstd


def norm_back(grad, gain, xhat, rstd):
    t = grad * gain
    mean_t = jnp.mean(t, axis=1, keepdims=True)
    mean_tx = jnp.mean(t * xhat, axis=1, keepdims=True)
    return rstd * (t - mean_t - xhat * mean_tx)


def gelu_both(x):
    k = 0.7978845608028654
    x2 = x * x
    g = 0.5 + 0.5 * jnp.tanh(x * (k + (k * 0.044715) * x2))
    h = x * g
    return h, g + h * (1.0 - g) * (2.0 * k + (6.0 * k * 0.044715) * x2)


def both_softmax(logit):
    up = jnp.exp(logit - jnp.max(logit, axis=0, keepdims=True))
    down = jnp.exp(jnp.min(logit, axis=0, keepdims=True) - logit)
    up = up * (1.0 / jnp.sum(up, axis=0, keepdims=True))
    down = down * (1.0 / jnp.sum(down, axis=0, keepdims=True))
    return jnp.concatenate([up.astype(BF), down.astype(BF)], axis=0)


def softmax_back(grad, feat):
    n = grad.shape[0] // 2
    g = grad * feat.astype(F32)
    p = feat.astype(F32)
    one = g[:n] - p[:n] * jnp.sum(g[:n], axis=0, keepdims=True)
    two = g[n:] - p[n:] * jnp.sum(g[n:], axis=0, keepdims=True)
    return one - two


def kernel(
    x_in, cot, starts, lengths, gain1, wqkv_h, fmap, wmix_h, gain2, up_h, down_h,
    act_o, ig_o, qkv_o, mix_o, small_o, up_o, down_o,
    wqkv, wmix, wup, wdown, wupt, rin, gin, mask,
    nrm_t, pt, vnat, qf, kf, st, mt, mtb, den_s, rmid, nm_all, nm_cat, gd_all, hb, gb, gp, part_f, act, igv,
    gbr, gqk, gpt, gacc, sbuf, rbuf,
    ynrm, ymtb, ygpt, ygbr, sb, ysb, hp, fin, from_out, from_opp, from_pair, hgd, hgw,
    lsem, xs, xr, cs, cr, la, ha, fs, hws, ys, yr, ars, arr, osem, tsem,
):
    s = lax.axis_index("section")
    d = lax.axis_index("dp")
    xi = lax.axis_index("mp")
    micro, half, width = x_in.shape
    rows = 2 * half
    span = micro * rows
    heads, hs = fmap.shape[1], fmap.shape[2]
    hw = heads * hs
    ff = up_h.shape[2]
    g = lax.rem(d, GROUP)
    base = d - g
    pos = lax.div(g, 2)
    par = lax.rem(g, 2)
    to_x = (s, d, 1 - xi)
    to_c = (1 - s, d, xi)
    to_y = (s, base + pos * 2 + 1 - par, xi)
    outer = (pos == 0) | (pos == LINE - 1)
    inner = (pos > 0) & (pos < LINE - 1)
    side = lax.div(pos, 2)
    to_mate = (s, base + (side * 4 + 1 - pos) * 2 + par, xi)
    to_opp = (s, base + (LINE - 1 - pos) * 2 + par, xi)

    def other_core(to):
        return (1 - s,) + to[1:]

    def other_core(to):
        return (1 - s,) + to[1:]

    def at(core, p, q):
        return (core, base + p * 2 + q, xi)

    def greet(act):
        for to in (to_x, to_c, to_y, other_core(to_y)):
            act(to)
        pl.when(pos < LINE - 1)(lambda: act(at(s, pos + 1, par)))
        pl.when(pos > 0)(lambda: act(at(s, pos - 1, par)))

    def local(src, dst, sem):
        return pltpu.make_async_copy(src, dst, sem)

    def remote(src, dst, ss, rs, to):
        return pltpu.make_async_remote_copy(
            src_ref=src, dst_ref=dst, send_sem=ss, recv_sem=rs, device_id=to, device_id_type=MESH
        )

    def cols(m):
        return pl.ds(pl.multiple_of(m * rows, rows), rows)

    def each_micro(f):
        lax.fori_loop(0, micro, lambda m, c: (f(m), c)[1], 0)

    def slot(i):
        return pl.ds(pl.multiple_of(i * span, span), span)

    own_x = local(x_in, rin.at[:, pl.ds(0, half)], lsem.at[4])
    own_c = [local(cot.at[m], gin.at[pl.ds(m * rows, half)], lsem.at[4 + m]) for m in range(micro)]
    loads = [
        local(wqkv_h.at[0], wqkv, lsem.at[0]),
        local(wmix_h.at[0], wmix, lsem.at[1]),
        local(up_h.at[0], wup, lsem.at[2]),
        local(down_h.at[0], wdown, lsem.at[3]),
    ]

    def first_x(m):
        return remote(rin.at[m, pl.ds(0, half)], rin.at[m, pl.ds(half, half)], xs.at[m], xr.at[m], to_x)

    def first_c(m):
        src, dst = gin.at[pl.ds(m * rows, half)], gin.at[pl.ds(m * rows + half, half)]
        return remote(src, dst, xs.at[m], xr.at[m], to_x)

    @pl.when(s == 0)
    def _():
        own_x.start()

    @pl.when(s == 1)
    def _():
        for c in own_c:
            c.start()

    for c in loads:
        c.start()

    barrier = pltpu.get_barrier_semaphore()
    greet(lambda to: pl.semaphore_signal(barrier, inc=1, device_id=to, device_id_type=MESH))
    pl.semaphore_wait(barrier, jnp.where(inner, 6, 5))

    @pl.when(s == 0)
    def _():
        own_x.wait()
        first_x(0).start()

    jj = lax.broadcasted_iota(jnp.int32, (rows, rows), 0)
    ii = lax.broadcasted_iota(jnp.int32, (rows, rows), 1)
    j_own, i_own = jj < half, ii < half
    inside = ((j_own == i_own) & (jj <= ii)).astype(F32)
    own_first = jnp.where(xi == 0, 1.0, 0.0)
    across = jnp.where(j_own & ~i_own, own_first, jnp.where(i_own & ~j_own, 1.0 - own_first, 0.0))
    slots = starts.shape[2]
    for m in range(micro):
        n0 = jnp.int32(0)
        n1 = jnp.int32(0)
        for j in range(slots):
            n0 += jnp.where(starts[m, 0, j] <= 0, 1, 0)
            n1 += jnp.where(starts[m, 0, j] <= STRETCH, 1, 0)
        same = jnp.where(n0 == n1, 1.0, 0.0)
        mask[m] = inside + across * same

    def live_of(m, part):
        block = xi if part == 0 else 1 - xi
        begin = jnp.int32(0)
        for j in range(slots):
            begin = jnp.where(starts[m, 0, j] <= block * STRETCH, jnp.maximum(begin, starts[m, 0, j]), begin)
        length = jnp.int32(0)
        for j in range(slots):
            length += jnp.where(starts[m, 0, j] == begin, lengths[m, 0, j], 0)
        row = block * STRETCH + lax.broadcasted_iota(jnp.int32, (half, width), 0)
        return (row - begin < length).astype(F32)

    def block_of(kind, p, q, m):
        i = p * 2 + q
        return nm_all.at[m, i] if kind == 0 else gd_all.at[pl.ds(pl.multiple_of(i * span + m * rows, rows), rows)]

    class Gather:
        def __init__(self, kind, layer):
            self.kind, self.layer = kind, layer
            self.same = (kind, layer) != (1, 0)
            self.core = layer if self.same else 1

        def held(self, p, m):
            if self.same:
                return block_of(self.kind, p, par, m)
            return hgd.at[p, cols(m)]

        def arrived(self, p, q, m):
            return la.at[self.kind, m, p * 2 + q]

        def arrival(self, p, m):
            return self.arrived(p, par, m) if self.same else ha.at[m, p]

        def sending(self, i, m):
            return fs.at[self.kind if self.same else 2, m, i]

        def to(self, core, p, q):
            return (core, base + p * 2 + q, xi)

        def step(self, i, p, q, m, ref):
            return remote(ref, self.held(p, m), self.sending(i, m), self.arrival(p, m), self.to(self.core, q, par))

        def pair(self, i, p, m, ref):
            to = self.to(self.layer, pos, 1 - par)
            return remote(ref, block_of(self.kind, p, par, m), self.sending(i, m), self.arrived(p, par, m), to)

        def home(self, i, p, m, ref):
            to = self.to(self.layer, pos, par)
            return remote(ref, block_of(self.kind, p, par, m), self.sending(i, m), self.arrived(p, par, m), to)

        def moves(self, way, j, m):
            p = pos - j if way == 0 else pos + j
            i = 3 * p
            if j == 0:
                ref = self.held(p, m) if self.same else igv.at[cols(m)]
                return [
                    (self.step(i, p, pos + 1, m, ref), pos < LINE - 1),
                    (self.step(i + 1, p, pos - 1, m, ref), pos > 0),
                    (self.pair(i + 2, p, m, ref), None),
                ]
            ref = self.held(p, m)
            came = (p >= 0) if way == 0 else (p < LINE)
            q = pos + 1 if way == 0 else pos - 1
            goes = (q < LINE) if way == 0 else (q >= 0)
            out = [(self.step(i, p, q, m, ref), came & goes), (self.pair(i + 1, p, m, ref), came)]
            if not self.same:
                out.append((self.home(i + 2, p, m, ref), came))
            return out

        def each(self, way, j, m, what):
            for copy, when in self.moves(way, j, m):
                if when is None:
                    what(copy)
                else:
                    pl.when(when)(functools.partial(what, copy))

        def own(self, m):
            self.each(0, 0, m, lambda c: c.start())

        def pass_on(self, j, m):
            for way in range(2):
                p = pos - j if way == 0 else pos + j

                @pl.when((p >= 0) if way == 0 else (p < LINE))
                def _():
                    self.step(0, p, pos, m, self.held(p, m)).wait_recv()

                self.each(way, j, m, lambda c: c.start())

        def pass_both(self, j):
            for m in range(micro):
                self.pass_on(j, m)

        def sent(self):
            for m in range(micro):
                self.each(0, 0, m, lambda c: c.wait_send())
                for way in range(2):
                    for j in range(1, LINE):
                        self.each(way, j, m, lambda c: c.wait_send())

        def wide_held(self, p, q, m):
            return block_of(self.kind, p, q, m) if self.same else hgw.at[m - 1, q, p]

        def wide_arrived(self, p, q, m):
            return self.arrived(p, q, m) if self.same else hws.at[m - 1, p * 2 + q]

        def wide(self, j, q, m):
            out = []
            for way in range(2):
                p = pos - j if way == 0 else pos + j
                t = pos + 1 if way == 0 else pos - 1
                when = (t < LINE) if way == 0 else (t >= 0)
                came = (p >= 0) if way == 0 else (p < LINE)
                ref = self.wide_held(p, q, m)
                if j == 0 and q is par and not self.same:
                    ref = igv.at[cols(m)]
                i = 4 * (0 if q is par else 1) + p
                if j == 0 and way == 1:
                    i = 16 + (0 if q is par else 1)
                copy = remote(
                    ref, self.wide_held(p, q, m), self.sending(i, m), self.wide_arrived(p, q, m), self.to(self.core, t, par)
                )
                out.append((copy, when if j == 0 else when & came))
            return out

        def wide_home(self, way, j, q, m):
            p = pos - j if way == 0 else pos + j
            i = 8 + 4 * (0 if q is par else 1) + p
            to = self.to(self.layer, pos, par)
            return remote(self.wide_held(p, q, m), block_of(self.kind, p, q, m), self.sending(i, m), self.arrived(p, q, m), to)

        def wide_pair(self, m):
            ref = block_of(self.kind, pos, par, m) if self.same else igv.at[cols(m)]
            to = self.to(self.core, pos, 1 - par)
            return remote(ref, self.wide_held(pos, par, m), self.sending(18, m), self.wide_arrived(pos, par, m), to)

        def wide_own(self, m):
            for copy, when in self.wide(0, par, m):
                pl.when(when)(copy.start)
            self.wide_pair(m).start()

        def wide_on(self, j, m):
            for q in (par, 1 - par):
                if j == 0 and q is par:
                    continue
                if j == 0:
                    ref = self.wide_held(pos, q, m)
                    remote(ref, ref, fs.at[0, 0, 0], self.wide_arrived(pos, q, m), to_y).wait_recv()
                    if not self.same:
                        self.wide_home(0, 0, q, m).start()
                for way, (copy, when) in enumerate(self.wide(j, q, m)):
                    if j > 0:
                        if self.same:
                            pl.when(when)(copy.wait_recv)
                        else:
                            p = pos - j if way == 0 else pos + j
                            came = (p >= 0) if way == 0 else (p < LINE)
                            pl.when(came)(copy.wait_recv)
                            pl.when(came)(self.wide_home(way, j, q, m).start)
                    pl.when(when)(copy.start)

        def mixed_own(self, m):
            if isinstance(m, int):
                (self.own if m == 0 else self.wide_own)(m)
                return
            pl.when(m == 0)(lambda: self.own(0))
            for n in range(1, micro):
                pl.when(m == n)(functools.partial(self.wide_own, n))

        def mixed_on(self, j):
            self.pass_on(j, 0)
            for m in range(1, micro):
                self.wide_on(j, m)

        def mixed_take(self):
            for k in range(LINE):
                p = lax.rem(pos + k, LINE)
                ref = block_of(self.kind, p, 1 - par, 0)
                remote(ref, ref, fs.at[0, 0, 0], self.arrived(p, 1 - par, 0), to_y).wait_recv()
            for way in range(2):
                for j in range(1, LINE):
                    p = pos - j if way == 0 else pos + j
                    last = (p >= 0) & (pos == LINE - 1) if way == 0 else (p < LINE) & (pos == 0)
                    for m in range(1, micro):
                        for q in (par, 1 - par):
                            ref = block_of(self.kind, p, q, m)
                            come = remote(ref, ref, fs.at[0, 0, 0], self.arrived(p, q, m), to_y)
                            pl.when(last)(come.wait_recv)

        def mixed_sent(self):
            self.each(0, 0, 0, lambda c: c.wait_send())
            for way in range(2):
                for j in range(1, LINE):
                    self.each(way, j, 0, lambda c: c.wait_send())
            for m in range(1, micro):
                self.wide_pair(m).wait_send()
                for j in range(LINE):
                    for q in (par, 1 - par):
                        for way, (copy, when) in enumerate(self.wide(j, q, m)):
                            if j == 0 and q is par:
                                pl.when(when)(copy.wait_send)
                                continue
                            pl.when(when)(copy.wait_send)
                            if self.same or (j == 0 and way == 1):
                                continue
                            p = pos - j if way == 0 else pos + j
                            came = (p >= 0) if way == 0 else (p < LINE)
                            pl.when(came)(self.wide_home(way, j, q, m).wait_send)

        def take(self, i):
            p, q = lax.div(i, 2), lax.rem(i, 2)
            for m in range(micro):
                ref = block_of(self.kind, p, q, m)
                remote(ref, ref, fs.at[0, 0, 0], self.arrived(p, q, m), to_y).wait_recv()

    nm0, nm1, gd0, gd1 = Gather(0, 0), Gather(0, 1), Gather(1, 0), Gather(1, 1)

    def grad_rows(m):
        return pl.ds(pl.multiple_of(g * span + m * rows, rows), rows)

    @pl.when(s == 0)
    def _():
        first_x(0).wait_recv()
        for m in range(1, micro):
            first_x(m).start()

    @pl.when(s == 1)
    def _():
        for c in loads:
            c.wait()
        wupt[...] = wup[...].T
        for c in own_c:
            c.wait()
        for m in range(micro):
            first_c(m).start()
        for m in range(micro):
            first_c(m).wait_recv()
            for part in range(2):
                pr = pl.ds(m * rows + part * half, half)
                to = pl.ds(pl.multiple_of(g * span + m * rows + part * half, half), half)
                gd_all[to] = (gin[pr].astype(F32) * live_of(m, part)).astype(BF)
            gd1.mixed_own(m)
        for m in range(1, micro):
            gd1.wide_on(0, m)
        gd1.mixed_on(1)

    def x_swap(e, m):
        i = (1 + e) * micro + m
        return remote(sbuf.at[e, m], rbuf.at[e, m], xs.at[i], xr.at[i], to_x)

    def give(e, m, part):
        part = part.astype(BF)
        sbuf[e, m, pl.ds(0, half)] = part[half:]
        sbuf[e, m, pl.ds(half, half)] = part[:half]
        x_swap(e, m).start()

    def c_copy(e, m):
        i = e * micro + m
        src, dst = ((act.at[m], rin.at[m]), (igv.at[cols(m)], gin.at[cols(m)]))[e]
        return remote(src, dst, cs.at[i], cr.at[i], to_c)

    def y_copies(when):
        out = []
        if when == 0:
            pairs = [(nrm_t, ynrm), (mtb, ymtb)]
        else:
            pairs = [(sb.at[1 - par], ysb)]
        for i, (src, dst) in enumerate(pairs):
            j = 2 * when + i
            out.append(remote(src, dst, ys.at[j], yr.at[j], to_y))
        return out

    def y_late(i, m):
        src, dst = (
            (gpt.at[1 - par, m], ygpt.at[0, m]),
            (gpt.at[2, m], ygpt.at[1, m]),
            (gbr.at[cols(m), pl.ds(pl.multiple_of((1 - par) * hw, 128), hw)], ygbr.at[cols(m)]),
        )[i]
        j = 3 + i * micro + m
        return remote(src, dst, ys.at[j], yr.at[j], to_y)

    def mixer_forward(m):
        @pl.when((s == 0) & (m > 0))
        def _():
            first_x(m).wait_recv()

        @pl.when(s == 1)
        def _():
            c_copy(0, m).wait_recv()

        @pl.when((s == 0) & (m == 0))
        def _():
            loads[0].wait()
            loads[1].wait()

        r = rin[m].astype(F32)
        n = (normed(r)[0] * gain1[...]).astype(BF)
        pts = []
        for q in range(3):
            p = dot(n, wqkv[q]).astype(BF)
            if q == 2:
                vnat[m] = p
            p = p.T
            pt[q, :, cols(m)] = p
            pts.append([p[h * hs : (h + 1) * hs] for h in range(heads)])
        nrm_t[:, cols(m)] = n.T
        ws = [fmap[0, h] for h in range(heads)]
        logits = [[dot(ws[h], pts[q][h], 0, 0) for h in range(heads)] for q in range(2)]
        feats = [[both_softmax(x) for x in logits[q]] for q in range(2)]
        scores = [dot(feats[1][h], feats[0][h], 0, 0) for h in range(heads)]
        keep = mask[m]
        scores = [x * keep for x in scores]
        dens = [1.0 / jnp.sum(x, axis=0, keepdims=True) for x in scores]
        scores = [x.astype(BF) for x in scores]
        mixed = [dot(pts[2][h], scores[h]) * dens[h] for h in range(heads)]
        for h in range(heads):
            hr = pl.ds(h * hs, hs)
            qf[m, h] = feats[0][h]
            kf[m, h] = feats[1][h]
            st[m, h] = scores[h]
            den_s[m, h] = jnp.broadcast_to(dens[h], (8, rows))
            mt[m, hr] = mixed[h]
            mtb[hr, cols(m)] = mixed[h].astype(BF)
        part = dot(mtb[:, cols(m)].T, wmix[...])
        give(0, m, part)
        rmid[m] = r + part

    def ffn_forward(m):
        x_swap(0, m).wait_recv()
        r = rmid[m] + rbuf[0, m].astype(F32)
        rmid[m] = r
        n = (normed(r)[0] * gain2[...]).astype(BF)
        nm_all[m, g] = n.T

        @pl.when(s == 0)
        def _():
            nm0.mixed_own(m)

        @pl.when(s == 1)
        def _():
            nm1.own(m)

        @pl.when((s == 0) & (m == 0))
        def _():
            loads[2].wait()
            loads[3].wait()

        h, slope = gelu_both(dot(n, wup[...]))
        h = h.astype(BF)
        gp[m] = slope.astype(BF)
        part = dot(h, wdown[...])
        give(1, m, part)
        part_f[m] = r + part

    def act_copy(m):
        return local(act.at[m, pl.ds(0, half)], act_o.at[0, m], osem.at[m])

    def ig_copy(m):
        return local(igv.at[pl.ds(pl.multiple_of(m * rows, half), half)], ig_o.at[0, m], osem.at[micro + m])

    def end_forward(m):
        x_swap(1, m).wait_recv()
        act[m] = (part_f[m] + rbuf[1, m].astype(F32)).astype(BF)

        @pl.when(s == 0)
        def _():
            c_copy(0, m).start()

        act_copy(m).start()

    each_micro(mixer_forward)
    @pl.when(s == 0)
    def _():
        for c in y_copies(0):
            c.start()

    @pl.when(s == 1)
    def _():
        gd1.mixed_on(2)

    each_micro(ffn_forward)
    each_micro(end_forward)

    @pl.when(s == 1)
    def _():
        gd1.mixed_on(3)


    tile = hb.shape[0]
    tiles = ff // tile

    def hid_rows(t):
        return pl.ds(pl.multiple_of(t * tile, tile), tile)

    @pl.when(s == 0)
    def _():
        wupt[...] = wup[...].T

        for m in range(1, micro):
            nm0.wide_on(0, m)
        for j in range(1, LINE):
            nm0.mixed_on(j)

    def ffn_back(m):
        @pl.when(s == 0)
        def _():
            c_copy(1, m).wait_recv()
            gd_all[grad_rows(m)] = gin[cols(m)]

        gd = gd_all[grad_rows(m)]
        gpre = (dot(gd, wdown[...], 1, 1) * gp[m].astype(F32)).astype(BF)
        part = dot(gpre, wup[...], 1, 1)
        give(2, m, part)
        part_f[m] = part

    def mixer_back(m):
        @pl.when((s == 1) & (m == 1))
        def _():
            nm1.pass_both(1)

        x_swap(2, m).wait_recv()
        gn = part_f[m] + rbuf[2, m].astype(F32)
        xhat, rstd = normed(rmid[m])
        gacc[1, m] = jnp.broadcast_to(jnp.sum(gn * xhat, axis=0, keepdims=True), (8, width))
        gm = gd_all[grad_rows(m)].astype(F32) + norm_back(gn, gain2[...], xhat, rstd)
        rmid[m] = gm
        gb_ = gm.astype(BF)
        gbr[cols(m)] = gb_

        @pl.when(s == 0)
        def _():
            y_late(2, m).start()

        gmt = dot(wmix[...], gb_, 1, 1).astype(BF)
        dens = [den_s[m, h, pl.ds(0, 1)] for h in range(heads)]
        gos = [gmt[h * hs : (h + 1) * hs].astype(F32) for h in range(heads)]
        gdens = [-jnp.sum(gos[h] * mt[m, pl.ds(h * hs, hs)], axis=0, keepdims=True) * dens[h] for h in range(heads)]
        gnums = [(gos[h] * dens[h]).astype(BF) for h in range(heads)]
        pad = jnp.zeros_like(gnums[0])
        wide = [jnp.concatenate([x, pad] if h % 2 == 0 else [pad, x], axis=0) for h, x in enumerate(gnums)]
        gsts = [dot(vnat[m, :, pl.ds((h // 2) * 2 * hs, 2 * hs)], wide[h]) + gdens[h] for h in range(heads)]
        keep = mask[m]
        gsts = [(x * keep).astype(BF) for x in gsts]
        qfs = [qf[m, h] for h in range(heads)]
        kfs = [kf[m, h] for h in range(heads)]
        gqf = [dot(kfs[h], gsts[h]) for h in range(heads)]
        gkf = [dot(qfs[h], gsts[h], 1, 1) for h in range(heads)]
        gvs = [dot(gnums[h], st[m, h], 1, 1).astype(BF) for h in range(heads)]
        gql = [softmax_back(gqf[h], qfs[h]).astype(BF) for h in range(heads)]
        gkl = [softmax_back(gkf[h], kfs[h]).astype(BF) for h in range(heads)]
        gpq = [dot(fmap[0, h], gql[h]).astype(BF) for h in range(heads)]
        gpk = [dot(fmap[0, h], gkl[h]).astype(BF) for h in range(heads)]
        for h in range(heads):
            hr = pl.ds(h * hs, hs)
            gqk[0, hr, cols(m)] = gql[h]
            gqk[1, hr, cols(m)] = gkl[h]
            gpt[0, m, hr] = gpq[h]
            gpt[1, m, hr] = gpk[h]
            gpt[2, m, hr] = gvs[h]

        @pl.when(s == 0)
        def _():
            y_late(0, m).start()
            y_late(1, m).start()

        gnt = dot(wqkv[0], gpt[0, m]) + dot(wqkv[1], gpt[1, m]) + dot(wqkv[2], gpt[2, m])
        part = gnt.T
        give(3, m, part)
        part_f[m] = part

    def end_back(m):
        x_swap(3, m).wait_recv()
        gn = part_f[m] + rbuf[3, m].astype(F32)
        xhat, rstd = normed(rin[m].astype(F32))
        gacc[0, m] = jnp.broadcast_to(jnp.sum(gn * xhat, axis=0, keepdims=True), (8, width))
        igv[cols(m)] = (rmid[m] + norm_back(gn, gain1[...], xhat, rstd)).astype(BF)

        @pl.when(s == 1)
        def _():
            c_copy(1, m).start()
            gd0.mixed_own(m)

        ig_copy(m).start()

    each_micro(ffn_back)

    each_micro(mixer_back)

    late = y_copies(1)

    cut = width // hw
    q_rows = pl.ds(0, width)
    v_rows = pl.ds(width, width // 2)
    m_rows = pl.ds(width + width // 2, hw)
    s_rows = pl.ds(width + width // 2 + hw, hs)
    v_part = pl.ds(pl.multiple_of(par * (width // 2), 16), width // 2)
    m_part = pl.ds(pl.multiple_of(par * hw, 128), hw)

    left = lax.broadcasted_iota(jnp.int32, (hs, 2 * hs), 1) < hs
    for p in range(heads // 2):
        pr = pl.ds(p * 2 * hs, 2 * hs)
        tot = dot(pt[0, pr], gqk[0, pr], 1, 1) + dot(pt[1, pr], gqk[1, pr], 1, 1)
        sb[0, :, pr] = jnp.where(left, tot[:hs], tot[hs:]).astype(BF)

    each_micro(end_back)

    row = lax.broadcasted_iota(jnp.int32, (hs, hw), 0)
    block = jnp.zeros((hs, hw), F32)
    for e in range(2):
        tot = gacc[e, 0, pl.ds(0, 1)]
        for m in range(1, micro):
            tot += gacc[e, m, pl.ds(0, 1)]
        for c in range(cut):
            block = jnp.where(row == e * cut + c, tot[:, c * hw : (c + 1) * hw], block)
    sb[1] = block.astype(BF)

    part_rows = hp.shape[0] // 2
    chunk = part_rows // 4

    class Line:
        def __init__(self, n):
            self.n = n

        def piece(self, near, j):
            group = side if near else 1 - side
            return pl.ds(pl.multiple_of((group * self.n + j) * chunk, 16), chunk)

        def final(self, near, j):
            if self.n == 4:
                return fin.at[self.piece(near, j)]
            group = side if near else 1 - side
            return fin.at[pl.ds(pl.multiple_of(par * part_rows + (group * self.n + j) * chunk, 16), chunk)]

        def send_in(self, near, j):
            i = 4 * near + j
            return remote(hp.at[self.piece(near, j)], from_out.at[i], ars.at[i], arr.at[i], to_mate)

        def send_over(self, j):
            return remote(hp.at[self.piece(0, j)], from_opp.at[j], ars.at[j], arr.at[8 + j], to_opp)

        def total_over(self, j):
            ref = self.final(1, j)
            return remote(ref, ref, ars.at[4 + j], arr.at[12 + j], to_opp)

        def total_out(self, near, j):
            i = 4 * near + j
            ref = self.final(near, j)
            return remote(ref, ref, ars.at[8 + i], arr.at[i], to_mate)

        def total_pair(self, near, j):
            i = 16 + 2 * near + j if self.n == 2 else 8 + 4 * near + j
            ref = self.final(near, j)
            return remote(ref, ref, ars.at[i], arr.at[i], to_y)

        def trade(self, j):
            return remote(hp.at[self.piece(1, j)], from_pair.at[j], ars.at[16 + j], arr.at[16 + j], to_y)

        def start(self, lo, hi):
            @pl.when(outer)
            def _():
                for j in range(lo, hi):
                    for near in range(2):
                        self.send_in(near, j).start()

        def collect(self, j):
            @pl.when(inner)
            def _():
                self.send_in(0, j).wait_recv()
                p = self.piece(0, j)
                hp[p] = (hp[p].astype(F32) + from_out[j].astype(F32)).astype(BF)
                self.send_over(j).start()

        def total(self, j):
            @pl.when(inner)
            def _():
                self.send_in(1, j).wait_recv()
                self.send_over(j).wait_recv()
                p = self.piece(1, j)
                tot = hp[p].astype(F32) + from_out[4 + j].astype(F32) + from_opp[j].astype(F32)
                if self.n == 4:
                    hp[p] = tot.astype(BF)
                    self.trade(j).start()
                else:
                    self.final(1, j)[...] = tot.astype(BF)
                    self.total_out(1, j).start()
                    self.total_over(j).start()

            if self.n == 2:
                @pl.when(outer)
                def _():
                    self.total_out(1, j).wait_recv()

                self.total_pair(1, j).start()

        def settle(self, j):
            @pl.when(inner)
            def _():
                self.trade(j).wait_recv()
                tot = hp[self.piece(1, j)].astype(F32) + from_pair[j].astype(F32)
                self.final(1, j)[...] = tot.astype(BF)
                self.total_out(1, j).start()
                self.total_over(j).start()

            self.across(1, j)

        def across(self, near, j):
            @pl.when(outer)
            def _():
                self.total_out(near, j).wait_recv()

        def passed(self, j):
            @pl.when(inner)
            def _():
                self.total_over(j).wait_recv()
                self.total_out(0, j).start()

            if self.n == 2:
                @pl.when(outer)
                def _():
                    self.total_out(0, j).wait_recv()

                self.total_pair(0, j).start()
            else:
                self.across(0, j)

        def last(self):
            if self.n == 2:
                for near in range(2):
                    for j in range(2):
                        self.total_pair(near, j).wait_recv()
                return

        def finish(self):
            for j in range(self.n):
                @pl.when(outer)
                def _():
                    self.send_in(0, j).wait_send()
                    self.send_in(1, j).wait_send()

                @pl.when(inner)
                def _():
                    self.send_over(j).wait_send()
                    self.total_over(j).wait_send()
                    if self.n == 4:
                        self.trade(j).wait_send()

                mine = par == j % 2
                for near in range(2):
                    pl.when(inner)(self.total_out(near, j).wait_send)
                    if self.n == 2:
                        self.total_pair(near, j).wait_send()

    first, second = Line(2), Line(4)

    @pl.when(s == 0)
    def _():
        late[0].start()
        for c in y_copies(0) + late:
            c.wait_recv()
        for m in range(micro):
            for i in range(3):
                y_late(i, m).wait_recv()
        q_tot = 0.0
        v_tot = 0.0
        for m in range(micro):
            q_tot += dot(nrm_t[:, cols(m)], gpt[par, m], 1, 1) + dot(ynrm[:, cols(m)], ygpt[0, m], 1, 1)
            v_tot += dot(nrm_t[v_part, cols(m)], gpt[2, m], 1, 1) + dot(ynrm[v_part, cols(m)], ygpt[1, m], 1, 1)
        hp[q_rows] = q_tot.astype(BF)
        hp[v_rows] = v_tot.astype(BF)
        hp[m_rows] = (dot(mtb[...], gbr[:, m_part]) + dot(ymtb[...], ygbr[...])).astype(BF)
        hp[s_rows] = (sb[par].astype(F32) + ysb[...].astype(F32)).astype(BF)
        first.start(0, 2)

    @pl.when(s == 1)
    def _():
        for q in range(3):
            tot = dot(nrm_t[:, cols(0)], gpt[q, 0], 1, 1)
            for m in range(1, micro):
                tot += dot(nrm_t[:, cols(m)], gpt[q, m], 1, 1)
            hp[pl.ds(q * width, width)] = tot.astype(BF)
        tot = dot(mtb[...], gbr[...]).astype(BF)
        for c in range(cut):
            hp[pl.ds(3 * width + c * hw, hw)] = tot[:, c * hw : (c + 1) * hw]
        for e in range(2):
            hp[pl.ds(3 * width + cut * hw + e * hs, hs)] = sb[e]
        for m in range(1, micro):
            gd0.wide_on(0, m)
        second.start(0, 2)
        gd0.mixed_on(1)
        nm1.pass_both(2)
        gd0.mixed_on(2)
        nm1.pass_both(3)
        gd1.mixed_take()

    @pl.when(s == 0)
    def _():
        nm0.mixed_take()
        for k in range(1, GROUP):
            gd0.take(lax.rem(g + k, GROUP))
        first.collect(0)

    @pl.when(s == 1)
    def _():
        second.collect(0)
        gd0.mixed_on(3)
        for k in range(1, GROUP, 2):
            nm1.take(lax.rem(g + k, GROUP))

    def up_copy(t):
        return local(wup.at[:, hid_rows(t)], up_o.at[:, hid_rows(t)], tsem.at[0, t])

    def down_copy(t):
        return local(wdown.at[hid_rows(t)], down_o.at[hid_rows(t)], tsem.at[1, t])

    for i in range(GROUP):
        for m in range(micro):
            nm_cat[:, pl.ds(i * span + m * rows, rows)] = nm_all[m, i]

    def tile_grads(t):
        hr = hid_rows(t)
        wu = wupt[hr]
        wd = wdown[hr]
        for i in range(GROUP):
            sl = slot(i)
            h, slope = gelu_both(dot(wu, nm_cat[:, sl]))
            hb[:, sl] = h.astype(BF)
            gb[:, sl] = (dot(wd, gd_all[sl], 1, 1) * slope).astype(BF)
        wup[:, hr] = dot(nm_cat[...], gb[...], 1, 1).astype(BF)
        wdown[hr] = dot(hb[...], gd_all[...]).astype(BF)
        up_copy(t).start()
        down_copy(t).start()

    plan = {
        (0, True): {
            0: [("total", 0)],
            1: [("collect", 1)],
            2: [("passed", 0), ("total", 1)],
            3: [("passed", 1)],
        },
        (0, False): {2: [("total", 0)], 3: [("passed", 0), ("total", 1)], 4: [("passed", 1)]},
        (1, True): {
            0: [("total", 0), ("collect", 1)],
            1: [("total", 1)],
            2: [("settle", 0)],
            3: [("settle", 1), ("collect", 2)],
            4: [("passed", 0), ("total", 2), ("collect", 3)],
            5: [
                ("passed", 1),
                ("settle", 2),
                ("total", 3),
                ("passed", 2),
                ("settle", 3),
                ("passed", 3),
            ],
        },
        (1, False): {
            0: [("start", 2, 4)],
            5: [(f, j) for j in range(4) for f in ("settle", "passed")],
        },
    }

    def one_tile(t, carry):
        tile_grads(t)
        for (layer, within), when in plan.items():
            for at, steps in when.items():
                @pl.when((s == layer) & (inner if within else outer) & (t == at))
                def _():
                    for name, *j in steps:
                        getattr((first, second)[layer], name)(*j)

        return carry

    lax.fori_loop(0, tiles, one_tile, 0)

    @pl.when(s == 0)
    def _():
        first.last()

    @pl.when(s == 1)
    def _():
        second.last()

    def outs_of(layer, out_copy):
        if layer == 1:
            out_copy(fin.at[pl.ds(0, 3 * width)], qkv_o)
            for c in range(cut):
                out_copy(fin.at[pl.ds(3 * width + c * hw, hw)], mix_o.at[:, pl.ds(c * hw, hw)])
            for e in range(2):
                out_copy(fin.at[pl.ds(3 * width + cut * hw + e * hs, hs)], small_o.at[e])
            return
        for e in range(2):
            at = e * part_rows
            out_copy(fin.at[pl.ds(at, width)], qkv_o.at[pl.ds(e * width, width)])
            at += width
            out_copy(fin.at[pl.ds(at, width // 2)], qkv_o.at[pl.ds(2 * width + e * (width // 2), width // 2)])
            at += width // 2
            out_copy(fin.at[pl.ds(at, hw)], mix_o.at[:, pl.ds(e * hw, hw)])
            at += hw
            out_copy(fin.at[pl.ds(at, hs)], small_o.at[e])

    def ended(layer):
        mine = []

        def keep(src, dst):
            c = local(src, dst, osem.at[2 * micro + 2 + len(mine)])
            c.start()
            mine.append(c)

        outs_of(layer, keep)
        for c in mine:
            c.wait()

    for t in range(tiles):
        up_copy(t).wait()
        down_copy(t).wait()

    @pl.when(s == 0)
    def _():
        ended(0)

    @pl.when(s == 1)
    def _():
        ended(1)

    @pl.when(s == 0)
    def _():
        for m in range(micro):
            first_x(m).wait_send()
            c_copy(0, m).wait_send()

    @pl.when(s == 1)
    def _():
        for m in range(micro):
            first_c(m).wait_send()
            c_copy(1, m).wait_send()

    for e in range(4):
        for m in range(micro):
            x_swap(e, m).wait_send()
    @pl.when(s == 0)
    def _():
        nm0.mixed_sent()

    @pl.when(s == 1)
    def _():
        gd1.mixed_sent()
        gd0.mixed_sent()
        nm1.sent()

    @pl.when(s == 0)
    def _():
        for c in y_copies(0) + y_copies(1):
            c.wait_send()
        for m in range(micro):
            for i in range(3):
                y_late(i, m).wait_send()
        first.finish()

    @pl.when(s == 1)
    def _():
        second.finish()

    for m in range(micro):
        act_copy(m).wait()
        ig_copy(m).wait()


def widen(act, ig, qkv, mix, small, up, down, act_o, ig_o, qkv_o, mix_o, feat_o, g1_o, g2_o, up_o, down_o, sem_in, sem_out, *bufs):
    hs = feat_o.shape[2]
    hw = mix.shape[0]
    cut = mix.shape[1] // hw
    blocks = []
    for src, dst, step in ((up, up_o, 192), (down, down_o, 384), (qkv, qkv_o, 768), (mix, mix_o, 192)):
        for lo in range(0, src.shape[0], step):
            if dst is qkv_o:
                blocks.append((src.at[pl.ds(lo, step)], dst.at[0, lo // step]))
            else:
                blocks.append((src.at[pl.ds(lo, step)], dst.at[0, pl.ds(lo, step)]))
    half = len(blocks)
    narrow, wide = bufs[:half], bufs[half : 2 * half]
    small_v, feat_v, g1_v, g2_v, act_v, ig_v = bufs[2 * half :]
    first = [
        pltpu.make_async_copy(src, dst, sem_in.at[half + i])
        for i, (src, dst) in enumerate(((small, small_v), (act, act_v), (ig, ig_v)))
    ]
    for c in first:
        c.start()
    loads = [pltpu.make_async_copy(b[0], n, sem_in.at[i]) for i, (b, n) in enumerate(zip(blocks, narrow))]
    for c in loads:
        c.start()
    outs = []

    def put(src, dst, i):
        c = pltpu.make_async_copy(src, dst, sem_out.at[i])
        c.start()
        outs.append(c)

    for c in first:
        c.wait()
    put(act_v, act_o, half + 3)
    put(ig_v, ig_o, half + 4)
    for h in range(feat_v.shape[1]):
        feat_v[0, h] = small_v[0, pl.ds(0, hs), pl.ds(h * hs, hs)].astype(F32)
    for c in range(cut):
        cs = pl.ds(c * hw, hw)
        g1_v[:, cs] = small_v[1, pl.ds(0, 16)].astype(F32)[c : c + 1]
        g2_v[:, cs] = small_v[1, pl.ds(0, 16)].astype(F32)[cut + c : cut + c + 1]
    put(feat_v, feat_o, half)
    put(g1_v, g1_o, half + 1)
    put(g2_v, g2_o, half + 2)
    for i, (b, n, w) in enumerate(zip(blocks, narrow, wide)):
        loads[i].wait()
        w[...] = n[...].astype(F32)
        put(w, b[1], i)
    for c in outs:
        c.wait()


def on_device(x, cot, starts, lengths, gain1, wqkv, fmap, wmix, gain2, wup, wdown):
    micro, half, width = x.shape
    rows = 2 * half
    span = micro * rows
    heads, hs = fmap.shape[1], fmap.shape[2]
    hw = heads * hs
    ff = wup.shape[2]
    cut = width // hw
    part_rows = width + width // 2 + hw + hs
    f, b = F32, BF
    vm = pltpu.VMEM
    dma = pltpu.SemaphoreType.DMA
    out = lambda shape, t=b: jax.ShapeDtypeStruct(shape, t)
    act, ig, qkv, mix, small, up, down = pl.pallas_call(
        kernel,
        out_shape=[
            out((1, micro, half, width)),
            out((1, micro, half, width)),
            out((3 * width, hw)),
            out((hw, width)),
            out((2, hs, hw)),
            out((width, ff)),
            out((ff, width)),
        ],
        in_specs=[ANY, ANY, SM, SM, VM, ANY, VM, ANY, VM, ANY, ANY],
        out_specs=[ANY] * 7,
        scratch_shapes=[
            vm((3, width, hw), b),
            vm((hw, width), b),
            vm((width, ff), b),
            vm((ff, width), b),
            vm((ff, width), b),
            vm((micro, rows, width), b),
            vm((span, width), b),
            vm((micro, rows, rows), f),
            vm((width, span), b),
            vm((3, hw, span), b),
            vm((micro, rows, hw), b),
            vm((micro, heads, 2 * hs, rows), b),
            vm((micro, heads, 2 * hs, rows), b),
            vm((micro, heads, rows, rows), b),
            vm((micro, hw, rows), f),
            vm((hw, span), b),
            vm((micro, heads, 8, rows), f),
            vm((micro, rows, width), f),
            vm((micro, GROUP, width, rows), b),
            vm((width, GROUP * span), b),
            vm((GROUP * span, width), b),
            vm((256, GROUP * span), b),
            vm((256, GROUP * span), b),
            vm((micro, rows, ff), b),
            vm((micro, rows, width), f),
            vm((micro, rows, width), b),
            vm((span, width), b),
            vm((span, width), b),
            vm((2, hw, span), b),
            vm((3, micro, hw, rows), b),
            vm((2, micro, 8, width), f),
            vm((4, micro, rows, width), b),
            vm((4, micro, rows, width), b),
            vm((width, span), b),
            vm((hw, span), b),
            vm((2, micro, hw, rows), b),
            vm((span, hw), b),
            vm((2, hs, hw), b),
            vm((hs, hw), b),
            vm((2 * part_rows, hw), b),
            vm((2 * part_rows, hw), b),
            vm((8, part_rows // 4, hw), b),
            vm((4, part_rows // 4, hw), b),
            vm((4, part_rows // 4, hw), b),
            vm((LINE, span, width), b),
            vm((micro - 1, 2, LINE, rows, width), b),
            dma((4 + micro,)),
            dma((5 * micro,)),
            dma((5 * micro,)),
            dma((2 * micro,)),
            dma((2 * micro,)),
            dma((2, micro, GROUP)),
            dma((micro, LINE)),
            dma((3, micro, 20)),
            dma((micro - 1, GROUP)),
            dma((3 + 3 * micro,)),
            dma((3 + 3 * micro,)),
            dma((20,)),
            dma((20,)),
            dma((2 * micro + 10,)),
            dma((2, ff // 256)),
        ],
        compiler_params=pltpu.CompilerParams(
            collective_id=0, has_side_effects=True, vmem_limit_bytes=60 * 1024 * 1024
        ),
    )(x, cot, starts, lengths, gain1, wqkv, fmap, wmix, gain2, wup, wdown)

    n = lax.axis_size("dp")
    if n > GROUP:
        same_place = [[i + j * GROUP for j in range(n // GROUP)] for i in range(GROUP)]
        qkv, mix, small, up, down = lax.psum((qkv, mix, small, up, down), "dp", axis_index_groups=same_place)

    shapes = []
    for a, step in ((up, 192), (down, 384), (qkv, 768), (mix, 192)):
        shapes += [(step, a.shape[1])] * (a.shape[0] // step)
    outs = [(1, 3, width, hw), (1, hw, width), (1, heads, hs, hs), (1, width), (1, width), (1, width, ff), (1, ff, width)]
    act, ig, qkv, mix, features, g1, g2, up, down = pl.pallas_call(
        widen,
        out_shape=[out(act.shape), out(ig.shape)] + [out(o, f) for o in outs],
        in_specs=[ANY] * 7,
        out_specs=[ANY] * 9,
        scratch_shapes=[dma((len(shapes) + 3,)), dma((len(shapes) + 5,))]
        + [vm(o, b) for o in shapes]
        + [vm(o, f) for o in shapes]
        + [vm(small.shape, b), vm(outs[2], f), vm(outs[3], f), vm(outs[4], f), vm(act.shape, b), vm(ig.shape, b)],
        compiler_params=pltpu.CompilerParams(vmem_limit_bytes=60 * 1024 * 1024),
    )(act, ig, qkv, mix, small, up, down)
    return act, ig, g1, qkv, features, mix, g2, up, down


def solution(mesh):
    in_specs = (
        P(None, ("dp", "mp"), None),
        P(None, ("dp", "mp"), None),
        P(None, "dp", None),
        P(None, "dp", None),
        P("section", None),
        P("section", None, None, "mp"),
        P("section", "mp", None, None),
        P("section", "mp", None),
        P("section", None),
        P("section", None, "mp"),
        P("section", "mp", None),
    )
    out_specs = (
        P("section", None, ("dp", "mp"), None),
        P("section", None, ("dp", "mp"), None),
        P("section", None),
        P("section", None, None, "mp"),
        P("section", "mp", None, None),
        P("section", "mp", None),
        P("section", None),
        P("section", None, "mp"),
        P("section", "mp", None),
    )
    return jax.shard_map(
        on_device, mesh=mesh, in_specs=in_specs, out_specs=out_specs, check_vma=False
    )
```

```python
import functools

import functools

import jax
import jax.numpy as jnp
from jax import lax
from jax.experimental import pallas as pl
from jax.experimental.pallas import tpu as pltpu
from jax.sharding import PartitionSpec as P

STRETCH = 64
GROUP = 8
LINE = 4
MESH = pl.DeviceIdType.MESH
BF = jnp.bfloat16
F32 = jnp.float32
ANY = pl.BlockSpec(memory_space=pl.ANY)
VM = pl.BlockSpec(memory_space=pltpu.VMEM)
SM = pl.BlockSpec(memory_space=pltpu.SMEM)


def dot(a, b, ca=1, cb=0):
    return lax.dot_general(a, b, (((ca,), (cb,)), ((), ())), preferred_element_type=F32)


def normed(v):
    mean = jnp.mean(v, axis=1, keepdims=True)
    c = v - mean
    rstd = lax.rsqrt(jnp.mean(c * c, axis=1, keepdims=True) + 1e-05)
    return c * rstd, rstd


def norm_back(grad, gain, xhat, rstd):
    t = grad * gain
    mean_t = jnp.mean(t, axis=1, keepdims=True)
    mean_tx = jnp.mean(t * xhat, axis=1, keepdims=True)
    return rstd * (t - mean_t - xhat * mean_tx)


def gelu_both(x):
    k = 0.7978845608028654
    x2 = x * x
    g = 0.5 + 0.5 * jnp.tanh(x * (k + (k * 0.044715) * x2))
    h = x * g
    return h, g + h * (1.0 - g) * (2.0 * k + (6.0 * k * 0.044715) * x2)


def both_softmax(logit):
    up = jnp.exp(logit - jnp.max(logit, axis=0, keepdims=True))
    down = jnp.exp(jnp.min(logit, axis=0, keepdims=True) - logit)
    up = up * (1.0 / jnp.sum(up, axis=0, keepdims=True))
    down = down * (1.0 / jnp.sum(down, axis=0, keepdims=True))
    return jnp.concatenate([up.astype(BF), down.astype(BF)], axis=0)


def softmax_back(grad, feat):
    n = grad.shape[0] // 2
    g = grad * feat.astype(F32)
    p = feat.astype(F32)
    one = g[:n] - p[:n] * jnp.sum(g[:n], axis=0, keepdims=True)
    two = g[n:] - p[n:] * jnp.sum(g[n:], axis=0, keepdims=True)
    return one - two


def kernel(
    x_in, cot, starts, lengths, gain1, wqkv_h, fmap, wmix_h, gain2, up_h, down_h,
    act_o, ig_o, qkv_o, mix_o, small_o, up_o, down_o,
    wqkv, wmix, wup, wdown, wupt, rin, gin, mask,
    nrm_t, pt, vnat, qf, kf, st, mt, mtb, den_s, rmid, nm_all, nm_cat, gd_all, hb, gb, gp, part_f, rout, act, igv,
    gbr, gqk, gpt, gacc, sbuf, rbuf,
    ynrm, ymtb, ygpt, ygbr, sb, ysb, hp, fin, from_out, from_opp, from_pair, hgd, hgw,
    lsem, xs, xr, cs, cr, la, ha, fs, hws, ys, yr, ars, arr, osem, tsem,
):
    s = lax.axis_index("section")
    d = lax.axis_index("dp")
    xi = lax.axis_index("mp")
    micro, half, width = x_in.shape
    rows = 2 * half
    span = micro * rows
    heads, hs = fmap.shape[1], fmap.shape[2]
    hw = heads * hs
    ff = up_h.shape[2]
    g = lax.rem(d, GROUP)
    base = d - g
    pos = lax.div(g, 2)
    par = lax.rem(g, 2)
    to_x = (s, d, 1 - xi)
    to_c = (1 - s, d, xi)
    to_y = (s, base + pos * 2 + 1 - par, xi)
    outer = (pos == 0) | (pos == LINE - 1)
    inner = (pos > 0) & (pos < LINE - 1)
    side = lax.div(pos, 2)
    to_mate = (s, base + (side * 4 + 1 - pos) * 2 + par, xi)
    to_opp = (s, base + (LINE - 1 - pos) * 2 + par, xi)

    def other_core(to):
        return (1 - s,) + to[1:]

    def other_core(to):
        return (1 - s,) + to[1:]

    def at(core, p, q):
        return (core, base + p * 2 + q, xi)

    def greet(act):
        for to in (to_x, to_c, to_y, other_core(to_y)):
            act(to)
        pl.when(pos < LINE - 1)(lambda: act(at(s, pos + 1, par)))
        pl.when(pos > 0)(lambda: act(at(s, pos - 1, par)))

    def local(src, dst, sem):
        return pltpu.make_async_copy(src, dst, sem)

    def remote(src, dst, ss, rs, to):
        return pltpu.make_async_remote_copy(
            src_ref=src, dst_ref=dst, send_sem=ss, recv_sem=rs, device_id=to, device_id_type=MESH
        )

    def cols(m):
        return pl.ds(pl.multiple_of(m * rows, rows), rows)

    def each_micro(f):
        lax.fori_loop(0, micro, lambda m, c: (f(m), c)[1], 0)

    def slot(i):
        return pl.ds(pl.multiple_of(i * span, span), span)

    own_x = local(x_in, rin.at[:, pl.ds(0, half)], lsem.at[4])
    own_c = [local(cot.at[m], gin.at[pl.ds(m * rows, half)], lsem.at[4 + m]) for m in range(micro)]
    loads = [
        local(wqkv_h.at[0], wqkv, lsem.at[0]),
        local(wmix_h.at[0], wmix, lsem.at[1]),
        local(up_h.at[0], wup, lsem.at[2]),
        local(down_h.at[0], wdown, lsem.at[3]),
    ]

    def first_x(m):
        return remote(rin.at[m, pl.ds(0, half)], rin.at[m, pl.ds(half, half)], xs.at[m], xr.at[m], to_x)

    def first_c(m):
        src, dst = gin.at[pl.ds(m * rows, half)], gin.at[pl.ds(m * rows + half, half)]
        return remote(src, dst, xs.at[m], xr.at[m], to_x)

    @pl.when(s == 0)
    def _():
        own_x.start()

    @pl.when(s == 1)
    def _():
        for c in own_c:
            c.start()

    for c in loads:
        c.start()

    barrier = pltpu.get_barrier_semaphore()
    greet(lambda to: pl.semaphore_signal(barrier, inc=1, device_id=to, device_id_type=MESH))
    pl.semaphore_wait(barrier, jnp.where(inner, 6, 5))

    @pl.when(s == 0)
    def _():
        own_x.wait()
        first_x(0).start()

    jj = lax.broadcasted_iota(jnp.int32, (rows, rows), 0)
    ii = lax.broadcasted_iota(jnp.int32, (rows, rows), 1)
    j_own, i_own = jj < half, ii < half
    inside = ((j_own == i_own) & (jj <= ii)).astype(F32)
    own_first = jnp.where(xi == 0, 1.0, 0.0)
    across = jnp.where(j_own & ~i_own, own_first, jnp.where(i_own & ~j_own, 1.0 - own_first, 0.0))
    slots = starts.shape[2]
    for m in range(micro):
        n0 = jnp.int32(0)
        n1 = jnp.int32(0)
        for j in range(slots):
            n0 += jnp.where(starts[m, 0, j] <= 0, 1, 0)
            n1 += jnp.where(starts[m, 0, j] <= STRETCH, 1, 0)
        same = jnp.where(n0 == n1, 1.0, 0.0)
        mask[m] = inside + across * same

    def live_of(m, part):
        block = xi if part == 0 else 1 - xi
        begin = jnp.int32(0)
        for j in range(slots):
            begin = jnp.where(starts[m, 0, j] <= block * STRETCH, jnp.maximum(begin, starts[m, 0, j]), begin)
        length = jnp.int32(0)
        for j in range(slots):
            length += jnp.where(starts[m, 0, j] == begin, lengths[m, 0, j], 0)
        row = block * STRETCH + lax.broadcasted_iota(jnp.int32, (half, width), 0)
        return (row - begin < length).astype(F32)

    def block_of(kind, p, q, m):
        i = p * 2 + q
        return nm_all.at[m, i] if kind == 0 else gd_all.at[pl.ds(pl.multiple_of(i * span + m * rows, rows), rows)]

    class Gather:
        def __init__(self, kind, layer, plain):
            self.kind, self.layer = kind, layer
            self.plain = plain
            self.same = (kind, layer) != (1, 0)
            self.core = layer if self.same else 1

        def held(self, p, m):
            if self.same:
                return block_of(self.kind, p, par, m)
            return hgd.at[p, cols(m)]

        def arrived(self, p, q, m):
            return la.at[self.kind, m, p * 2 + q]

        def arrival(self, p, m):
            return self.arrived(p, par, m) if self.same else ha.at[m, p]

        def sending(self, i, m):
            return fs.at[self.kind if self.same else 2, m, i]

        def to(self, core, p, q):
            return (core, base + p * 2 + q, xi)

        def step(self, i, p, q, m, ref):
            return remote(ref, self.held(p, m), self.sending(i, m), self.arrival(p, m), self.to(self.core, q, par))

        def pair(self, i, p, m, ref):
            to = self.to(self.layer, pos, 1 - par)
            return remote(ref, block_of(self.kind, p, par, m), self.sending(i, m), self.arrived(p, par, m), to)

        def home(self, i, p, m, ref):
            to = self.to(self.layer, pos, par)
            return remote(ref, block_of(self.kind, p, par, m), self.sending(i, m), self.arrived(p, par, m), to)

        def moves(self, way, j, m):
            p = pos - j if way == 0 else pos + j
            i = 3 * p
            if j == 0:
                ref = self.held(p, m) if self.same else igv.at[cols(m)]
                return [
                    (self.step(i, p, pos + 1, m, ref), pos < LINE - 1),
                    (self.step(i + 1, p, pos - 1, m, ref), pos > 0),
                    (self.pair(i + 2, p, m, ref), None),
                ]
            ref = self.held(p, m)
            came = (p >= 0) if way == 0 else (p < LINE)
            q = pos + 1 if way == 0 else pos - 1
            goes = (q < LINE) if way == 0 else (q >= 0)
            out = [(self.step(i, p, q, m, ref), came & goes), (self.pair(i + 1, p, m, ref), came)]
            if not self.same:
                out.append((self.home(i + 2, p, m, ref), came))
            return out

        def each(self, way, j, m, what):
            for copy, when in self.moves(way, j, m):
                if when is None:
                    what(copy)
                else:
                    pl.when(when)(functools.partial(what, copy))

        def own(self, m):
            self.each(0, 0, m, lambda c: c.start())

        def pass_on(self, j, m):
            for way in range(2):
                p = pos - j if way == 0 else pos + j

                @pl.when((p >= 0) if way == 0 else (p < LINE))
                def _():
                    self.step(0, p, pos, m, self.held(p, m)).wait_recv()

                self.each(way, j, m, lambda c: c.start())

        def wide_held(self, p, q, m):
            return block_of(self.kind, p, q, m) if self.same else hgw.at[m, q, p]

        def wide_arrived(self, p, q, m):
            return self.arrived(p, q, m) if self.same else hws.at[m, p * 2 + q]

        def wide(self, j, q, m):
            out = []
            for way in range(2):
                p = pos - j if way == 0 else pos + j
                t = pos + 1 if way == 0 else pos - 1
                when = (t < LINE) if way == 0 else (t >= 0)
                came = (p >= 0) if way == 0 else (p < LINE)
                ref = self.wide_held(p, q, m)
                if j == 0 and q is par and not self.same:
                    ref = igv.at[cols(m)]
                i = 4 * (0 if q is par else 1) + p
                if j == 0 and way == 1:
                    i = 16 + (0 if q is par else 1)
                copy = remote(
                    ref, self.wide_held(p, q, m), self.sending(i, m), self.wide_arrived(p, q, m), self.to(self.core, t, par)
                )
                out.append((copy, when if j == 0 else when & came))
            return out

        def wide_home(self, way, j, q, m):
            p = pos - j if way == 0 else pos + j
            i = 8 + 4 * (0 if q is par else 1) + p
            to = self.to(self.layer, pos, par)
            return remote(self.wide_held(p, q, m), block_of(self.kind, p, q, m), self.sending(i, m), self.arrived(p, q, m), to)

        def wide_pair(self, m):
            ref = block_of(self.kind, pos, par, m) if self.same else igv.at[cols(m)]
            to = self.to(self.core, pos, 1 - par)
            return remote(ref, self.wide_held(pos, par, m), self.sending(18, m), self.wide_arrived(pos, par, m), to)

        def wide_own(self, m):
            for copy, when in self.wide(0, par, m):
                pl.when(when)(copy.start)
            self.wide_pair(m).start()

        def wide_on(self, j, m):
            for q in (par, 1 - par):
                if j == 0 and q is par:
                    continue
                if j == 0:
                    ref = self.wide_held(pos, q, m)
                    remote(ref, ref, fs.at[0, 0, 0], self.wide_arrived(pos, q, m), to_y).wait_recv()
                    if not self.same:
                        self.wide_home(0, 0, q, m).start()
                for way, (copy, when) in enumerate(self.wide(j, q, m)):
                    if j > 0:
                        if self.same:
                            pl.when(when)(copy.wait_recv)
                        else:
                            p = pos - j if way == 0 else pos + j
                            came = (p >= 0) if way == 0 else (p < LINE)
                            pl.when(came)(copy.wait_recv)
                            pl.when(came)(self.wide_home(way, j, q, m).start)
                    pl.when(when)(copy.start)

        def mixed_own(self, m):
            if isinstance(m, int):
                (self.own if m < self.plain else self.wide_own)(m)
                return
            for n in range(micro):
                pl.when(m == n)(functools.partial(self.mixed_own, n))

        def crossed(self):
            for m in range(self.plain, micro):
                self.wide_on(0, m)

        def mixed_on(self, j):
            for m in range(micro):
                (self.pass_on if m < self.plain else self.wide_on)(j, m)

        def mixed_take(self):
            for m in range(self.plain):
                for k in range(LINE):
                    p = lax.rem(pos + k, LINE)
                    ref = block_of(self.kind, p, 1 - par, m)
                    remote(ref, ref, fs.at[0, 0, 0], self.arrived(p, 1 - par, m), to_y).wait_recv()
            for way in range(2):
                for j in range(1, LINE):
                    p = pos - j if way == 0 else pos + j
                    last = (p >= 0) & (pos == LINE - 1) if way == 0 else (p < LINE) & (pos == 0)
                    for m in range(self.plain, micro):
                        for q in (par, 1 - par):
                            ref = block_of(self.kind, p, q, m)
                            come = remote(ref, ref, fs.at[0, 0, 0], self.arrived(p, q, m), to_y)
                            pl.when(last)(come.wait_recv)

        def mixed_sent(self):
            for m in range(self.plain):
                self.each(0, 0, m, lambda c: c.wait_send())
                for way in range(2):
                    for j in range(1, LINE):
                        self.each(way, j, m, lambda c: c.wait_send())
            for m in range(self.plain, micro):
                self.wide_pair(m).wait_send()
                for j in range(LINE):
                    for q in (par, 1 - par):
                        for way, (copy, when) in enumerate(self.wide(j, q, m)):
                            pl.when(when)(copy.wait_send)
                            if self.same or j == 0 and (q is par or way == 1):
                                continue
                            p = pos - j if way == 0 else pos + j
                            came = (p >= 0) if way == 0 else (p < LINE)
                            pl.when(came)(self.wide_home(way, j, q, m).wait_send)

        def take(self, i):
            p, q = lax.div(i, 2), lax.rem(i, 2)
            for m in range(micro):
                ref = block_of(self.kind, p, q, m)
                remote(ref, ref, fs.at[0, 0, 0], self.arrived(p, q, m), to_y).wait_recv()

    nm0, nm1, gd0, gd1 = Gather(0, 0, 1), Gather(0, 1, 1), Gather(1, 0, 1), Gather(1, 1, 1)

    def grad_rows(m):
        return pl.ds(pl.multiple_of(g * span + m * rows, rows), rows)

    @pl.when(s == 0)
    def _():
        first_x(0).wait_recv()
        for m in range(1, micro):
            first_x(m).start()

    @pl.when(s == 1)
    def _():
        for c in loads:
            c.wait()
        wupt[...] = wup[...].T
        for c in own_c:
            c.wait()
        for m in range(micro):
            first_c(m).start()
        for m in range(micro):
            first_c(m).wait_recv()
            for part in range(2):
                pr = pl.ds(m * rows + part * half, half)
                to = pl.ds(pl.multiple_of(g * span + m * rows + part * half, half), half)
                gd_all[to] = (gin[pr].astype(F32) * live_of(m, part)).astype(BF)
            gd1.mixed_own(m)
        gd1.crossed()
        gd1.mixed_on(1)

    def x_swap(e, m):
        i = (1 + e) * micro + m
        return remote(sbuf.at[e, m], rbuf.at[e, m], xs.at[i], xr.at[i], to_x)

    def give(e, m, part):
        part = part.astype(BF)
        sbuf[e, m, pl.ds(0, half)] = part[half:]
        sbuf[e, m, pl.ds(half, half)] = part[:half]
        x_swap(e, m).start()

    def c_copy(e, m):
        i = e * micro + m
        src, dst = ((act.at[m], rin.at[m]), (igv.at[cols(m)], gin.at[cols(m)]))[e]
        return remote(src, dst, cs.at[i], cr.at[i], to_c)

    def y_copies(when):
        out = []
        if when == 0:
            pairs = [(nrm_t, ynrm), (mtb, ymtb)]
        else:
            pairs = [(sb.at[1 - par], ysb)]
        for i, (src, dst) in enumerate(pairs):
            j = 2 * when + i
            out.append(remote(src, dst, ys.at[j], yr.at[j], to_y))
        return out

    def y_late(i, m):
        src, dst = (
            (gpt.at[1 - par, m], ygpt.at[0, m]),
            (gpt.at[2, m], ygpt.at[1, m]),
            (gbr.at[cols(m), pl.ds(pl.multiple_of((1 - par) * hw, 128), hw)], ygbr.at[cols(m)]),
        )[i]
        j = 3 + i * micro + m
        return remote(src, dst, ys.at[j], yr.at[j], to_y)

    def mixer_forward(m):
        @pl.when((s == 0) & (m > 0))
        def _():
            first_x(m).wait_recv()

        @pl.when(s == 1)
        def _():
            c_copy(0, m).wait_recv()

        @pl.when((s == 0) & (m == 0))
        def _():
            loads[0].wait()
            loads[1].wait()

        r = rin[m].astype(F32)
        n = (normed(r)[0] * gain1[...]).astype(BF)
        pts = []
        for q in range(3):
            p = dot(n, wqkv[q]).astype(BF)
            if q == 2:
                vnat[m] = p
            p = p.T
            pt[q, :, cols(m)] = p
            pts.append([p[h * hs : (h + 1) * hs] for h in range(heads)])
        nrm_t[:, cols(m)] = n.T
        ws = [fmap[0, h] for h in range(heads)]
        logits = [[dot(ws[h], pts[q][h], 0, 0) for h in range(heads)] for q in range(2)]
        feats = [[both_softmax(x) for x in logits[q]] for q in range(2)]
        scores = [dot(feats[1][h], feats[0][h], 0, 0) for h in range(heads)]
        keep = mask[m]
        scores = [x * keep for x in scores]
        dens = [1.0 / jnp.sum(x, axis=0, keepdims=True) for x in scores]
        scores = [x.astype(BF) for x in scores]
        mixed = [dot(pts[2][h], scores[h]) * dens[h] for h in range(heads)]
        for h in range(heads):
            hr = pl.ds(h * hs, hs)
            qf[m, h] = feats[0][h]
            kf[m, h] = feats[1][h]
            st[m, h] = scores[h]
            den_s[m, h] = jnp.broadcast_to(dens[h], (8, rows))
            mt[m, hr] = mixed[h]
            mtb[hr, cols(m)] = mixed[h].astype(BF)
        part = dot(mtb[:, cols(m)].T, wmix[...])
        give(0, m, part)
        rmid[m] = r + part

    def ffn_forward(m):
        x_swap(0, m).wait_recv()
        r = rmid[m] + rbuf[0, m].astype(F32)
        rmid[m] = r
        n = (normed(r)[0] * gain2[...]).astype(BF)
        nm_all[m, g] = n.T

        @pl.when(s == 0)
        def _():
            nm0.mixed_own(m)

        @pl.when(s == 1)
        def _():
            nm1.mixed_own(m)

        @pl.when((s == 0) & (m == 0))
        def _():
            loads[2].wait()
            loads[3].wait()

        h, slope = gelu_both(dot(n, wup[...]))
        h = h.astype(BF)
        gp[m] = slope.astype(BF)
        part = dot(h, wdown[...])
        give(1, m, part)
        rout[m] = r + part

    def act_copy(m):
        return local(act.at[m, pl.ds(0, half)], act_o.at[0, m], osem.at[m])

    def ig_copy(m):
        return local(igv.at[pl.ds(pl.multiple_of(m * rows, half), half)], ig_o.at[0, m], osem.at[micro + m])

    def end_forward(m):
        x_swap(1, m).wait_recv()
        act[m] = (rout[m] + rbuf[1, m].astype(F32)).astype(BF)

        @pl.when(s == 0)
        def _():
            c_copy(0, m).start()

        act_copy(m).start()

    each_micro(mixer_forward)
    @pl.when(s == 0)
    def _():
        for c in y_copies(0):
            c.start()

    @pl.when(s == 1)
    def _():
        gd1.mixed_on(2)

    each_micro(ffn_forward)
    @pl.when(s == 0)
    def _():
        each_micro(end_forward)


    tile = hb.shape[0]
    tiles = ff // tile

    def hid_rows(t):
        return pl.ds(pl.multiple_of(t * tile, tile), tile)

    @pl.when(s == 0)
    def _():
        wupt[...] = wup[...].T

        nm0.crossed()
        for j in range(1, LINE - 1):
            nm0.mixed_on(j)

    def ffn_back(m):
        @pl.when(s == 0)
        def _():
            c_copy(1, m).wait_recv()
            gd_all[grad_rows(m)] = gin[cols(m)]

        gd = gd_all[grad_rows(m)]
        gpre = (dot(gd, wdown[...], 1, 1) * gp[m].astype(F32)).astype(BF)
        part = dot(gpre, wup[...], 1, 1)
        give(2, m, part)
        part_f[m] = part

    def mixer_back(m):
        @pl.when((s == 1) & (m == 1))
        def _():
            nm1.crossed()
            nm1.mixed_on(1)

        x_swap(2, m).wait_recv()
        gn = part_f[m] + rbuf[2, m].astype(F32)
        xhat, rstd = normed(rmid[m])
        gacc[1, m] = jnp.broadcast_to(jnp.sum(gn * xhat, axis=0, keepdims=True), (8, width))
        gm = gd_all[grad_rows(m)].astype(F32) + norm_back(gn, gain2[...], xhat, rstd)
        rmid[m] = gm
        gb_ = gm.astype(BF)
        gbr[cols(m)] = gb_

        @pl.when(s == 0)
        def _():
            y_late(2, m).start()

        gmt = dot(wmix[...], gb_, 1, 1).astype(BF)
        dens = [den_s[m, h, pl.ds(0, 1)] for h in range(heads)]
        gos = [gmt[h * hs : (h + 1) * hs].astype(F32) for h in range(heads)]
        gdens = [-jnp.sum(gos[h] * mt[m, pl.ds(h * hs, hs)], axis=0, keepdims=True) * dens[h] for h in range(heads)]
        gnums = [(gos[h] * dens[h]).astype(BF) for h in range(heads)]
        pad = jnp.zeros_like(gnums[0])
        wide = [jnp.concatenate([x, pad] if h % 2 == 0 else [pad, x], axis=0) for h, x in enumerate(gnums)]
        gsts = [dot(vnat[m, :, pl.ds((h // 2) * 2 * hs, 2 * hs)], wide[h]) + gdens[h] for h in range(heads)]
        keep = mask[m]
        gsts = [(x * keep).astype(BF) for x in gsts]
        qfs = [qf[m, h] for h in range(heads)]
        kfs = [kf[m, h] for h in range(heads)]
        gqf = [dot(kfs[h], gsts[h]) for h in range(heads)]
        gkf = [dot(qfs[h], gsts[h], 1, 1) for h in range(heads)]
        gvs = [dot(gnums[h], st[m, h], 1, 1).astype(BF) for h in range(heads)]
        gql = [softmax_back(gqf[h], qfs[h]).astype(BF) for h in range(heads)]
        gkl = [softmax_back(gkf[h], kfs[h]).astype(BF) for h in range(heads)]
        gpq = [dot(fmap[0, h], gql[h]).astype(BF) for h in range(heads)]
        gpk = [dot(fmap[0, h], gkl[h]).astype(BF) for h in range(heads)]
        for h in range(heads):
            hr = pl.ds(h * hs, hs)
            gqk[0, hr, cols(m)] = gql[h]
            gqk[1, hr, cols(m)] = gkl[h]
            gpt[0, m, hr] = gpq[h]
            gpt[1, m, hr] = gpk[h]
            gpt[2, m, hr] = gvs[h]

        @pl.when(s == 0)
        def _():
            y_late(0, m).start()
            y_late(1, m).start()

        gnt = dot(wqkv[0], gpt[0, m]) + dot(wqkv[1], gpt[1, m]) + dot(wqkv[2], gpt[2, m])
        part = gnt.T
        give(3, m, part)
        part_f[m] = part

    def end_back(m):
        x_swap(3, m).wait_recv()
        gn = part_f[m] + rbuf[3, m].astype(F32)
        xhat, rstd = normed(rin[m].astype(F32))
        gacc[0, m] = jnp.broadcast_to(jnp.sum(gn * xhat, axis=0, keepdims=True), (8, width))
        igv[cols(m)] = (rmid[m] + norm_back(gn, gain1[...], xhat, rstd)).astype(BF)

        @pl.when(s == 1)
        def _():
            c_copy(1, m).start()
            gd0.mixed_own(m)

        ig_copy(m).start()

    each_micro(ffn_back)

    @pl.when(s == 0)
    def _():
        nm0.mixed_on(LINE - 1)

    @pl.when(s == 1)
    def _():
        each_micro(end_forward)
        gd1.mixed_on(3)

    each_micro(mixer_back)

    late = y_copies(1)

    cut = width // hw
    q_rows = pl.ds(0, width)
    v_rows = pl.ds(width, width // 2)
    m_rows = pl.ds(width + width // 2, hw)
    s_rows = pl.ds(width + width // 2 + hw, hs)
    v_part = pl.ds(pl.multiple_of(par * (width // 2), 16), width // 2)
    m_part = pl.ds(pl.multiple_of(par * hw, 128), hw)

    left = lax.broadcasted_iota(jnp.int32, (hs, 2 * hs), 1) < hs
    for p in range(heads // 2):
        pr = pl.ds(p * 2 * hs, 2 * hs)
        tot = dot(pt[0, pr], gqk[0, pr], 1, 1) + dot(pt[1, pr], gqk[1, pr], 1, 1)
        sb[0, :, pr] = jnp.where(left, tot[:hs], tot[hs:]).astype(BF)

    each_micro(end_back)

    row = lax.broadcasted_iota(jnp.int32, (hs, hw), 0)
    block = jnp.zeros((hs, hw), F32)
    for e in range(2):
        tot = gacc[e, 0, pl.ds(0, 1)]
        for m in range(1, micro):
            tot += gacc[e, m, pl.ds(0, 1)]
        for c in range(cut):
            block = jnp.where(row == e * cut + c, tot[:, c * hw : (c + 1) * hw], block)
    sb[1] = block.astype(BF)

    part_rows = hp.shape[0] // 2
    most = part_rows // 4
    cut_at = -(-most // 32) * 16

    class Line:
        def __init__(self, whole):
            self.whole = whole
            ends = [most * (i + 1) for i in range(3 if whole else 1)]
            self.ends = [0] + ends + [ends[-1] + cut_at, ends[-1] + most]
            self.n = len(self.ends) - 1

        def size(self, j):
            return self.ends[j + 1] - self.ends[j]

        def at(self, near, j):
            group = side if near else 1 - side
            return group * self.ends[-1] + self.ends[j]

        def piece(self, near, j):
            return pl.ds(pl.multiple_of(self.at(near, j), 16), self.size(j))

        def final(self, near, j):
            first_row = self.at(near, j) + (0 if self.whole else par * part_rows)
            return fin.at[pl.ds(pl.multiple_of(first_row, 16), self.size(j))]

        def come_out(self, near, j):
            return from_out.at[5 * near + j, pl.ds(0, self.size(j))]

        def come_opp(self, j):
            return from_opp.at[j, pl.ds(0, self.size(j))]

        def come_pair(self, j):
            return from_pair.at[j, pl.ds(0, self.size(j))]

        def send_in(self, near, j):
            i = 5 * near + j
            return remote(hp.at[self.piece(near, j)], self.come_out(near, j), ars.at[i], arr.at[i], to_mate)

        def send_over(self, j):
            return remote(hp.at[self.piece(0, j)], self.come_opp(j), ars.at[j], arr.at[10 + j], to_opp)

        def total_over(self, j):
            ref = self.final(1, j)
            return remote(ref, ref, ars.at[5 + j], arr.at[15 + j], to_opp)

        def total_out(self, near, j):
            i = 5 * near + j
            ref = self.final(near, j)
            return remote(ref, ref, ars.at[10 + i], arr.at[i], to_mate)

        def total_pair(self, near, j):
            i = 20 + 3 * near + j
            ref = self.final(near, j)
            return remote(ref, ref, ars.at[i], arr.at[i], to_y)

        def trade(self, j):
            return remote(hp.at[self.piece(1, j)], self.come_pair(j), ars.at[20 + j], arr.at[20 + j], to_y)

        def start(self, lo, hi):
            @pl.when(outer)
            def _():
                for j in range(lo, hi):
                    for near in range(2):
                        self.send_in(near, j).start()

        def collect(self, j):
            @pl.when(inner)
            def _():
                self.send_in(0, j).wait_recv()
                p = self.piece(0, j)
                hp[p] = (hp[p].astype(F32) + self.come_out(0, j)[...].astype(F32)).astype(BF)
                self.send_over(j).start()

        def total(self, j):
            @pl.when(inner)
            def _():
                self.send_in(1, j).wait_recv()
                self.send_over(j).wait_recv()
                p = self.piece(1, j)
                tot = hp[p].astype(F32) + self.come_out(1, j)[...].astype(F32) + self.come_opp(j)[...].astype(F32)
                if self.whole:
                    hp[p] = tot.astype(BF)
                    self.trade(j).start()
                else:
                    self.final(1, j)[...] = tot.astype(BF)
                    self.total_out(1, j).start()
                    self.total_over(j).start()

            if not self.whole:
                @pl.when(outer)
                def _():
                    self.total_out(1, j).wait_recv()

                self.total_pair(1, j).start()

        def settle(self, j):
            @pl.when(inner)
            def _():
                self.trade(j).wait_recv()
                tot = hp[self.piece(1, j)].astype(F32) + self.come_pair(j)[...].astype(F32)
                self.final(1, j)[...] = tot.astype(BF)
                self.total_out(1, j).start()
                self.total_over(j).start()

            self.across(1, j)

        def across(self, near, j):
            @pl.when(outer)
            def _():
                self.total_out(near, j).wait_recv()

        def passed(self, j):
            @pl.when(inner)
            def _():
                self.total_over(j).wait_recv()
                self.total_out(0, j).start()

            if not self.whole:
                @pl.when(outer)
                def _():
                    self.total_out(0, j).wait_recv()

                self.total_pair(0, j).start()
            else:
                self.across(0, j)

        def last(self):
            for near in range(2):
                for j in range(self.n):
                    self.total_pair(near, j).wait_recv()

        def finish(self):
            for j in range(self.n):
                @pl.when(outer)
                def _():
                    self.send_in(0, j).wait_send()
                    self.send_in(1, j).wait_send()

                @pl.when(inner)
                def _():
                    self.send_over(j).wait_send()
                    self.total_over(j).wait_send()
                    if self.whole:
                        self.trade(j).wait_send()

                mine = par == j % 2
                for near in range(2):
                    pl.when(inner)(self.total_out(near, j).wait_send)
                    if not self.whole:
                        self.total_pair(near, j).wait_send()

    first, second = Line(False), Line(True)

    @pl.when(s == 0)
    def _():
        late[0].start()
        for c in y_copies(0) + late:
            c.wait_recv()
        for m in range(micro):
            for i in range(3):
                y_late(i, m).wait_recv()
        q_tot = 0.0
        v_tot = 0.0
        for m in range(micro):
            q_tot += dot(nrm_t[:, cols(m)], gpt[par, m], 1, 1) + dot(ynrm[:, cols(m)], ygpt[0, m], 1, 1)
            v_tot += dot(nrm_t[v_part, cols(m)], gpt[2, m], 1, 1) + dot(ynrm[v_part, cols(m)], ygpt[1, m], 1, 1)
        hp[q_rows] = q_tot.astype(BF)
        hp[v_rows] = v_tot.astype(BF)
        hp[m_rows] = (dot(mtb[...], gbr[:, m_part]) + dot(ymtb[...], ygbr[...])).astype(BF)
        hp[s_rows] = (sb[par].astype(F32) + ysb[...].astype(F32)).astype(BF)
        first.start(0, first.n)

    @pl.when(s == 1)
    def _():
        for q in range(3):
            tot = dot(nrm_t[:, cols(0)], gpt[q, 0], 1, 1)
            for m in range(1, micro):
                tot += dot(nrm_t[:, cols(m)], gpt[q, m], 1, 1)
            hp[pl.ds(q * width, width)] = tot.astype(BF)
        tot = dot(mtb[...], gbr[...]).astype(BF)
        for c in range(cut):
            hp[pl.ds(3 * width + c * hw, hw)] = tot[:, c * hw : (c + 1) * hw]
        for e in range(2):
            hp[pl.ds(3 * width + cut * hw + e * hs, hs)] = sb[e]
        gd0.crossed()
        second.start(0, 2)
        gd0.mixed_on(1)
        nm1.mixed_on(2)
        gd0.mixed_on(2)
        nm1.mixed_on(3)
        gd1.mixed_take()

    @pl.when(s == 0)
    def _():
        nm0.mixed_take()
        for k in range(1, GROUP):
            gd0.take(lax.rem(g + k, GROUP))
        first.collect(0)

    @pl.when(s == 1)
    def _():
        second.collect(0)
        gd0.mixed_on(3)
        second.start(2, second.n)
        nm1.mixed_take()

    def up_copy(t):
        return local(wup.at[:, hid_rows(t)], up_o.at[:, hid_rows(t)], tsem.at[0, t])

    def down_copy(t):
        return local(wdown.at[hid_rows(t)], down_o.at[hid_rows(t)], tsem.at[1, t])

    for i in range(GROUP):
        for m in range(micro):
            nm_cat[:, pl.ds(i * span + m * rows, rows)] = nm_all[m, i]

    def tile_grads(t):
        hr = hid_rows(t)
        wu = wupt[hr]
        wd = wdown[hr]
        for i in range(GROUP):
            sl = slot(i)
            h, slope = gelu_both(dot(wu, nm_cat[:, sl]))
            hb[:, sl] = h.astype(BF)
            gb[:, sl] = (dot(wd, gd_all[sl], 1, 1) * slope).astype(BF)
        wup[:, hr] = dot(nm_cat[...], gb[...], 1, 1).astype(BF)
        wdown[hr] = dot(hb[...], gd_all[...]).astype(BF)
        up_copy(t).start()
        down_copy(t).start()

    plan = {
        (0, True): {
            0: [("total", 0)],
            1: [("collect", 1)],
            2: [("collect", 2), ("passed", 0), ("total", 1)],
            3: [("total", 2), ("passed", 1)],
            4: [("passed", 2)],
        },
        (0, False): {
            2: [("total", 0)],
            3: [("passed", 0), ("total", 1)],
            4: [("total", 2), ("passed", 1)],
            5: [("passed", 2)],
        },
        (1, True): {
            0: [("total", 0), ("collect", 1)],
            1: [("total", 1)],
            2: [("settle", 0)],
            3: [("collect", 2), ("settle", 1)],
            4: [("collect", 3), ("passed", 0), ("total", 2)],
            5: [
                ("collect", 4),
                ("passed", 1),
                ("total", 3),
                ("settle", 2),
                ("total", 4),
                ("settle", 3),
                ("passed", 2),
                ("settle", 4),
                ("passed", 3),
                ("passed", 4),
            ],
        },
        (1, False): {5: [(f, j) for j in range(5) for f in ("settle", "passed")]},
    }

    def one_tile(t, carry):
        tile_grads(t)
        for (layer, within), when in plan.items():
            for at, steps in when.items():
                @pl.when((s == layer) & (inner if within else outer) & (t == at))
                def _():
                    for name, *j in steps:
                        getattr((first, second)[layer], name)(*j)

        return carry

    lax.fori_loop(0, tiles, one_tile, 0)

    @pl.when(s == 0)
    def _():
        first.last()

    def outs_of(layer, out_copy):
        if layer == 1:
            out_copy(fin.at[pl.ds(0, 3 * width)], qkv_o)
            for c in range(cut):
                out_copy(fin.at[pl.ds(3 * width + c * hw, hw)], mix_o.at[:, pl.ds(c * hw, hw)])
            for e in range(2):
                out_copy(fin.at[pl.ds(3 * width + cut * hw + e * hs, hs)], small_o.at[e])
            return
        for e in range(2):
            at = e * part_rows
            out_copy(fin.at[pl.ds(at, width)], qkv_o.at[pl.ds(e * width, width)])
            at += width
            out_copy(fin.at[pl.ds(at, width // 2)], qkv_o.at[pl.ds(2 * width + e * (width // 2), width // 2)])
            at += width // 2
            out_copy(fin.at[pl.ds(at, hw)], mix_o.at[:, pl.ds(e * hw, hw)])
            at += hw
            out_copy(fin.at[pl.ds(at, hs)], small_o.at[e])

    def ended(layer):
        mine = []

        def keep(src, dst):
            c = local(src, dst, osem.at[2 * micro + 2 + len(mine)])
            c.start()
            mine.append(c)

        outs_of(layer, keep)
        for c in mine:
            c.wait()

    for t in range(tiles):
        up_copy(t).wait()
        down_copy(t).wait()

    @pl.when(s == 0)
    def _():
        ended(0)

    @pl.when(s == 1)
    def _():
        ended(1)

    @pl.when(s == 0)
    def _():
        for m in range(micro):
            first_x(m).wait_send()
            c_copy(0, m).wait_send()

    @pl.when(s == 1)
    def _():
        for m in range(micro):
            first_c(m).wait_send()
            c_copy(1, m).wait_send()

    for e in range(4):
        for m in range(micro):
            x_swap(e, m).wait_send()
    @pl.when(s == 0)
    def _():
        nm0.mixed_sent()

    @pl.when(s == 1)
    def _():
        gd1.mixed_sent()
        gd0.mixed_sent()
        nm1.mixed_sent()

    @pl.when(s == 0)
    def _():
        for c in y_copies(0) + y_copies(1):
            c.wait_send()
        for m in range(micro):
            for i in range(3):
                y_late(i, m).wait_send()
        first.finish()

    @pl.when(s == 1)
    def _():
        second.finish()

    for m in range(micro):
        act_copy(m).wait()
        ig_copy(m).wait()


def widen(act, ig, qkv, mix, small, up, down, act_o, ig_o, qkv_o, mix_o, feat_o, g1_o, g2_o, up_o, down_o, sem_in, sem_out, *bufs):
    hs = feat_o.shape[2]
    hw = mix.shape[0]
    cut = mix.shape[1] // hw
    blocks = []
    for src, dst, step in ((up, up_o, 192), (down, down_o, 384), (qkv, qkv_o, 768), (mix, mix_o, 192)):
        for lo in range(0, src.shape[0], step):
            if dst is qkv_o:
                blocks.append((src.at[pl.ds(lo, step)], dst.at[0, lo // step]))
            else:
                blocks.append((src.at[pl.ds(lo, step)], dst.at[0, pl.ds(lo, step)]))
    half = len(blocks)
    narrow, wide = bufs[:half], bufs[half : 2 * half]
    small_v, feat_v, g1_v, g2_v, act_v, ig_v = bufs[2 * half :]
    first = [
        pltpu.make_async_copy(src, dst, sem_in.at[half + i])
        for i, (src, dst) in enumerate(((small, small_v), (act, act_v), (ig, ig_v)))
    ]
    for c in first:
        c.start()
    loads = [pltpu.make_async_copy(b[0], n, sem_in.at[i]) for i, (b, n) in enumerate(zip(blocks, narrow))]
    for c in loads:
        c.start()
    outs = []

    def put(src, dst, i):
        c = pltpu.make_async_copy(src, dst, sem_out.at[i])
        c.start()
        outs.append(c)

    for c in first:
        c.wait()
    put(act_v, act_o, half + 3)
    put(ig_v, ig_o, half + 4)
    for h in range(feat_v.shape[1]):
        feat_v[0, h] = small_v[0, pl.ds(0, hs), pl.ds(h * hs, hs)].astype(F32)
    for c in range(cut):
        cs = pl.ds(c * hw, hw)
        g1_v[:, cs] = small_v[1, pl.ds(0, 16)].astype(F32)[c : c + 1]
        g2_v[:, cs] = small_v[1, pl.ds(0, 16)].astype(F32)[cut + c : cut + c + 1]
    put(feat_v, feat_o, half)
    put(g1_v, g1_o, half + 1)
    put(g2_v, g2_o, half + 2)
    for i, (b, n, w) in enumerate(zip(blocks, narrow, wide)):
        loads[i].wait()
        w[...] = n[...].astype(F32)
        put(w, b[1], i)
    for c in outs:
        c.wait()


def on_device(x, cot, starts, lengths, gain1, wqkv, fmap, wmix, gain2, wup, wdown):
    micro, half, width = x.shape
    rows = 2 * half
    span = micro * rows
    heads, hs = fmap.shape[1], fmap.shape[2]
    hw = heads * hs
    ff = wup.shape[2]
    cut = width // hw
    part_rows = width + width // 2 + hw + hs
    f, b = F32, BF
    vm = pltpu.VMEM
    dma = pltpu.SemaphoreType.DMA
    out = lambda shape, t=b: jax.ShapeDtypeStruct(shape, t)
    act, ig, qkv, mix, small, up, down = pl.pallas_call(
        kernel,
        out_shape=[
            out((1, micro, half, width)),
            out((1, micro, half, width)),
            out((3 * width, hw)),
            out((hw, width)),
            out((2, hs, hw)),
            out((width, ff)),
            out((ff, width)),
        ],
        in_specs=[ANY, ANY, SM, SM, VM, ANY, VM, ANY, VM, ANY, ANY],
        out_specs=[ANY] * 7,
        scratch_shapes=[
            vm((3, width, hw), b),
            vm((hw, width), b),
            vm((width, ff), b),
            vm((ff, width), b),
            vm((ff, width), b),
            vm((micro, rows, width), b),
            vm((span, width), b),
            vm((micro, rows, rows), f),
            vm((width, span), b),
            vm((3, hw, span), b),
            vm((micro, rows, hw), b),
            vm((micro, heads, 2 * hs, rows), b),
            vm((micro, heads, 2 * hs, rows), b),
            vm((micro, heads, rows, rows), b),
            vm((micro, hw, rows), f),
            vm((hw, span), b),
            vm((micro, heads, 8, rows), f),
            vm((micro, rows, width), f),
            vm((micro, GROUP, width, rows), b),
            vm((width, GROUP * span), b),
            vm((GROUP * span, width), b),
            vm((256, GROUP * span), b),
            vm((256, GROUP * span), b),
            vm((micro, rows, ff), b),
            vm((micro, rows, width), f),
            vm((micro, rows, width), f),
            vm((micro, rows, width), b),
            vm((span, width), b),
            vm((span, width), b),
            vm((2, hw, span), b),
            vm((3, micro, hw, rows), b),
            vm((2, micro, 8, width), f),
            vm((4, micro, rows, width), b),
            vm((4, micro, rows, width), b),
            vm((width, span), b),
            vm((hw, span), b),
            vm((2, micro, hw, rows), b),
            vm((span, hw), b),
            vm((2, hs, hw), b),
            vm((hs, hw), b),
            vm((2 * part_rows, hw), b),
            vm((2 * part_rows, hw), b),
            vm((10, part_rows // 4, hw), b),
            vm((5, part_rows // 4, hw), b),
            vm((5, part_rows // 4, hw), b),
            vm((LINE, span, width), b),
            vm((micro, 2, LINE, rows, width), b),
            dma((4 + micro,)),
            dma((5 * micro,)),
            dma((5 * micro,)),
            dma((2 * micro,)),
            dma((2 * micro,)),
            dma((2, micro, GROUP)),
            dma((micro, LINE)),
            dma((3, micro, 20)),
            dma((micro, GROUP)),
            dma((3 + 3 * micro,)),
            dma((3 + 3 * micro,)),
            dma((26,)),
            dma((26,)),
            dma((2 * micro + 10,)),
            dma((2, ff // 256)),
        ],
        compiler_params=pltpu.CompilerParams(
            collective_id=0, has_side_effects=True, vmem_limit_bytes=60 * 1024 * 1024
        ),
    )(x, cot, starts, lengths, gain1, wqkv, fmap, wmix, gain2, wup, wdown)

    n = lax.axis_size("dp")
    if n > GROUP:
        same_place = [[i + j * GROUP for j in range(n // GROUP)] for i in range(GROUP)]
        qkv, mix, small, up, down = lax.psum((qkv, mix, small, up, down), "dp", axis_index_groups=same_place)

    shapes = []
    for a, step in ((up, 192), (down, 384), (qkv, 768), (mix, 192)):
        shapes += [(step, a.shape[1])] * (a.shape[0] // step)
    outs = [(1, 3, width, hw), (1, hw, width), (1, heads, hs, hs), (1, width), (1, width), (1, width, ff), (1, ff, width)]
    act, ig, qkv, mix, features, g1, g2, up, down = pl.pallas_call(
        widen,
        out_shape=[out(act.shape), out(ig.shape)] + [out(o, f) for o in outs],
        in_specs=[ANY] * 7,
        out_specs=[ANY] * 9,
        scratch_shapes=[dma((len(shapes) + 3,)), dma((len(shapes) + 5,))]
        + [vm(o, b) for o in shapes]
        + [vm(o, f) for o in shapes]
        + [vm(small.shape, b), vm(outs[2], f), vm(outs[3], f), vm(outs[4], f), vm(act.shape, b), vm(ig.shape, b)],
        compiler_params=pltpu.CompilerParams(vmem_limit_bytes=60 * 1024 * 1024),
    )(act, ig, qkv, mix, small, up, down)
    return act, ig, g1, qkv, features, mix, g2, up, down


def solution(mesh):
    in_specs = (
        P(None, ("dp", "mp"), None),
        P(None, ("dp", "mp"), None),
        P(None, "dp", None),
        P(None, "dp", None),
        P("section", None),
        P("section", None, None, "mp"),
        P("section", "mp", None, None),
        P("section", "mp", None),
        P("section", None),
        P("section", None, "mp"),
        P("section", "mp", None),
    )
    out_specs = (
        P("section", None, ("dp", "mp"), None),
        P("section", None, ("dp", "mp"), None),
        P("section", None),
        P("section", None, None, "mp"),
        P("section", "mp", None, None),
        P("section", "mp", None),
        P("section", None),
        P("section", None, "mp"),
        P("section", "mp", None),
    )
    return jax.shard_map(
        on_device, mesh=mesh, in_specs=in_specs, out_specs=out_specs, check_vma=False
    )
```

```python
import functools

import functools

import jax
import jax.numpy as jnp
from jax import lax
from jax.experimental import pallas as pl
from jax.experimental.pallas import tpu as pltpu
from jax.sharding import PartitionSpec as P

STRETCH = 64
GROUP = 8
LINE = 4
MESH = pl.DeviceIdType.MESH
BF = jnp.bfloat16
F32 = jnp.float32
ANY = pl.BlockSpec(memory_space=pl.ANY)
VM = pl.BlockSpec(memory_space=pltpu.VMEM)
SM = pl.BlockSpec(memory_space=pltpu.SMEM)


def dot(a, b, ca=1, cb=0):
    return lax.dot_general(a, b, (((ca,), (cb,)), ((), ())), preferred_element_type=F32)


def normed(v):
    mean = jnp.mean(v, axis=1, keepdims=True)
    c = v - mean
    rstd = lax.rsqrt(jnp.mean(c * c, axis=1, keepdims=True) + 1e-05)
    return c * rstd, rstd


def norm_back(grad, gain, xhat, rstd):
    t = grad * gain
    mean_t = jnp.mean(t, axis=1, keepdims=True)
    mean_tx = jnp.mean(t * xhat, axis=1, keepdims=True)
    return rstd * (t - mean_t - xhat * mean_tx)


def gelu_both(x):
    k = 0.7978845608028654
    x2 = x * x
    g = 0.5 + 0.5 * jnp.tanh(x * (k + (k * 0.044715) * x2))
    h = x * g
    return h, g + h * (1.0 - g) * (2.0 * k + (6.0 * k * 0.044715) * x2)


def both_softmax(logit):
    up = jnp.exp(logit - jnp.max(logit, axis=0, keepdims=True))
    down = jnp.exp(jnp.min(logit, axis=0, keepdims=True) - logit)
    up = up * (1.0 / jnp.sum(up, axis=0, keepdims=True))
    down = down * (1.0 / jnp.sum(down, axis=0, keepdims=True))
    return jnp.concatenate([up.astype(BF), down.astype(BF)], axis=0)


def softmax_back(grad, feat):
    n = grad.shape[0] // 2
    g = grad * feat.astype(F32)
    p = feat.astype(F32)
    one = g[:n] - p[:n] * jnp.sum(g[:n], axis=0, keepdims=True)
    two = g[n:] - p[n:] * jnp.sum(g[n:], axis=0, keepdims=True)
    return one - two


def kernel(
    x_in, cot, starts, lengths, gain1, wqkv_h, fmap, wmix_h, gain2, up_h, down_h,
    act_o, ig_o, qkv_o, mix_o, small_o, up_o, down_o,
    wqkv, wmix, wup, wdown, wupt, rin, gin, mask,
    nrm_t, pt, vnat, qf, kf, st, mt, mtb, den_s, rmid, nm_all, nm_cat, gd_all, hb, gb, gp, part_f, rout, act, igv,
    gbr, gqk, gpt, gacc, sbuf, rbuf,
    ynrm, ymtb, ygpt, ygbr, sb, ysb, hp, fin, from_out, from_opp, from_pair, hgd, hgw,
    lsem, xs, xr, cs, cr, la, ha, fs, hws, ys, yr, ars, arr, osem, tsem,
):
    s = lax.axis_index("section")
    d = lax.axis_index("dp")
    xi = lax.axis_index("mp")
    micro, half, width = x_in.shape
    rows = 2 * half
    span = micro * rows
    heads, hs = fmap.shape[1], fmap.shape[2]
    hw = heads * hs
    ff = up_h.shape[2]
    g = lax.rem(d, GROUP)
    base = d - g
    pos = lax.div(g, 2)
    par = lax.rem(g, 2)
    to_x = (s, d, 1 - xi)
    to_c = (1 - s, d, xi)
    to_y = (s, base + pos * 2 + 1 - par, xi)
    outer = (pos == 0) | (pos == LINE - 1)
    inner = (pos > 0) & (pos < LINE - 1)
    side = lax.div(pos, 2)
    to_mate = (s, base + (side * 4 + 1 - pos) * 2 + par, xi)
    to_opp = (s, base + (LINE - 1 - pos) * 2 + par, xi)

    def other_core(to):
        return (1 - s,) + to[1:]

    def other_core(to):
        return (1 - s,) + to[1:]

    def at(core, p, q):
        return (core, base + p * 2 + q, xi)

    def greet(act):
        for to in (to_x, to_c, to_y, other_core(to_y)):
            act(to)
        pl.when(pos < LINE - 1)(lambda: act(at(s, pos + 1, par)))
        pl.when(pos > 0)(lambda: act(at(s, pos - 1, par)))

    def local(src, dst, sem):
        return pltpu.make_async_copy(src, dst, sem)

    def remote(src, dst, ss, rs, to):
        return pltpu.make_async_remote_copy(
            src_ref=src, dst_ref=dst, send_sem=ss, recv_sem=rs, device_id=to, device_id_type=MESH
        )

    def cols(m):
        return pl.ds(pl.multiple_of(m * rows, rows), rows)

    def each_micro(f):
        lax.fori_loop(0, micro, lambda m, c: (f(m), c)[1], 0)

    def slot(i):
        return pl.ds(pl.multiple_of(i * span, span), span)

    own_x = local(x_in, rin.at[:, pl.ds(0, half)], lsem.at[4])
    own_c = [local(cot.at[m], gin.at[pl.ds(m * rows, half)], lsem.at[4 + m]) for m in range(micro)]
    loads = [
        local(wqkv_h.at[0], wqkv, lsem.at[0]),
        local(wmix_h.at[0], wmix, lsem.at[1]),
        local(up_h.at[0], wup, lsem.at[2]),
        local(down_h.at[0], wdown, lsem.at[3]),
    ]

    def first_x(m):
        return remote(rin.at[m, pl.ds(0, half)], rin.at[m, pl.ds(half, half)], xs.at[m], xr.at[m], to_x)

    def first_c(m):
        src, dst = gin.at[pl.ds(m * rows, half)], gin.at[pl.ds(m * rows + half, half)]
        return remote(src, dst, xs.at[m], xr.at[m], to_x)

    @pl.when(s == 0)
    def _():
        own_x.start()

    @pl.when(s == 1)
    def _():
        for c in own_c:
            c.start()

    for c in loads:
        c.start()

    barrier = pltpu.get_barrier_semaphore()
    greet(lambda to: pl.semaphore_signal(barrier, inc=1, device_id=to, device_id_type=MESH))
    pl.semaphore_wait(barrier, jnp.where(inner, 6, 5))

    @pl.when(s == 0)
    def _():
        own_x.wait()
        first_x(0).start()

    jj = lax.broadcasted_iota(jnp.int32, (rows, rows), 0)
    ii = lax.broadcasted_iota(jnp.int32, (rows, rows), 1)
    j_own, i_own = jj < half, ii < half
    inside = ((j_own == i_own) & (jj <= ii)).astype(F32)
    own_first = jnp.where(xi == 0, 1.0, 0.0)
    across = jnp.where(j_own & ~i_own, own_first, jnp.where(i_own & ~j_own, 1.0 - own_first, 0.0))
    slots = starts.shape[2]
    for m in range(micro):
        n0 = jnp.int32(0)
        n1 = jnp.int32(0)
        for j in range(slots):
            n0 += jnp.where(starts[m, 0, j] <= 0, 1, 0)
            n1 += jnp.where(starts[m, 0, j] <= STRETCH, 1, 0)
        same = jnp.where(n0 == n1, 1.0, 0.0)
        mask[m] = inside + across * same

    def live_of(m, part):
        block = xi if part == 0 else 1 - xi
        begin = jnp.int32(0)
        for j in range(slots):
            begin = jnp.where(starts[m, 0, j] <= block * STRETCH, jnp.maximum(begin, starts[m, 0, j]), begin)
        length = jnp.int32(0)
        for j in range(slots):
            length += jnp.where(starts[m, 0, j] == begin, lengths[m, 0, j], 0)
        row = block * STRETCH + lax.broadcasted_iota(jnp.int32, (half, width), 0)
        return (row - begin < length).astype(F32)

    def block_of(kind, p, q, m):
        i = p * 2 + q
        return nm_all.at[m, i] if kind == 0 else gd_all.at[pl.ds(pl.multiple_of(i * span + m * rows, rows), rows)]

    class Gather:
        def __init__(self, kind, layer, plain):
            self.kind, self.layer = kind, layer
            self.plain = plain
            self.same = (kind, layer) != (1, 0)
            self.core = layer if self.same else 1

        def held(self, p, m):
            if self.same:
                return block_of(self.kind, p, par, m)
            return hgd.at[p, cols(m)]

        def arrived(self, p, q, m):
            return la.at[self.kind, m, p * 2 + q]

        def arrival(self, p, m):
            return self.arrived(p, par, m) if self.same else ha.at[m, p]

        def sending(self, i, m):
            return fs.at[self.kind if self.same else 2, i + 12 * m]

        def to(self, core, p, q):
            return (core, base + p * 2 + q, xi)

        def step(self, i, p, q, m, ref):
            return remote(ref, self.held(p, m), self.sending(i, m), self.arrival(p, m), self.to(self.core, q, par))

        def pair(self, i, p, m, ref):
            to = self.to(self.layer, pos, 1 - par)
            return remote(ref, block_of(self.kind, p, par, m), self.sending(i, m), self.arrived(p, par, m), to)

        def home(self, i, p, m, ref):
            to = self.to(self.layer, pos, par)
            return remote(ref, block_of(self.kind, p, par, m), self.sending(i, m), self.arrived(p, par, m), to)

        def moves(self, way, j, m):
            p = pos - j if way == 0 else pos + j
            i = 3 * p
            if j == 0:
                ref = self.held(p, m) if self.same else igv.at[cols(m)]
                return [
                    (self.step(i, p, pos + 1, m, ref), pos < LINE - 1),
                    (self.step(i + 1, p, pos - 1, m, ref), pos > 0),
                    (self.pair(i + 2, p, m, ref), None),
                ]
            ref = self.held(p, m)
            came = (p >= 0) if way == 0 else (p < LINE)
            q = pos + 1 if way == 0 else pos - 1
            goes = (q < LINE) if way == 0 else (q >= 0)
            out = [(self.step(i, p, q, m, ref), came & goes), (self.pair(i + 1, p, m, ref), came)]
            if not self.same:
                out.append((self.home(i + 2, p, m, ref), came))
            return out

        def each(self, way, j, m, what):
            for copy, when in self.moves(way, j, m):
                if when is None:
                    what(copy)
                else:
                    pl.when(when)(functools.partial(what, copy))

        def own(self, m):
            self.each(0, 0, m, lambda c: c.start())

        def pass_on(self, j, m):
            for way in range(2):
                p = pos - j if way == 0 else pos + j

                @pl.when((p >= 0) if way == 0 else (p < LINE))
                def _():
                    self.step(0, p, pos, m, self.held(p, m)).wait_recv()

                self.each(way, j, m, lambda c: c.start())

        def wide_held(self, p, q, m):
            return block_of(self.kind, p, q, m) if self.same else hgw.at[m, q, p]

        def wide_arrived(self, p, q, m):
            return self.arrived(p, q, m) if self.same else hws.at[m, p * 2 + q]

        def wide(self, j, q, m):
            out = []
            for way in range(2):
                p = pos - j if way == 0 else pos + j
                t = pos + 1 if way == 0 else pos - 1
                when = (t < LINE) if way == 0 else (t >= 0)
                came = (p >= 0) if way == 0 else (p < LINE)
                ref = self.wide_held(p, q, m)
                if j == 0 and q is par and not self.same:
                    ref = igv.at[cols(m)]
                i = 4 * (0 if q is par else 1) + p
                if j == 0 and way == 1:
                    i = 16 + (0 if q is par else 1)
                copy = remote(
                    ref, self.wide_held(p, q, m), self.sending(i, m), self.wide_arrived(p, q, m), self.to(self.core, t, par)
                )
                out.append((copy, when if j == 0 else when & came))
            return out

        def wide_home(self, way, j, q, m):
            p = pos - j if way == 0 else pos + j
            i = 8 + 4 * (0 if q is par else 1) + p
            to = self.to(self.layer, pos, par)
            return remote(self.wide_held(p, q, m), block_of(self.kind, p, q, m), self.sending(i, m), self.arrived(p, q, m), to)

        def wide_pair(self, m):
            ref = block_of(self.kind, pos, par, m) if self.same else igv.at[cols(m)]
            to = self.to(self.core, pos, 1 - par)
            return remote(ref, self.wide_held(pos, par, m), self.sending(18, m), self.wide_arrived(pos, par, m), to)

        def wide_own(self, m):
            for copy, when in self.wide(0, par, m):
                pl.when(when)(copy.start)
            self.wide_pair(m).start()

        def wide_on(self, j, m):
            for q in (par, 1 - par):
                if j == 0 and q is par:
                    continue
                if j == 0:
                    ref = self.wide_held(pos, q, m)
                    remote(ref, ref, fs.at[0, 0], self.wide_arrived(pos, q, m), to_y).wait_recv()
                    if not self.same:
                        self.wide_home(0, 0, q, m).start()
                for way, (copy, when) in enumerate(self.wide(j, q, m)):
                    if j > 0:
                        if self.same:
                            pl.when(when)(copy.wait_recv)
                        else:
                            p = pos - j if way == 0 else pos + j
                            came = (p >= 0) if way == 0 else (p < LINE)
                            pl.when(came)(copy.wait_recv)
                            pl.when(came)(self.wide_home(way, j, q, m).start)
                    pl.when(when)(copy.start)

        def mixed_own(self, m):
            if isinstance(m, int):
                (self.own if m < self.plain else self.wide_own)(m)
                return
            for n in range(micro):
                pl.when(m == n)(functools.partial(self.mixed_own, n))

        def crossed(self):
            for m in range(self.plain, micro):
                self.wide_on(0, m)

        def mixed_on(self, j):
            for m in range(micro):
                (self.pass_on if m < self.plain else self.wide_on)(j, m)

        def mixed_take(self):
            for m in range(self.plain):
                for k in range(LINE):
                    p = lax.rem(pos + k, LINE)
                    ref = block_of(self.kind, p, 1 - par, m)
                    remote(ref, ref, fs.at[0, 0], self.arrived(p, 1 - par, m), to_y).wait_recv()
            for way in range(2):
                for j in range(1, LINE):
                    p = pos - j if way == 0 else pos + j
                    last = (p >= 0) & (pos == LINE - 1) if way == 0 else (p < LINE) & (pos == 0)
                    for m in range(self.plain, micro):
                        for q in (par, 1 - par):
                            ref = block_of(self.kind, p, q, m)
                            come = remote(ref, ref, fs.at[0, 0], self.arrived(p, q, m), to_y)
                            pl.when(last)(come.wait_recv)

        def mixed_sent(self):
            for m in range(self.plain):
                self.each(0, 0, m, lambda c: c.wait_send())
                for way in range(2):
                    for j in range(1, LINE):
                        self.each(way, j, m, lambda c: c.wait_send())
            for m in range(self.plain, micro):
                self.wide_pair(m).wait_send()
                for j in range(LINE):
                    for q in (par, 1 - par):
                        for way, (copy, when) in enumerate(self.wide(j, q, m)):
                            pl.when(when)(copy.wait_send)
                            if self.same or j == 0 and (q is par or way == 1):
                                continue
                            p = pos - j if way == 0 else pos + j
                            came = (p >= 0) if way == 0 else (p < LINE)
                            pl.when(came)(self.wide_home(way, j, q, m).wait_send)

        def take(self, i):
            p, q = lax.div(i, 2), lax.rem(i, 2)
            for m in range(micro):
                ref = block_of(self.kind, p, q, m)
                remote(ref, ref, fs.at[0, 0], self.arrived(p, q, m), to_y).wait_recv()

    nm0, nm1, gd0, gd1 = Gather(0, 0, 1), Gather(0, 1, 1), Gather(1, 0, 1), Gather(1, 1, 1)

    def grad_rows(m):
        return pl.ds(pl.multiple_of(g * span + m * rows, rows), rows)

    @pl.when(s == 0)
    def _():
        first_x(0).wait_recv()
        for m in range(1, micro):
            first_x(m).start()

    @pl.when(s == 1)
    def _():
        for c in loads:
            c.wait()
        wupt[...] = wup[...].T
        for c in own_c:
            c.wait()
        for m in range(micro):
            first_c(m).start()
        for m in range(micro):
            first_c(m).wait_recv()
            for part in range(2):
                pr = pl.ds(m * rows + part * half, half)
                to = pl.ds(pl.multiple_of(g * span + m * rows + part * half, half), half)
                gd_all[to] = (gin[pr].astype(F32) * live_of(m, part)).astype(BF)
            gd1.mixed_own(m)
        gd1.crossed()
        gd1.mixed_on(1)

    def x_swap(e, m):
        i = (1 + e) * micro + m
        return remote(sbuf.at[e, m], rbuf.at[e, m], xs.at[i], xr.at[i], to_x)

    def give(e, m, part):
        part = part.astype(BF)
        sbuf[e, m, pl.ds(0, half)] = part[half:]
        sbuf[e, m, pl.ds(half, half)] = part[:half]
        x_swap(e, m).start()

    def c_copy(e, m):
        i = e * micro + m
        src, dst = ((act.at[m], rin.at[m]), (igv.at[cols(m)], gin.at[cols(m)]))[e]
        return remote(src, dst, cs.at[i], cr.at[i], to_c)

    def y_copies(when):
        out = []
        if when == 0:
            pairs = [(nrm_t, ynrm), (mtb, ymtb)]
        else:
            pairs = [(sb.at[1 - par], ysb)]
        for i, (src, dst) in enumerate(pairs):
            j = 2 * when + i
            out.append(remote(src, dst, ys.at[j], yr.at[j], to_y))
        return out

    def y_late(i, m):
        src, dst = (
            (gpt.at[1 - par, m], ygpt.at[0, m]),
            (gpt.at[2, m], ygpt.at[1, m]),
            (gbr.at[cols(m), pl.ds(pl.multiple_of((1 - par) * hw, 128), hw)], ygbr.at[cols(m)]),
        )[i]
        j = 3 + i * micro + m
        return remote(src, dst, ys.at[j], yr.at[j], to_y)

    def mixer_forward(m):
        @pl.when((s == 0) & (m > 0))
        def _():
            first_x(m).wait_recv()

        @pl.when(s == 1)
        def _():
            c_copy(0, m).wait_recv()

        @pl.when((s == 0) & (m == 0))
        def _():
            loads[0].wait()
            loads[1].wait()

        r = rin[m].astype(F32)
        n = (normed(r)[0] * gain1[...]).astype(BF)
        pts = []
        for q in range(3):
            p = dot(n, wqkv[q]).astype(BF)
            if q == 2:
                vnat[m] = p
            p = p.T
            pt[q, :, cols(m)] = p
            pts.append([p[h * hs : (h + 1) * hs] for h in range(heads)])
        nrm_t[:, cols(m)] = n.T
        ws = [fmap[0, h] for h in range(heads)]
        logits = [[dot(ws[h], pts[q][h], 0, 0) for h in range(heads)] for q in range(2)]
        feats = [[both_softmax(x) for x in logits[q]] for q in range(2)]
        scores = [dot(feats[1][h], feats[0][h], 0, 0) for h in range(heads)]
        keep = mask[m]
        scores = [x * keep for x in scores]
        dens = [1.0 / jnp.sum(x, axis=0, keepdims=True) for x in scores]
        scores = [x.astype(BF) for x in scores]
        mixed = [dot(pts[2][h], scores[h]) * dens[h] for h in range(heads)]
        for h in range(heads):
            hr = pl.ds(h * hs, hs)
            qf[m, h] = feats[0][h]
            kf[m, h] = feats[1][h]
            st[m, h] = scores[h]
            den_s[m, h] = jnp.broadcast_to(dens[h], (8, rows))
            mt[m, hr] = mixed[h]
            mtb[hr, cols(m)] = mixed[h].astype(BF)
        part = dot(mtb[:, cols(m)].T, wmix[...])
        give(0, m, part)
        rmid[m] = r + part

    def ffn_forward(m):
        x_swap(0, m).wait_recv()
        r = rmid[m] + rbuf[0, m].astype(F32)
        rmid[m] = r
        n = (normed(r)[0] * gain2[...]).astype(BF)
        nm_all[m, g] = n.T

        @pl.when(s == 0)
        def _():
            nm0.mixed_own(m)

        @pl.when(s == 1)
        def _():
            nm1.mixed_own(m)

        @pl.when((s == 0) & (m == 0))
        def _():
            loads[2].wait()
            loads[3].wait()

        h, slope = gelu_both(dot(n, wup[...]))
        h = h.astype(BF)
        gp[m] = slope.astype(BF)
        part = dot(h, wdown[...])
        give(1, m, part)
        rout[m] = r + part

    def act_copy(m):
        return local(act.at[m, pl.ds(0, half)], act_o.at[0, m], osem.at[m])

    def ig_copy(m):
        return local(igv.at[pl.ds(pl.multiple_of(m * rows, half), half)], ig_o.at[0, m], osem.at[micro + m])

    def end_forward(m):
        x_swap(1, m).wait_recv()
        act[m] = (rout[m] + rbuf[1, m].astype(F32)).astype(BF)

        @pl.when(s == 0)
        def _():
            c_copy(0, m).start()

        act_copy(m).start()

    each_micro(mixer_forward)
    @pl.when(s == 0)
    def _():
        for c in y_copies(0):
            c.start()

    @pl.when(s == 1)
    def _():
        gd1.mixed_on(2)

    each_micro(ffn_forward)
    @pl.when(s == 0)
    def _():
        each_micro(end_forward)


    tile = hb.shape[0]
    tiles = ff // tile

    def hid_rows(t):
        return pl.ds(pl.multiple_of(t * tile, tile), tile)

    @pl.when(s == 0)
    def _():
        wupt[...] = wup[...].T

        nm0.crossed()
        for j in range(1, LINE - 1):
            nm0.mixed_on(j)

    def ffn_back(m):
        @pl.when(s == 0)
        def _():
            c_copy(1, m).wait_recv()
            gd_all[grad_rows(m)] = gin[cols(m)]

        gd = gd_all[grad_rows(m)]
        gpre = (dot(gd, wdown[...], 1, 1) * gp[m].astype(F32)).astype(BF)
        part = dot(gpre, wup[...], 1, 1)
        give(2, m, part)
        part_f[m] = part

    def mixer_back(m):
        @pl.when((s == 1) & (m == 1))
        def _():
            nm1.crossed()

        x_swap(2, m).wait_recv()
        gn = part_f[m] + rbuf[2, m].astype(F32)
        xhat, rstd = normed(rmid[m])
        gacc[1, m] = jnp.broadcast_to(jnp.sum(gn * xhat, axis=0, keepdims=True), (8, width))
        gm = gd_all[grad_rows(m)].astype(F32) + norm_back(gn, gain2[...], xhat, rstd)
        rmid[m] = gm
        gb_ = gm.astype(BF)
        gbr[cols(m)] = gb_

        @pl.when(s == 0)
        def _():
            y_late(2, m).start()

        gmt = dot(wmix[...], gb_, 1, 1).astype(BF)
        dens = [den_s[m, h, pl.ds(0, 1)] for h in range(heads)]
        gos = [gmt[h * hs : (h + 1) * hs].astype(F32) for h in range(heads)]
        gdens = [-jnp.sum(gos[h] * mt[m, pl.ds(h * hs, hs)], axis=0, keepdims=True) * dens[h] for h in range(heads)]
        gnums = [(gos[h] * dens[h]).astype(BF) for h in range(heads)]
        pad = jnp.zeros_like(gnums[0])
        wide = [jnp.concatenate([x, pad] if h % 2 == 0 else [pad, x], axis=0) for h, x in enumerate(gnums)]
        gsts = [dot(vnat[m, :, pl.ds((h // 2) * 2 * hs, 2 * hs)], wide[h]) + gdens[h] for h in range(heads)]
        keep = mask[m]
        gsts = [(x * keep).astype(BF) for x in gsts]
        qfs = [qf[m, h] for h in range(heads)]
        kfs = [kf[m, h] for h in range(heads)]
        gqf = [dot(kfs[h], gsts[h]) for h in range(heads)]
        gkf = [dot(qfs[h], gsts[h], 1, 1) for h in range(heads)]
        gvs = [dot(gnums[h], st[m, h], 1, 1).astype(BF) for h in range(heads)]
        gql = [softmax_back(gqf[h], qfs[h]).astype(BF) for h in range(heads)]
        gkl = [softmax_back(gkf[h], kfs[h]).astype(BF) for h in range(heads)]
        gpq = [dot(fmap[0, h], gql[h]).astype(BF) for h in range(heads)]
        gpk = [dot(fmap[0, h], gkl[h]).astype(BF) for h in range(heads)]
        for h in range(heads):
            hr = pl.ds(h * hs, hs)
            gqk[0, hr, cols(m)] = gql[h]
            gqk[1, hr, cols(m)] = gkl[h]
            gpt[0, m, hr] = gpq[h]
            gpt[1, m, hr] = gpk[h]
            gpt[2, m, hr] = gvs[h]

        @pl.when(s == 0)
        def _():
            y_late(0, m).start()
            y_late(1, m).start()

        gnt = dot(wqkv[0], gpt[0, m]) + dot(wqkv[1], gpt[1, m]) + dot(wqkv[2], gpt[2, m])
        part = gnt.T
        give(3, m, part)
        part_f[m] = part

    def end_back(m):
        x_swap(3, m).wait_recv()
        gn = part_f[m] + rbuf[3, m].astype(F32)
        xhat, rstd = normed(rin[m].astype(F32))
        gacc[0, m] = jnp.broadcast_to(jnp.sum(gn * xhat, axis=0, keepdims=True), (8, width))
        igv[cols(m)] = (rmid[m] + norm_back(gn, gain1[...], xhat, rstd)).astype(BF)

        @pl.when(s == 1)
        def _():
            c_copy(1, m).start()
            gd0.mixed_own(m)

        ig_copy(m).start()

    each_micro(ffn_back)

    @pl.when(s == 0)
    def _():
        nm0.mixed_on(LINE - 1)

    @pl.when(s == 1)
    def _():
        each_micro(end_forward)
        gd1.mixed_on(3)

    each_micro(mixer_back)

    late = y_copies(1)

    cut = width // hw
    q_rows = pl.ds(0, width)
    v_rows = pl.ds(width, width // 2)
    m_rows = pl.ds(width + width // 2, hw)
    s_rows = pl.ds(width + width // 2 + hw, hs)
    v_part = pl.ds(pl.multiple_of(par * (width // 2), 16), width // 2)
    m_part = pl.ds(pl.multiple_of(par * hw, 128), hw)

    left = lax.broadcasted_iota(jnp.int32, (hs, 2 * hs), 1) < hs
    for p in range(heads // 2):
        pr = pl.ds(p * 2 * hs, 2 * hs)
        tot = dot(pt[0, pr], gqk[0, pr], 1, 1) + dot(pt[1, pr], gqk[1, pr], 1, 1)
        sb[0, :, pr] = jnp.where(left, tot[:hs], tot[hs:]).astype(BF)

    each_micro(end_back)

    row = lax.broadcasted_iota(jnp.int32, (hs, hw), 0)
    block = jnp.zeros((hs, hw), F32)
    for e in range(2):
        tot = gacc[e, 0, pl.ds(0, 1)]
        for m in range(1, micro):
            tot += gacc[e, m, pl.ds(0, 1)]
        for c in range(cut):
            block = jnp.where(row == e * cut + c, tot[:, c * hw : (c + 1) * hw], block)
    sb[1] = block.astype(BF)

    part_rows = hp.shape[0] // 2
    most = 464

    def ends_of(total, shares):
        out = [0]
        for share in shares:
            out.append(min(total, -(-total * share // 1600) * 16))
        return out

    WHOLE, HALF = (25, 50, 75, 88, 100), (50, 76, 100)

    class Line:
        def __init__(self, whole):
            self.whole = whole
            self.ends = ends_of(part_rows * (2 if whole else 1) // 2, WHOLE if whole else HALF)
            self.n = len(self.ends) - 1

        def size(self, j):
            return self.ends[j + 1] - self.ends[j]

        def at(self, near, j):
            group = side if near else 1 - side
            return group * self.ends[-1] + self.ends[j]

        def piece(self, near, j):
            return pl.ds(pl.multiple_of(self.at(near, j), 16), self.size(j))

        def final(self, near, j):
            first_row = self.at(near, j) + (0 if self.whole else par * part_rows)
            return fin.at[pl.ds(pl.multiple_of(first_row, 16), self.size(j))]

        def come_out(self, near, j):
            return from_out.at[5 * near + j, pl.ds(0, self.size(j))]

        def come_opp(self, j):
            return from_opp.at[j, pl.ds(0, self.size(j))]

        def come_pair(self, j):
            return from_pair.at[j, pl.ds(0, self.size(j))]

        def send_in(self, near, j):
            i = 5 * near + j
            return remote(hp.at[self.piece(near, j)], self.come_out(near, j), ars.at[i], arr.at[i], to_mate)

        def send_over(self, j):
            return remote(hp.at[self.piece(0, j)], self.come_opp(j), ars.at[j], arr.at[10 + j], to_opp)

        def total_over(self, j):
            ref = self.final(1, j)
            return remote(ref, ref, ars.at[5 + j], arr.at[15 + j], to_opp)

        def total_out(self, near, j):
            i = 5 * near + j
            ref = self.final(near, j)
            return remote(ref, ref, ars.at[10 + i], arr.at[i], to_mate)

        def total_pair(self, near, j):
            i = 20 + 3 * near + j
            ref = self.final(near, j)
            return remote(ref, ref, ars.at[i], arr.at[i], to_y)

        def trade(self, j):
            return remote(hp.at[self.piece(1, j)], self.come_pair(j), ars.at[20 + j], arr.at[20 + j], to_y)

        def start(self, lo, hi):
            @pl.when(outer)
            def _():
                for j in range(lo, hi):
                    for near in range(2):
                        self.send_in(near, j).start()

        def collect(self, j):
            @pl.when(inner)
            def _():
                self.send_in(0, j).wait_recv()
                p = self.piece(0, j)
                hp[p] = (hp[p].astype(F32) + self.come_out(0, j)[...].astype(F32)).astype(BF)
                self.send_over(j).start()

        def total(self, j):
            @pl.when(inner)
            def _():
                self.send_in(1, j).wait_recv()
                self.send_over(j).wait_recv()
                p = self.piece(1, j)
                tot = hp[p].astype(F32) + self.come_out(1, j)[...].astype(F32) + self.come_opp(j)[...].astype(F32)
                if self.whole:
                    hp[p] = tot.astype(BF)
                    self.trade(j).start()
                else:
                    self.final(1, j)[...] = tot.astype(BF)
                    self.total_out(1, j).start()
                    self.total_over(j).start()

            if not self.whole:
                @pl.when(outer)
                def _():
                    self.total_out(1, j).wait_recv()

                self.total_pair(1, j).start()

        def settle(self, j):
            @pl.when(inner)
            def _():
                self.trade(j).wait_recv()
                tot = hp[self.piece(1, j)].astype(F32) + self.come_pair(j)[...].astype(F32)
                self.final(1, j)[...] = tot.astype(BF)
                self.total_out(1, j).start()
                self.total_over(j).start()

            self.across(1, j)

        def across(self, near, j):
            @pl.when(outer)
            def _():
                self.total_out(near, j).wait_recv()

        def passed(self, j):
            @pl.when(inner)
            def _():
                self.total_over(j).wait_recv()
                self.total_out(0, j).start()

            if not self.whole:
                @pl.when(outer)
                def _():
                    self.total_out(0, j).wait_recv()

                self.total_pair(0, j).start()
            else:
                self.across(0, j)

        def last(self):
            for near in range(2):
                for j in range(self.n):
                    self.total_pair(near, j).wait_recv()

        def finish(self):
            for j in range(self.n):
                @pl.when(outer)
                def _():
                    self.send_in(0, j).wait_send()
                    self.send_in(1, j).wait_send()

                @pl.when(inner)
                def _():
                    self.send_over(j).wait_send()
                    self.total_over(j).wait_send()
                    if self.whole:
                        self.trade(j).wait_send()

                mine = par == j % 2
                for near in range(2):
                    pl.when(inner)(self.total_out(near, j).wait_send)
                    if not self.whole:
                        self.total_pair(near, j).wait_send()

    first, second = Line(False), Line(True)

    @pl.when(s == 0)
    def _():
        late[0].start()
        for c in y_copies(0) + late:
            c.wait_recv()
        for m in range(micro):
            for i in range(3):
                y_late(i, m).wait_recv()
        q_tot = 0.0
        v_tot = 0.0
        for m in range(micro):
            q_tot += dot(nrm_t[:, cols(m)], gpt[par, m], 1, 1) + dot(ynrm[:, cols(m)], ygpt[0, m], 1, 1)
            v_tot += dot(nrm_t[v_part, cols(m)], gpt[2, m], 1, 1) + dot(ynrm[v_part, cols(m)], ygpt[1, m], 1, 1)
        hp[q_rows] = q_tot.astype(BF)
        hp[v_rows] = v_tot.astype(BF)
        hp[m_rows] = (dot(mtb[...], gbr[:, m_part]) + dot(ymtb[...], ygbr[...])).astype(BF)
        hp[s_rows] = (sb[par].astype(F32) + ysb[...].astype(F32)).astype(BF)
        first.start(0, first.n)

    @pl.when(s == 1)
    def _():
        for q in range(3):
            tot = dot(nrm_t[:, cols(0)], gpt[q, 0], 1, 1)
            for m in range(1, micro):
                tot += dot(nrm_t[:, cols(m)], gpt[q, m], 1, 1)
            hp[pl.ds(q * width, width)] = tot.astype(BF)
        tot = dot(mtb[...], gbr[...]).astype(BF)
        for c in range(cut):
            hp[pl.ds(3 * width + c * hw, hw)] = tot[:, c * hw : (c + 1) * hw]
        for e in range(2):
            hp[pl.ds(3 * width + cut * hw + e * hs, hs)] = sb[e]
        gd0.crossed()
        nm1.mixed_on(1)
        second.start(0, 2)
        gd0.mixed_on(1)
        nm1.mixed_on(2)
        gd0.mixed_on(2)
        nm1.mixed_on(3)
        gd1.mixed_take()

    @pl.when(s == 0)
    def _():
        nm0.mixed_take()
        for k in range(1, GROUP):
            gd0.take(lax.rem(g + k, GROUP))
        first.collect(0)

    @pl.when(s == 1)
    def _():
        second.collect(0)
        gd0.mixed_on(3)
        second.start(2, second.n)
        nm1.mixed_take()

    def up_copy(t):
        return local(wup.at[:, hid_rows(t)], up_o.at[:, hid_rows(t)], tsem.at[0, t])

    def down_copy(t):
        return local(wdown.at[hid_rows(t)], down_o.at[hid_rows(t)], tsem.at[1, t])

    for i in range(GROUP):
        for m in range(micro):
            nm_cat[:, pl.ds(i * span + m * rows, rows)] = nm_all[m, i]

    def tile_grads(t):
        hr = hid_rows(t)
        wu = wupt[hr]
        wd = wdown[hr]
        for i in range(GROUP):
            sl = slot(i)
            h, slope = gelu_both(dot(wu, nm_cat[:, sl]))
            hb[:, sl] = h.astype(BF)
            gb[:, sl] = (dot(wd, gd_all[sl], 1, 1) * slope).astype(BF)
        wup[:, hr] = dot(nm_cat[...], gb[...], 1, 1).astype(BF)
        wdown[hr] = dot(hb[...], gd_all[...]).astype(BF)
        up_copy(t).start()
        down_copy(t).start()

    plan = {
        (0, True): {
            0: [("total", 0)],
            1: [("collect", 1)],
            2: [("collect", 2), ("passed", 0), ("total", 1)],
            3: [("total", 2), ("passed", 1)],
            4: [("passed", 2)],
        },
        (0, False): {
            2: [("total", 0)],
            3: [("passed", 0), ("total", 1)],
            4: [("total", 2), ("passed", 1)],
            5: [("passed", 2)],
        },
        (1, True): {
            0: [("total", 0), ("collect", 1)],
            1: [("total", 1)],
            2: [("settle", 0)],
            3: [("collect", 2), ("settle", 1)],
            4: [("collect", 3), ("passed", 0), ("total", 2)],
            5: [
                ("collect", 4),
                ("passed", 1),
                ("total", 3),
                ("settle", 2),
                ("total", 4),
                ("settle", 3),
                ("passed", 2),
                ("settle", 4),
                ("passed", 3),
                ("passed", 4),
            ],
        },
        (1, False): {5: [(f, j) for j in range(5) for f in ("settle", "passed")]},
    }

    def one_tile(t, carry):
        tile_grads(t)
        for (layer, within), when in plan.items():
            for at, steps in when.items():
                @pl.when((s == layer) & (inner if within else outer) & (t == at))
                def _():
                    for name, *j in steps:
                        getattr((first, second)[layer], name)(*j)

        return carry

    lax.fori_loop(0, tiles, one_tile, 0)

    @pl.when(s == 0)
    def _():
        first.last()

    def outs_of(layer, out_copy):
        if layer == 1:
            out_copy(fin.at[pl.ds(0, 3 * width)], qkv_o)
            for c in range(cut):
                out_copy(fin.at[pl.ds(3 * width + c * hw, hw)], mix_o.at[:, pl.ds(c * hw, hw)])
            for e in range(2):
                out_copy(fin.at[pl.ds(3 * width + cut * hw + e * hs, hs)], small_o.at[e])
            return
        for e in range(2):
            at = e * part_rows
            out_copy(fin.at[pl.ds(at, width)], qkv_o.at[pl.ds(e * width, width)])
            at += width
            out_copy(fin.at[pl.ds(at, width // 2)], qkv_o.at[pl.ds(2 * width + e * (width // 2), width // 2)])
            at += width // 2
            out_copy(fin.at[pl.ds(at, hw)], mix_o.at[:, pl.ds(e * hw, hw)])
            at += hw
            out_copy(fin.at[pl.ds(at, hs)], small_o.at[e])

    def ended(layer):
        mine = []

        def keep(src, dst):
            c = local(src, dst, osem.at[2 * micro + 2 + len(mine)])
            c.start()
            mine.append(c)

        outs_of(layer, keep)
        for c in mine:
            c.wait()

    for t in range(tiles):
        up_copy(t).wait()
        down_copy(t).wait()

    @pl.when(s == 0)
    def _():
        ended(0)

    @pl.when(s == 1)
    def _():
        ended(1)

    @pl.when(s == 0)
    def _():
        for m in range(micro):
            first_x(m).wait_send()
            c_copy(0, m).wait_send()

    @pl.when(s == 1)
    def _():
        for m in range(micro):
            first_c(m).wait_send()
            c_copy(1, m).wait_send()

    for e in range(4):
        for m in range(micro):
            x_swap(e, m).wait_send()
    @pl.when(s == 0)
    def _():
        nm0.mixed_sent()

    @pl.when(s == 1)
    def _():
        gd1.mixed_sent()
        gd0.mixed_sent()
        nm1.mixed_sent()

    @pl.when(s == 0)
    def _():
        for c in y_copies(0) + y_copies(1):
            c.wait_send()
        for m in range(micro):
            for i in range(3):
                y_late(i, m).wait_send()
        first.finish()

    @pl.when(s == 1)
    def _():
        second.finish()

    for m in range(micro):
        act_copy(m).wait()
        ig_copy(m).wait()


def widen(act, ig, qkv, mix, small, up, down, act_o, ig_o, qkv_o, mix_o, feat_o, g1_o, g2_o, up_o, down_o, sem_in, sem_out, *bufs):
    hs = feat_o.shape[2]
    hw = mix.shape[0]
    cut = mix.shape[1] // hw
    blocks = []
    for src, dst, step in ((up, up_o, 192), (down, down_o, 384), (qkv, qkv_o, 768), (mix, mix_o, 192)):
        for lo in range(0, src.shape[0], step):
            if dst is qkv_o:
                blocks.append((src.at[pl.ds(lo, step)], dst.at[0, lo // step]))
            else:
                blocks.append((src.at[pl.ds(lo, step)], dst.at[0, pl.ds(lo, step)]))
    half = len(blocks)
    narrow, wide = bufs[:half], bufs[half : 2 * half]
    small_v, feat_v, g1_v, g2_v, act_v, ig_v = bufs[2 * half :]
    first = [
        pltpu.make_async_copy(src, dst, sem_in.at[half + i])
        for i, (src, dst) in enumerate(((small, small_v), (act, act_v), (ig, ig_v)))
    ]
    for c in first:
        c.start()
    loads = [pltpu.make_async_copy(b[0], n, sem_in.at[i]) for i, (b, n) in enumerate(zip(blocks, narrow))]
    for c in loads:
        c.start()
    outs = []

    def put(src, dst, i):
        c = pltpu.make_async_copy(src, dst, sem_out.at[i])
        c.start()
        outs.append(c)

    for c in first:
        c.wait()
    put(act_v, act_o, half + 3)
    put(ig_v, ig_o, half + 4)
    for h in range(feat_v.shape[1]):
        feat_v[0, h] = small_v[0, pl.ds(0, hs), pl.ds(h * hs, hs)].astype(F32)
    for c in range(cut):
        cs = pl.ds(c * hw, hw)
        g1_v[:, cs] = small_v[1, pl.ds(0, 16)].astype(F32)[c : c + 1]
        g2_v[:, cs] = small_v[1, pl.ds(0, 16)].astype(F32)[cut + c : cut + c + 1]
    put(feat_v, feat_o, half)
    put(g1_v, g1_o, half + 1)
    put(g2_v, g2_o, half + 2)
    for i, (b, n, w) in enumerate(zip(blocks, narrow, wide)):
        loads[i].wait()
        w[...] = n[...].astype(F32)
        put(w, b[1], i)
    for c in outs:
        c.wait()


def on_device(x, cot, starts, lengths, gain1, wqkv, fmap, wmix, gain2, wup, wdown):
    micro, half, width = x.shape
    rows = 2 * half
    span = micro * rows
    heads, hs = fmap.shape[1], fmap.shape[2]
    hw = heads * hs
    ff = wup.shape[2]
    cut = width // hw
    part_rows = width + width // 2 + hw + hs
    f, b = F32, BF
    vm = pltpu.VMEM
    dma = pltpu.SemaphoreType.DMA
    out = lambda shape, t=b: jax.ShapeDtypeStruct(shape, t)
    act, ig, qkv, mix, small, up, down = pl.pallas_call(
        kernel,
        out_shape=[
            out((1, micro, half, width)),
            out((1, micro, half, width)),
            out((3 * width, hw)),
            out((hw, width)),
            out((2, hs, hw)),
            out((width, ff)),
            out((ff, width)),
        ],
        in_specs=[ANY, ANY, SM, SM, VM, ANY, VM, ANY, VM, ANY, ANY],
        out_specs=[ANY] * 7,
        scratch_shapes=[
            vm((3, width, hw), b),
            vm((hw, width), b),
            vm((width, ff), b),
            vm((ff, width), b),
            vm((ff, width), b),
            vm((micro, rows, width), b),
            vm((span, width), b),
            vm((micro, rows, rows), f),
            vm((width, span), b),
            vm((3, hw, span), b),
            vm((micro, rows, hw), b),
            vm((micro, heads, 2 * hs, rows), b),
            vm((micro, heads, 2 * hs, rows), b),
            vm((micro, heads, rows, rows), b),
            vm((micro, hw, rows), f),
            vm((hw, span), b),
            vm((micro, heads, 8, rows), f),
            vm((micro, rows, width), f),
            vm((micro, GROUP, width, rows), b),
            vm((width, GROUP * span), b),
            vm((GROUP * span, width), b),
            vm((256, GROUP * span), b),
            vm((256, GROUP * span), b),
            vm((micro, rows, ff), b),
            vm((micro, rows, width), f),
            vm((micro, rows, width), f),
            vm((micro, rows, width), b),
            vm((span, width), b),
            vm((span, width), b),
            vm((2, hw, span), b),
            vm((3, micro, hw, rows), b),
            vm((2, micro, 8, width), f),
            vm((4, micro, rows, width), b),
            vm((4, micro, rows, width), b),
            vm((width, span), b),
            vm((hw, span), b),
            vm((2, micro, hw, rows), b),
            vm((span, hw), b),
            vm((2, hs, hw), b),
            vm((hs, hw), b),
            vm((2 * part_rows, hw), b),
            vm((2 * part_rows, hw), b),
            vm((10, 464, hw), b),
            vm((5, 464, hw), b),
            vm((5, 464, hw), b),
            vm((LINE, span, width), b),
            vm((micro, 2, LINE, rows, width), b),
            dma((4 + micro,)),
            dma((5 * micro,)),
            dma((5 * micro,)),
            dma((2 * micro,)),
            dma((2 * micro,)),
            dma((2, micro, GROUP)),
            dma((micro, LINE)),
            dma((3, 12 * (micro - 1) + 20)),
            dma((micro, GROUP)),
            dma((3 + 3 * micro,)),
            dma((3 + 3 * micro,)),
            dma((26,)),
            dma((26,)),
            dma((2 * micro + 10,)),
            dma((2, ff // 256)),
        ],
        compiler_params=pltpu.CompilerParams(
            collective_id=0, has_side_effects=True, vmem_limit_bytes=60 * 1024 * 1024
        ),
    )(x, cot, starts, lengths, gain1, wqkv, fmap, wmix, gain2, wup, wdown)

    n = lax.axis_size("dp")
    if n > GROUP:
        same_place = [[i + j * GROUP for j in range(n // GROUP)] for i in range(GROUP)]
        qkv, mix, small, up, down = lax.psum((qkv, mix, small, up, down), "dp", axis_index_groups=same_place)

    shapes = []
    for a, step in ((up, 192), (down, 384), (qkv, 768), (mix, 192)):
        shapes += [(step, a.shape[1])] * (a.shape[0] // step)
    outs = [(1, 3, width, hw), (1, hw, width), (1, heads, hs, hs), (1, width), (1, width), (1, width, ff), (1, ff, width)]
    act, ig, qkv, mix, features, g1, g2, up, down = pl.pallas_call(
        widen,
        out_shape=[out(act.shape), out(ig.shape)] + [out(o, f) for o in outs],
        in_specs=[ANY] * 7,
        out_specs=[ANY] * 9,
        scratch_shapes=[dma((len(shapes) + 3,)), dma((len(shapes) + 5,))]
        + [vm(o, b) for o in shapes]
        + [vm(o, f) for o in shapes]
        + [vm(small.shape, b), vm(outs[2], f), vm(outs[3], f), vm(outs[4], f), vm(act.shape, b), vm(ig.shape, b)],
        compiler_params=pltpu.CompilerParams(vmem_limit_bytes=60 * 1024 * 1024),
    )(act, ig, qkv, mix, small, up, down)
    return act, ig, g1, qkv, features, mix, g2, up, down


def solution(mesh):
    in_specs = (
        P(None, ("dp", "mp"), None),
        P(None, ("dp", "mp"), None),
        P(None, "dp", None),
        P(None, "dp", None),
        P("section", None),
        P("section", None, None, "mp"),
        P("section", "mp", None, None),
        P("section", "mp", None),
        P("section", None),
        P("section", None, "mp"),
        P("section", "mp", None),
    )
    out_specs = (
        P("section", None, ("dp", "mp"), None),
        P("section", None, ("dp", "mp"), None),
        P("section", None),
        P("section", None, None, "mp"),
        P("section", "mp", None, None),
        P("section", "mp", None),
        P("section", None),
        P("section", None, "mp"),
        P("section", "mp", None),
    )
    return jax.shard_map(
        on_device, mesh=mesh, in_specs=in_specs, out_specs=out_specs, check_vma=False
    )
```

```python
import functools

import functools

import jax
import jax.numpy as jnp
from jax import lax
from jax.experimental import pallas as pl
from jax.experimental.pallas import tpu as pltpu
from jax.sharding import PartitionSpec as P

STRETCH = 64
GROUP = 8
LINE = 4
MESH = pl.DeviceIdType.MESH
BF = jnp.bfloat16
F32 = jnp.float32
ANY = pl.BlockSpec(memory_space=pl.ANY)
VM = pl.BlockSpec(memory_space=pltpu.VMEM)
SM = pl.BlockSpec(memory_space=pltpu.SMEM)


def dot(a, b, ca=1, cb=0):
    return lax.dot_general(a, b, (((ca,), (cb,)), ((), ())), preferred_element_type=F32)


def normed(v):
    mean = jnp.mean(v, axis=1, keepdims=True)
    c = v - mean
    rstd = lax.rsqrt(jnp.mean(c * c, axis=1, keepdims=True) + 1e-05)
    return c * rstd, rstd


def norm_back(grad, gain, xhat, rstd):
    t = grad * gain
    mean_t = jnp.mean(t, axis=1, keepdims=True)
    mean_tx = jnp.mean(t * xhat, axis=1, keepdims=True)
    return rstd * (t - mean_t - xhat * mean_tx)


def gelu_both(x):
    k = 0.7978845608028654
    x2 = x * x
    g = 0.5 + 0.5 * jnp.tanh(x * (k + (k * 0.044715) * x2))
    h = x * g
    return h, g + h * (1.0 - g) * (2.0 * k + (6.0 * k * 0.044715) * x2)


def both_softmax(logit):
    up = jnp.exp(logit - jnp.max(logit, axis=0, keepdims=True))
    down = jnp.exp(jnp.min(logit, axis=0, keepdims=True) - logit)
    up = up * (1.0 / jnp.sum(up, axis=0, keepdims=True))
    down = down * (1.0 / jnp.sum(down, axis=0, keepdims=True))
    return jnp.concatenate([up.astype(BF), down.astype(BF)], axis=0)


def softmax_back(grad, feat):
    n = grad.shape[0] // 2
    g = grad * feat.astype(F32)
    p = feat.astype(F32)
    one = g[:n] - p[:n] * jnp.sum(g[:n], axis=0, keepdims=True)
    two = g[n:] - p[n:] * jnp.sum(g[n:], axis=0, keepdims=True)
    return one - two


def kernel(
    x_in, cot, starts, lengths, gain1, wqkv_h, fmap, wmix_h, gain2, up_h, down_h,
    act_o, ig_o, qkv_o, mix_o, small_o, up_o, down_o,
    wqkv, wmix, wup, wdown, wupt, rin, gin, mask,
    nrm_t, pt, vnat, qf, kf, st, mt, mtb, den_s, rmid, nm_all, nm_cat, gd_all, hb, gb, gp, part_f, rout, act, igv,
    gbr, gqk, gpt, gacc, sbuf, rbuf,
    ynrm, ymtb, ygpt, ygbr, sb, ysb, hp, fin, from_out, from_opp, from_pair, hgd, hgw,
    lsem, xs, xr, cs, cr, la, ha, fs, hws, ys, yr, ars, arr, osem, tsem,
):
    s = lax.axis_index("section")
    d = lax.axis_index("dp")
    xi = lax.axis_index("mp")
    micro, half, width = x_in.shape
    rows = 2 * half
    span = micro * rows
    heads, hs = fmap.shape[1], fmap.shape[2]
    hw = heads * hs
    ff = up_h.shape[2]
    g = lax.rem(d, GROUP)
    base = d - g
    pos = lax.div(g, 2)
    par = lax.rem(g, 2)
    to_x = (s, d, 1 - xi)
    to_c = (1 - s, d, xi)
    to_y = (s, base + pos * 2 + 1 - par, xi)
    outer = (pos == 0) | (pos == LINE - 1)
    inner = (pos > 0) & (pos < LINE - 1)
    side = lax.div(pos, 2)
    to_mate = (s, base + (side * 4 + 1 - pos) * 2 + par, xi)
    to_opp = (s, base + (LINE - 1 - pos) * 2 + par, xi)

    def other_core(to):
        return (1 - s,) + to[1:]

    def other_core(to):
        return (1 - s,) + to[1:]

    def at(core, p, q):
        return (core, base + p * 2 + q, xi)

    def greet(act):
        for to in (to_x, to_c, to_y, other_core(to_y)):
            act(to)
        pl.when(pos < LINE - 1)(lambda: act(at(s, pos + 1, par)))
        pl.when(pos > 0)(lambda: act(at(s, pos - 1, par)))

    def local(src, dst, sem):
        return pltpu.make_async_copy(src, dst, sem)

    def remote(src, dst, ss, rs, to):
        return pltpu.make_async_remote_copy(
            src_ref=src, dst_ref=dst, send_sem=ss, recv_sem=rs, device_id=to, device_id_type=MESH
        )

    def cols(m):
        return pl.ds(pl.multiple_of(m * rows, rows), rows)

    def each_micro(f):
        lax.fori_loop(0, micro, lambda m, c: (f(m), c)[1], 0)

    def slot(i):
        return pl.ds(pl.multiple_of(i * span, span), span)

    own_x = local(x_in, rin.at[:, pl.ds(0, half)], lsem.at[4])
    own_c = [local(cot.at[m], gin.at[pl.ds(m * rows, half)], lsem.at[4 + m]) for m in range(micro)]
    loads = [
        local(wqkv_h.at[0], wqkv, lsem.at[0]),
        local(wmix_h.at[0], wmix, lsem.at[1]),
        local(up_h.at[0], wup, lsem.at[2]),
        local(down_h.at[0], wdown, lsem.at[3]),
    ]

    def first_x(m):
        return remote(rin.at[m, pl.ds(0, half)], rin.at[m, pl.ds(half, half)], xs.at[m], xr.at[m], to_x)

    def first_c(m):
        src, dst = gin.at[pl.ds(m * rows, half)], gin.at[pl.ds(m * rows + half, half)]
        return remote(src, dst, xs.at[m], xr.at[m], to_x)

    @pl.when(s == 0)
    def _():
        own_x.start()

    @pl.when(s == 1)
    def _():
        for c in own_c:
            c.start()

    for c in loads:
        c.start()

    barrier = pltpu.get_barrier_semaphore()
    greet(lambda to: pl.semaphore_signal(barrier, inc=1, device_id=to, device_id_type=MESH))
    pl.semaphore_wait(barrier, jnp.where(inner, 6, 5))

    @pl.when(s == 0)
    def _():
        own_x.wait()
        first_x(0).start()

    jj = lax.broadcasted_iota(jnp.int32, (rows, rows), 0)
    ii = lax.broadcasted_iota(jnp.int32, (rows, rows), 1)
    j_own, i_own = jj < half, ii < half
    inside = ((j_own == i_own) & (jj <= ii)).astype(F32)
    own_first = jnp.where(xi == 0, 1.0, 0.0)
    across = jnp.where(j_own & ~i_own, own_first, jnp.where(i_own & ~j_own, 1.0 - own_first, 0.0))
    slots = starts.shape[2]
    for m in range(micro):
        n0 = jnp.int32(0)
        n1 = jnp.int32(0)
        for j in range(slots):
            n0 += jnp.where(starts[m, 0, j] <= 0, 1, 0)
            n1 += jnp.where(starts[m, 0, j] <= STRETCH, 1, 0)
        same = jnp.where(n0 == n1, 1.0, 0.0)
        mask[m] = inside + across * same

    def live_of(m, part):
        block = xi if part == 0 else 1 - xi
        begin = jnp.int32(0)
        for j in range(slots):
            begin = jnp.where(starts[m, 0, j] <= block * STRETCH, jnp.maximum(begin, starts[m, 0, j]), begin)
        length = jnp.int32(0)
        for j in range(slots):
            length += jnp.where(starts[m, 0, j] == begin, lengths[m, 0, j], 0)
        row = block * STRETCH + lax.broadcasted_iota(jnp.int32, (half, width), 0)
        return (row - begin < length).astype(F32)

    def block_of(kind, p, q, m):
        i = p * 2 + q
        return nm_all.at[m, i] if kind == 0 else gd_all.at[pl.ds(pl.multiple_of(i * span + m * rows, rows), rows)]

    class Gather:
        def __init__(self, kind, layer, plain):
            self.kind, self.layer = kind, layer
            self.plain = plain
            self.same = (kind, layer) != (1, 0)
            self.core = layer if self.same else 1

        def held(self, p, m):
            if self.same:
                return block_of(self.kind, p, par, m)
            return hgd.at[p, cols(m)]

        def arrived(self, p, q, m):
            return la.at[self.kind, m, p * 2 + q]

        def arrival(self, p, m):
            return self.arrived(p, par, m) if self.same else ha.at[m, p]

        def sending(self, i, m):
            return fs.at[self.kind if self.same else 2, i + 12 * m]

        def to(self, core, p, q):
            return (core, base + p * 2 + q, xi)

        def step(self, i, p, q, m, ref):
            return remote(ref, self.held(p, m), self.sending(i, m), self.arrival(p, m), self.to(self.core, q, par))

        def pair(self, i, p, m, ref):
            to = self.to(self.layer, pos, 1 - par)
            return remote(ref, block_of(self.kind, p, par, m), self.sending(i, m), self.arrived(p, par, m), to)

        def home(self, i, p, m, ref):
            to = self.to(self.layer, pos, par)
            return remote(ref, block_of(self.kind, p, par, m), self.sending(i, m), self.arrived(p, par, m), to)

        def moves(self, way, j, m):
            p = pos - j if way == 0 else pos + j
            i = 3 * p
            if j == 0:
                ref = self.held(p, m) if self.same else igv.at[cols(m)]
                return [
                    (self.step(i, p, pos + 1, m, ref), pos < LINE - 1),
                    (self.step(i + 1, p, pos - 1, m, ref), pos > 0),
                    (self.pair(i + 2, p, m, ref), None),
                ]
            ref = self.held(p, m)
            came = (p >= 0) if way == 0 else (p < LINE)
            q = pos + 1 if way == 0 else pos - 1
            goes = (q < LINE) if way == 0 else (q >= 0)
            out = [(self.step(i, p, q, m, ref), came & goes), (self.pair(i + 1, p, m, ref), came)]
            if not self.same:
                out.append((self.home(i + 2, p, m, ref), came))
            return out

        def each(self, way, j, m, what):
            for copy, when in self.moves(way, j, m):
                if when is None:
                    what(copy)
                else:
                    pl.when(when)(functools.partial(what, copy))

        def own(self, m):
            self.each(0, 0, m, lambda c: c.start())

        def pass_on(self, j, m):
            for way in range(2):
                p = pos - j if way == 0 else pos + j

                @pl.when((p >= 0) if way == 0 else (p < LINE))
                def _():
                    self.step(0, p, pos, m, self.held(p, m)).wait_recv()

                self.each(way, j, m, lambda c: c.start())

        def wide_held(self, p, q, m):
            return block_of(self.kind, p, q, m) if self.same else hgw.at[m, q, p]

        def wide_arrived(self, p, q, m):
            return self.arrived(p, q, m) if self.same else hws.at[m, p * 2 + q]

        def wide(self, j, q, m):
            out = []
            for way in range(2):
                p = pos - j if way == 0 else pos + j
                t = pos + 1 if way == 0 else pos - 1
                when = (t < LINE) if way == 0 else (t >= 0)
                came = (p >= 0) if way == 0 else (p < LINE)
                ref = self.wide_held(p, q, m)
                if j == 0 and q is par and not self.same:
                    ref = igv.at[cols(m)]
                i = 4 * (0 if q is par else 1) + p
                if j == 0 and way == 1:
                    i = 16 + (0 if q is par else 1)
                copy = remote(
                    ref, self.wide_held(p, q, m), self.sending(i, m), self.wide_arrived(p, q, m), self.to(self.core, t, par)
                )
                out.append((copy, when if j == 0 else when & came))
            return out

        def wide_home(self, way, j, q, m):
            p = pos - j if way == 0 else pos + j
            i = 8 + 4 * (0 if q is par else 1) + p
            to = self.to(self.layer, pos, par)
            return remote(self.wide_held(p, q, m), block_of(self.kind, p, q, m), self.sending(i, m), self.arrived(p, q, m), to)

        def wide_pair(self, m):
            ref = block_of(self.kind, pos, par, m) if self.same else igv.at[cols(m)]
            to = self.to(self.core, pos, 1 - par)
            return remote(ref, self.wide_held(pos, par, m), self.sending(18, m), self.wide_arrived(pos, par, m), to)

        def wide_own(self, m):
            for copy, when in self.wide(0, par, m):
                pl.when(when)(copy.start)
            self.wide_pair(m).start()

        def wide_on(self, j, m):
            for q in (par, 1 - par):
                if j == 0 and q is par:
                    continue
                if j == 0:
                    ref = self.wide_held(pos, q, m)
                    remote(ref, ref, fs.at[0, 0], self.wide_arrived(pos, q, m), to_y).wait_recv()
                    if not self.same:
                        self.wide_home(0, 0, q, m).start()
                for way, (copy, when) in enumerate(self.wide(j, q, m)):
                    if j > 0:
                        if self.same:
                            pl.when(when)(copy.wait_recv)
                        else:
                            p = pos - j if way == 0 else pos + j
                            came = (p >= 0) if way == 0 else (p < LINE)
                            pl.when(came)(copy.wait_recv)
                            pl.when(came)(self.wide_home(way, j, q, m).start)
                    pl.when(when)(copy.start)

        def mixed_own(self, m):
            if isinstance(m, int):
                (self.own if m < self.plain else self.wide_own)(m)
                return
            for n in range(micro):
                pl.when(m == n)(functools.partial(self.mixed_own, n))

        def crossed(self):
            for m in range(self.plain, micro):
                self.wide_on(0, m)

        def mixed_on(self, j):
            for m in range(micro):
                (self.pass_on if m < self.plain else self.wide_on)(j, m)

        def mixed_take(self):
            for m in range(self.plain):
                for k in range(LINE):
                    p = lax.rem(pos + k, LINE)
                    ref = block_of(self.kind, p, 1 - par, m)
                    remote(ref, ref, fs.at[0, 0], self.arrived(p, 1 - par, m), to_y).wait_recv()
            for way in range(2):
                for j in range(1, LINE):
                    p = pos - j if way == 0 else pos + j
                    last = (p >= 0) & (pos == LINE - 1) if way == 0 else (p < LINE) & (pos == 0)
                    for m in range(self.plain, micro):
                        for q in (par, 1 - par):
                            ref = block_of(self.kind, p, q, m)
                            come = remote(ref, ref, fs.at[0, 0], self.arrived(p, q, m), to_y)
                            pl.when(last)(come.wait_recv)

        def mixed_sent(self):
            for m in range(self.plain):
                self.each(0, 0, m, lambda c: c.wait_send())
                for way in range(2):
                    for j in range(1, LINE):
                        self.each(way, j, m, lambda c: c.wait_send())
            for m in range(self.plain, micro):
                self.wide_pair(m).wait_send()
                for j in range(LINE):
                    for q in (par, 1 - par):
                        for way, (copy, when) in enumerate(self.wide(j, q, m)):
                            pl.when(when)(copy.wait_send)
                            if self.same or j == 0 and (q is par or way == 1):
                                continue
                            p = pos - j if way == 0 else pos + j
                            came = (p >= 0) if way == 0 else (p < LINE)
                            pl.when(came)(self.wide_home(way, j, q, m).wait_send)

        def take(self, i):
            p, q = lax.div(i, 2), lax.rem(i, 2)
            for m in range(micro):
                ref = block_of(self.kind, p, q, m)
                remote(ref, ref, fs.at[0, 0], self.arrived(p, q, m), to_y).wait_recv()

    nm0, nm1, gd0, gd1 = Gather(0, 0, 1), Gather(0, 1, 1), Gather(1, 0, 1), Gather(1, 1, 1)

    def grad_rows(m):
        return pl.ds(pl.multiple_of(g * span + m * rows, rows), rows)

    @pl.when(s == 0)
    def _():
        first_x(0).wait_recv()
        for m in range(1, micro):
            first_x(m).start()

    @pl.when(s == 1)
    def _():
        for c in loads:
            c.wait()
        wupt[...] = wup[...].T
        for c in own_c:
            c.wait()
        for m in range(micro):
            first_c(m).start()
        for m in range(micro):
            first_c(m).wait_recv()
            for part in range(2):
                pr = pl.ds(m * rows + part * half, half)
                to = pl.ds(pl.multiple_of(g * span + m * rows + part * half, half), half)
                gd_all[to] = (gin[pr].astype(F32) * live_of(m, part)).astype(BF)
            gd1.mixed_own(m)
        gd1.crossed()
        gd1.mixed_on(1)

    def x_swap(e, m):
        i = (1 + e) * micro + m
        return remote(sbuf.at[e, m], rbuf.at[e, m], xs.at[i], xr.at[i], to_x)

    def give(e, m, part):
        part = part.astype(BF)
        sbuf[e, m, pl.ds(0, half)] = part[half:]
        sbuf[e, m, pl.ds(half, half)] = part[:half]
        x_swap(e, m).start()

    def c_copy(e, m):
        i = e * micro + m
        src, dst = ((act.at[m], rin.at[m]), (igv.at[cols(m)], gin.at[cols(m)]))[e]
        return remote(src, dst, cs.at[i], cr.at[i], to_c)

    def y_copies(when):
        out = []
        if when == 0:
            pairs = [(nrm_t, ynrm), (mtb, ymtb)]
        else:
            pairs = [(sb.at[1 - par], ysb)]
        for i, (src, dst) in enumerate(pairs):
            j = 2 * when + i
            out.append(remote(src, dst, ys.at[j], yr.at[j], to_y))
        return out

    def y_late(i, m):
        src, dst = (
            (gpt.at[1 - par, m], ygpt.at[0, m]),
            (gpt.at[2, m], ygpt.at[1, m]),
            (gbr.at[cols(m), pl.ds(pl.multiple_of((1 - par) * hw, 128), hw)], ygbr.at[cols(m)]),
        )[i]
        j = 3 + i * micro + m
        return remote(src, dst, ys.at[j], yr.at[j], to_y)

    def mixer_forward(m):
        @pl.when((s == 0) & (m > 0))
        def _():
            first_x(m).wait_recv()

        @pl.when(s == 1)
        def _():
            c_copy(0, m).wait_recv()

        @pl.when((s == 0) & (m == 0))
        def _():
            loads[0].wait()
            loads[1].wait()

        r = rin[m].astype(F32)
        n = (normed(r)[0] * gain1[...]).astype(BF)
        pts = []
        for q in range(3):
            p = dot(n, wqkv[q]).astype(BF)
            if q == 2:
                vnat[m] = p
            p = p.T
            pt[q, :, cols(m)] = p
            pts.append([p[h * hs : (h + 1) * hs] for h in range(heads)])
        nrm_t[:, cols(m)] = n.T
        ws = [fmap[0, h] for h in range(heads)]
        logits = [[dot(ws[h], pts[q][h], 0, 0) for h in range(heads)] for q in range(2)]
        feats = [[both_softmax(x) for x in logits[q]] for q in range(2)]
        scores = [dot(feats[1][h], feats[0][h], 0, 0) for h in range(heads)]
        keep = mask[m]
        scores = [x * keep for x in scores]
        dens = [1.0 / jnp.sum(x, axis=0, keepdims=True) for x in scores]
        scores = [x.astype(BF) for x in scores]
        mixed = [dot(pts[2][h], scores[h]) * dens[h] for h in range(heads)]
        for h in range(heads):
            hr = pl.ds(h * hs, hs)
            qf[m, h] = feats[0][h]
            kf[m, h] = feats[1][h]
            st[m, h] = scores[h]
            den_s[m, h] = jnp.broadcast_to(dens[h], (8, rows))
            mt[m, hr] = mixed[h]
            mtb[hr, cols(m)] = mixed[h].astype(BF)
        part = dot(mtb[:, cols(m)].T, wmix[...])
        give(0, m, part)
        rmid[m] = r + part

    def ffn_forward(m):
        x_swap(0, m).wait_recv()
        r = rmid[m] + rbuf[0, m].astype(F32)
        rmid[m] = r
        n = (normed(r)[0] * gain2[...]).astype(BF)
        nm_all[m, g] = n.T

        @pl.when(s == 0)
        def _():
            nm0.mixed_own(m)

        @pl.when(s == 1)
        def _():
            nm1.mixed_own(m)

        @pl.when((s == 0) & (m == 0))
        def _():
            loads[2].wait()
            loads[3].wait()

        h, slope = gelu_both(dot(n, wup[...]))
        h = h.astype(BF)
        gp[m] = slope.astype(BF)
        part = dot(h, wdown[...])
        give(1, m, part)
        rout[m] = r + part

    def act_copy(m):
        return local(act.at[m, pl.ds(0, half)], act_o.at[0, m], osem.at[m])

    def ig_copy(m):
        return local(igv.at[pl.ds(pl.multiple_of(m * rows, half), half)], ig_o.at[0, m], osem.at[micro + m])

    def end_forward(m):
        x_swap(1, m).wait_recv()
        act[m] = (rout[m] + rbuf[1, m].astype(F32)).astype(BF)

        @pl.when(s == 0)
        def _():
            c_copy(0, m).start()

        act_copy(m).start()

    each_micro(mixer_forward)
    @pl.when(s == 0)
    def _():
        for c in y_copies(0):
            c.start()

    @pl.when(s == 1)
    def _():
        gd1.mixed_on(2)

    each_micro(ffn_forward)
    @pl.when(s == 0)
    def _():
        each_micro(end_forward)


    tile = hb.shape[0]
    tiles = ff // tile

    def hid_rows(t):
        return pl.ds(pl.multiple_of(t * tile, tile), tile)

    @pl.when(s == 0)
    def _():
        wupt[...] = wup[...].T

        nm0.crossed()
        for j in range(1, LINE - 1):
            nm0.mixed_on(j)

    def ffn_back(m):
        @pl.when(s == 0)
        def _():
            c_copy(1, m).wait_recv()
            gd_all[grad_rows(m)] = gin[cols(m)]

        gd = gd_all[grad_rows(m)]
        gpre = (dot(gd, wdown[...], 1, 1) * gp[m].astype(F32)).astype(BF)
        part = dot(gpre, wup[...], 1, 1)
        give(2, m, part)
        part_f[m] = part

    def mixer_back(m):
        @pl.when((s == 1) & (m == 1))
        def _():
            nm1.crossed()

        x_swap(2, m).wait_recv()
        gn = part_f[m] + rbuf[2, m].astype(F32)
        xhat, rstd = normed(rmid[m])
        gacc[1, m] = jnp.broadcast_to(jnp.sum(gn * xhat, axis=0, keepdims=True), (8, width))
        gm = gd_all[grad_rows(m)].astype(F32) + norm_back(gn, gain2[...], xhat, rstd)
        rmid[m] = gm
        gb_ = gm.astype(BF)
        gbr[cols(m)] = gb_

        @pl.when(s == 0)
        def _():
            y_late(2, m).start()

        gmt = dot(wmix[...], gb_, 1, 1).astype(BF)
        dens = [den_s[m, h, pl.ds(0, 1)] for h in range(heads)]
        gos = [gmt[h * hs : (h + 1) * hs].astype(F32) for h in range(heads)]
        gdens = [-jnp.sum(gos[h] * mt[m, pl.ds(h * hs, hs)], axis=0, keepdims=True) * dens[h] for h in range(heads)]
        gnums = [(gos[h] * dens[h]).astype(BF) for h in range(heads)]
        pad = jnp.zeros_like(gnums[0])
        wide = [jnp.concatenate([x, pad] if h % 2 == 0 else [pad, x], axis=0) for h, x in enumerate(gnums)]
        gsts = [dot(vnat[m, :, pl.ds((h // 2) * 2 * hs, 2 * hs)], wide[h]) + gdens[h] for h in range(heads)]
        keep = mask[m]
        gsts = [(x * keep).astype(BF) for x in gsts]
        qfs = [qf[m, h] for h in range(heads)]
        kfs = [kf[m, h] for h in range(heads)]
        gqf = [dot(kfs[h], gsts[h]) for h in range(heads)]
        gkf = [dot(qfs[h], gsts[h], 1, 1) for h in range(heads)]
        gvs = [dot(gnums[h], st[m, h], 1, 1).astype(BF) for h in range(heads)]
        gql = [softmax_back(gqf[h], qfs[h]).astype(BF) for h in range(heads)]
        gkl = [softmax_back(gkf[h], kfs[h]).astype(BF) for h in range(heads)]
        gpq = [dot(fmap[0, h], gql[h]).astype(BF) for h in range(heads)]
        gpk = [dot(fmap[0, h], gkl[h]).astype(BF) for h in range(heads)]
        for h in range(heads):
            hr = pl.ds(h * hs, hs)
            gqk[0, hr, cols(m)] = gql[h]
            gqk[1, hr, cols(m)] = gkl[h]
            gpt[0, m, hr] = gpq[h]
            gpt[1, m, hr] = gpk[h]
            gpt[2, m, hr] = gvs[h]

        @pl.when(s == 0)
        def _():
            y_late(0, m).start()
            y_late(1, m).start()

        gnt = dot(wqkv[0], gpt[0, m]) + dot(wqkv[1], gpt[1, m]) + dot(wqkv[2], gpt[2, m])
        part = gnt.T
        give(3, m, part)
        part_f[m] = part

    def end_back(m):
        x_swap(3, m).wait_recv()
        gn = part_f[m] + rbuf[3, m].astype(F32)
        xhat, rstd = normed(rin[m].astype(F32))
        gacc[0, m] = jnp.broadcast_to(jnp.sum(gn * xhat, axis=0, keepdims=True), (8, width))
        igv[cols(m)] = (rmid[m] + norm_back(gn, gain1[...], xhat, rstd)).astype(BF)

        @pl.when(s == 1)
        def _():
            c_copy(1, m).start()
            gd0.mixed_own(m)

        ig_copy(m).start()

    each_micro(ffn_back)

    @pl.when(s == 0)
    def _():
        nm0.mixed_on(LINE - 1)

    @pl.when(s == 1)
    def _():
        each_micro(end_forward)
        gd1.mixed_on(3)

    each_micro(mixer_back)

    late = y_copies(1)

    cut = width // hw
    q_rows = pl.ds(0, width)
    v_rows = pl.ds(width, width // 2)
    m_rows = pl.ds(width + width // 2, hw)
    s_rows = pl.ds(width + width // 2 + hw, hs)
    v_part = pl.ds(pl.multiple_of(par * (width // 2), 16), width // 2)
    m_part = pl.ds(pl.multiple_of(par * hw, 128), hw)

    left = lax.broadcasted_iota(jnp.int32, (hs, 2 * hs), 1) < hs
    for p in range(heads // 2):
        pr = pl.ds(p * 2 * hs, 2 * hs)
        tot = dot(pt[0, pr], gqk[0, pr], 1, 1) + dot(pt[1, pr], gqk[1, pr], 1, 1)
        sb[0, :, pr] = jnp.where(left, tot[:hs], tot[hs:]).astype(BF)

    each_micro(end_back)

    row = lax.broadcasted_iota(jnp.int32, (hs, hw), 0)
    block = jnp.zeros((hs, hw), F32)
    for e in range(2):
        tot = gacc[e, 0, pl.ds(0, 1)]
        for m in range(1, micro):
            tot += gacc[e, m, pl.ds(0, 1)]
        for c in range(cut):
            block = jnp.where(row == e * cut + c, tot[:, c * hw : (c + 1) * hw], block)
    sb[1] = block.astype(BF)

    part_rows = hp.shape[0] // 2
    most = 464

    def ends_of(total, shares):
        out = [0]
        for share in shares:
            out.append(min(total, -(-total * share // 1600) * 16))
        return out

    WHOLE, HALF = (25, 50, 75, 88, 100), (50, 76, 100)

    class Line:
        def __init__(self, whole):
            self.whole = whole
            self.ends = ends_of(part_rows * (2 if whole else 1) // 2, WHOLE if whole else HALF)
            self.n = len(self.ends) - 1

        def size(self, j):
            return self.ends[j + 1] - self.ends[j]

        def at(self, near, j):
            group = side if near else 1 - side
            return group * self.ends[-1] + self.ends[j]

        def piece(self, near, j):
            return pl.ds(pl.multiple_of(self.at(near, j), 16), self.size(j))

        def final(self, near, j):
            first_row = self.at(near, j) + (0 if self.whole else par * part_rows)
            return fin.at[pl.ds(pl.multiple_of(first_row, 16), self.size(j))]

        def come_out(self, near, j):
            return from_out.at[5 * near + j, pl.ds(0, self.size(j))]

        def come_opp(self, j):
            return from_opp.at[j, pl.ds(0, self.size(j))]

        def come_pair(self, j):
            return from_pair.at[j, pl.ds(0, self.size(j))]

        def send_in(self, near, j):
            i = 5 * near + j
            return remote(hp.at[self.piece(near, j)], self.come_out(near, j), ars.at[i], arr.at[i], to_mate)

        def send_over(self, j):
            return remote(hp.at[self.piece(0, j)], self.come_opp(j), ars.at[j], arr.at[10 + j], to_opp)

        def total_over(self, j):
            ref = self.final(1, j)
            return remote(ref, ref, ars.at[5 + j], arr.at[15 + j], to_opp)

        def total_out(self, near, j):
            i = 5 * near + j
            ref = self.final(near, j)
            return remote(ref, ref, ars.at[10 + i], arr.at[i], to_mate)

        def total_pair(self, near, j):
            i = 20 + 3 * near + j
            ref = self.final(near, j)
            return remote(ref, ref, ars.at[i], arr.at[i], to_y)

        def trade(self, j):
            return remote(hp.at[self.piece(1, j)], self.come_pair(j), ars.at[20 + j], arr.at[20 + j], to_y)

        def start(self, lo, hi):
            @pl.when(outer)
            def _():
                for j in range(lo, hi):
                    for near in range(2):
                        self.send_in(near, j).start()

        def collect(self, j):
            @pl.when(inner)
            def _():
                self.send_in(0, j).wait_recv()
                p = self.piece(0, j)
                hp[p] = (hp[p].astype(F32) + self.come_out(0, j)[...].astype(F32)).astype(BF)
                self.send_over(j).start()

        def total(self, j):
            @pl.when(inner)
            def _():
                self.send_in(1, j).wait_recv()
                self.send_over(j).wait_recv()
                p = self.piece(1, j)
                tot = hp[p].astype(F32) + self.come_out(1, j)[...].astype(F32) + self.come_opp(j)[...].astype(F32)
                if self.whole:
                    hp[p] = tot.astype(BF)
                    self.trade(j).start()
                else:
                    self.final(1, j)[...] = tot.astype(BF)
                    self.total_out(1, j).start()
                    self.total_over(j).start()

            if not self.whole:
                @pl.when(outer)
                def _():
                    self.total_out(1, j).wait_recv()

                self.total_pair(1, j).start()

        def settle(self, j):
            @pl.when(inner)
            def _():
                self.trade(j).wait_recv()
                tot = hp[self.piece(1, j)].astype(F32) + self.come_pair(j)[...].astype(F32)
                self.final(1, j)[...] = tot.astype(BF)
                self.total_out(1, j).start()
                self.total_over(j).start()

            self.across(1, j)

        def across(self, near, j):
            @pl.when(outer)
            def _():
                self.total_out(near, j).wait_recv()

        def passed(self, j):
            @pl.when(inner)
            def _():
                self.total_over(j).wait_recv()
                self.total_out(0, j).start()

            if not self.whole:
                @pl.when(outer)
                def _():
                    self.total_out(0, j).wait_recv()

                self.total_pair(0, j).start()
            else:
                self.across(0, j)

        def ready(self):
            rows_done = [(0, self.ends[3]), (self.ends[-1], min(self.ends[-1] + self.ends[3], 3 * width))]
            return [
                local(fin.at[pl.ds(lo, hi - lo)], qkv_o.at[pl.ds(lo, hi - lo)], osem.at[2 * micro + 8 + i])
                for i, (lo, hi) in enumerate(rows_done)
            ]

        def early(self):
            for c in self.ready():
                c.start()

        def last(self):
            for near in range(2):
                for j in range(self.n):
                    self.total_pair(near, j).wait_recv()

        def finish(self):
            for j in range(self.n):
                @pl.when(outer)
                def _():
                    self.send_in(0, j).wait_send()
                    self.send_in(1, j).wait_send()

                @pl.when(inner)
                def _():
                    self.send_over(j).wait_send()
                    self.total_over(j).wait_send()
                    if self.whole:
                        self.trade(j).wait_send()

                mine = par == j % 2
                for near in range(2):
                    pl.when(inner)(self.total_out(near, j).wait_send)
                    if not self.whole:
                        self.total_pair(near, j).wait_send()

    first, second = Line(False), Line(True)

    @pl.when(s == 0)
    def _():
        late[0].start()
        for c in y_copies(0) + late:
            c.wait_recv()
        for m in range(micro):
            for i in range(3):
                y_late(i, m).wait_recv()
        q_tot = 0.0
        v_tot = 0.0
        for m in range(micro):
            q_tot += dot(nrm_t[:, cols(m)], gpt[par, m], 1, 1) + dot(ynrm[:, cols(m)], ygpt[0, m], 1, 1)
            v_tot += dot(nrm_t[v_part, cols(m)], gpt[2, m], 1, 1) + dot(ynrm[v_part, cols(m)], ygpt[1, m], 1, 1)
        hp[q_rows] = q_tot.astype(BF)
        hp[v_rows] = v_tot.astype(BF)
        hp[m_rows] = (dot(mtb[...], gbr[:, m_part]) + dot(ymtb[...], ygbr[...])).astype(BF)
        hp[s_rows] = (sb[par].astype(F32) + ysb[...].astype(F32)).astype(BF)
        first.start(0, first.n)

    @pl.when(s == 1)
    def _():
        for q in range(3):
            tot = dot(nrm_t[:, cols(0)], gpt[q, 0], 1, 1)
            for m in range(1, micro):
                tot += dot(nrm_t[:, cols(m)], gpt[q, m], 1, 1)
            hp[pl.ds(q * width, width)] = tot.astype(BF)
        tot = dot(mtb[...], gbr[...]).astype(BF)
        for c in range(cut):
            hp[pl.ds(3 * width + c * hw, hw)] = tot[:, c * hw : (c + 1) * hw]
        for e in range(2):
            hp[pl.ds(3 * width + cut * hw + e * hs, hs)] = sb[e]
        gd0.crossed()
        nm1.mixed_on(1)
        second.start(0, 2)
        gd0.mixed_on(1)
        nm1.mixed_on(2)
        gd0.mixed_on(2)
        nm1.mixed_on(3)
        gd1.mixed_take()

    @pl.when(s == 0)
    def _():
        nm0.mixed_take()
        for k in range(1, GROUP):
            gd0.take(lax.rem(g + k, GROUP))
        first.collect(0)

    @pl.when(s == 1)
    def _():
        second.collect(0)
        gd0.mixed_on(3)
        second.start(2, second.n)
        nm1.mixed_take()

    def up_copy(t):
        return local(wup.at[:, hid_rows(t)], up_o.at[:, hid_rows(t)], tsem.at[0, t])

    def down_copy(t):
        return local(wdown.at[hid_rows(t)], down_o.at[hid_rows(t)], tsem.at[1, t])

    for i in range(GROUP):
        for m in range(micro):
            nm_cat[:, pl.ds(i * span + m * rows, rows)] = nm_all[m, i]

    def tile_grads(t):
        hr = hid_rows(t)
        wu = wupt[hr]
        wd = wdown[hr]
        for i in range(GROUP):
            sl = slot(i)
            h, slope = gelu_both(dot(wu, nm_cat[:, sl]))
            hb[:, sl] = h.astype(BF)
            gb[:, sl] = (dot(wd, gd_all[sl], 1, 1) * slope).astype(BF)
        wup[:, hr] = dot(nm_cat[...], gb[...], 1, 1).astype(BF)
        wdown[hr] = dot(hb[...], gd_all[...]).astype(BF)
        up_copy(t).start()
        down_copy(t).start()

    plan = {
        (0, True): {
            0: [("total", 0)],
            1: [("collect", 1)],
            2: [("collect", 2), ("passed", 0), ("total", 1)],
            3: [("total", 2), ("passed", 1)],
            4: [("passed", 2)],
        },
        (0, False): {
            2: [("total", 0)],
            3: [("passed", 0), ("total", 1)],
            4: [("total", 2), ("passed", 1)],
            5: [("passed", 2)],
        },
        (1, True): {
            0: [("total", 0), ("collect", 1)],
            1: [("total", 1)],
            2: [("settle", 0)],
            3: [("collect", 2), ("settle", 1)],
            4: [("collect", 3), ("passed", 0), ("total", 2)],
            5: [
                ("collect", 4),
                ("passed", 1),
                ("total", 3),
                ("settle", 2),
                ("total", 4),
                ("settle", 3),
                ("passed", 2),
                ("early",),
                ("settle", 4),
                ("passed", 3),
                ("passed", 4),
            ],
        },
        (1, False): {
            5: [(f, j) for j in range(3) for f in ("settle", "passed")]
            + [("early",)]
            + [(f, j) for j in range(3, 5) for f in ("settle", "passed")]
        },
    }

    def one_tile(t, carry):
        tile_grads(t)
        for (layer, within), when in plan.items():
            for at, steps in when.items():
                @pl.when((s == layer) & (inner if within else outer) & (t == at))
                def _():
                    for name, *j in steps:
                        getattr((first, second)[layer], name)(*j)

        return carry

    lax.fori_loop(0, tiles, one_tile, 0)

    @pl.when(s == 0)
    def _():
        first.last()

    def outs_of(layer, out_copy):
        if layer == 1:
            lo, hi = second.ends[3], second.ends[-1]
            out_copy(fin.at[pl.ds(lo, hi - lo)], qkv_o.at[pl.ds(lo, hi - lo)])
            for c in range(cut):
                out_copy(fin.at[pl.ds(3 * width + c * hw, hw)], mix_o.at[:, pl.ds(c * hw, hw)])
            for e in range(2):
                out_copy(fin.at[pl.ds(3 * width + cut * hw + e * hs, hs)], small_o.at[e])
            return
        for e in range(2):
            at = e * part_rows
            out_copy(fin.at[pl.ds(at, width)], qkv_o.at[pl.ds(e * width, width)])
            at += width
            out_copy(fin.at[pl.ds(at, width // 2)], qkv_o.at[pl.ds(2 * width + e * (width // 2), width // 2)])
            at += width // 2
            out_copy(fin.at[pl.ds(at, hw)], mix_o.at[:, pl.ds(e * hw, hw)])
            at += hw
            out_copy(fin.at[pl.ds(at, hs)], small_o.at[e])

    def ended(layer):
        mine = []

        def keep(src, dst):
            c = local(src, dst, osem.at[2 * micro + 2 + len(mine)])
            c.start()
            mine.append(c)

        outs_of(layer, keep)
        for c in mine:
            c.wait()

    for t in range(tiles):
        up_copy(t).wait()
        down_copy(t).wait()

    @pl.when(s == 0)
    def _():
        ended(0)

    @pl.when(s == 1)
    def _():
        ended(1)
        for c in second.ready():
            c.wait()

    @pl.when(s == 0)
    def _():
        for m in range(micro):
            first_x(m).wait_send()
            c_copy(0, m).wait_send()

    @pl.when(s == 1)
    def _():
        for m in range(micro):
            first_c(m).wait_send()
            c_copy(1, m).wait_send()

    for e in range(4):
        for m in range(micro):
            x_swap(e, m).wait_send()
    @pl.when(s == 0)
    def _():
        nm0.mixed_sent()

    @pl.when(s == 1)
    def _():
        gd1.mixed_sent()
        gd0.mixed_sent()
        nm1.mixed_sent()

    @pl.when(s == 0)
    def _():
        for c in y_copies(0) + y_copies(1):
            c.wait_send()
        for m in range(micro):
            for i in range(3):
                y_late(i, m).wait_send()
        first.finish()

    @pl.when(s == 1)
    def _():
        second.finish()

    for m in range(micro):
        act_copy(m).wait()
        ig_copy(m).wait()


def widen(act, ig, qkv, mix, small, up, down, act_o, ig_o, qkv_o, mix_o, feat_o, g1_o, g2_o, up_o, down_o, sem_in, sem_out, *bufs):
    hs = feat_o.shape[2]
    hw = mix.shape[0]
    cut = mix.shape[1] // hw
    blocks = []
    for src, dst, step in ((up, up_o, 192), (down, down_o, 384), (qkv, qkv_o, 768), (mix, mix_o, 192)):
        for lo in range(0, src.shape[0], step):
            if dst is qkv_o:
                blocks.append((src.at[pl.ds(lo, step)], dst.at[0, lo // step]))
            else:
                blocks.append((src.at[pl.ds(lo, step)], dst.at[0, pl.ds(lo, step)]))
    half = len(blocks)
    narrow, wide = bufs[:half], bufs[half : 2 * half]
    small_v, feat_v, g1_v, g2_v, act_v, ig_v = bufs[2 * half :]
    first = [
        pltpu.make_async_copy(src, dst, sem_in.at[half + i])
        for i, (src, dst) in enumerate(((small, small_v), (act, act_v), (ig, ig_v)))
    ]
    for c in first:
        c.start()
    loads = [pltpu.make_async_copy(b[0], n, sem_in.at[i]) for i, (b, n) in enumerate(zip(blocks, narrow))]
    for c in loads:
        c.start()
    outs = []

    def put(src, dst, i):
        c = pltpu.make_async_copy(src, dst, sem_out.at[i])
        c.start()
        outs.append(c)

    for c in first:
        c.wait()
    put(act_v, act_o, half + 3)
    put(ig_v, ig_o, half + 4)
    for h in range(feat_v.shape[1]):
        feat_v[0, h] = small_v[0, pl.ds(0, hs), pl.ds(h * hs, hs)].astype(F32)
    for c in range(cut):
        cs = pl.ds(c * hw, hw)
        g1_v[:, cs] = small_v[1, pl.ds(0, 16)].astype(F32)[c : c + 1]
        g2_v[:, cs] = small_v[1, pl.ds(0, 16)].astype(F32)[cut + c : cut + c + 1]
    put(feat_v, feat_o, half)
    put(g1_v, g1_o, half + 1)
    put(g2_v, g2_o, half + 2)
    for i, (b, n, w) in enumerate(zip(blocks, narrow, wide)):
        loads[i].wait()
        w[...] = n[...].astype(F32)
        put(w, b[1], i)
    for c in outs:
        c.wait()


def on_device(x, cot, starts, lengths, gain1, wqkv, fmap, wmix, gain2, wup, wdown):
    micro, half, width = x.shape
    rows = 2 * half
    span = micro * rows
    heads, hs = fmap.shape[1], fmap.shape[2]
    hw = heads * hs
    ff = wup.shape[2]
    cut = width // hw
    part_rows = width + width // 2 + hw + hs
    f, b = F32, BF
    vm = pltpu.VMEM
    dma = pltpu.SemaphoreType.DMA
    out = lambda shape, t=b: jax.ShapeDtypeStruct(shape, t)
    act, ig, qkv, mix, small, up, down = pl.pallas_call(
        kernel,
        out_shape=[
            out((1, micro, half, width)),
            out((1, micro, half, width)),
            out((3 * width, hw)),
            out((hw, width)),
            out((2, hs, hw)),
            out((width, ff)),
            out((ff, width)),
        ],
        in_specs=[ANY, ANY, SM, SM, VM, ANY, VM, ANY, VM, ANY, ANY],
        out_specs=[ANY] * 7,
        scratch_shapes=[
            vm((3, width, hw), b),
            vm((hw, width), b),
            vm((width, ff), b),
            vm((ff, width), b),
            vm((ff, width), b),
            vm((micro, rows, width), b),
            vm((span, width), b),
            vm((micro, rows, rows), f),
            vm((width, span), b),
            vm((3, hw, span), b),
            vm((micro, rows, hw), b),
            vm((micro, heads, 2 * hs, rows), b),
            vm((micro, heads, 2 * hs, rows), b),
            vm((micro, heads, rows, rows), b),
            vm((micro, hw, rows), f),
            vm((hw, span), b),
            vm((micro, heads, 8, rows), f),
            vm((micro, rows, width), f),
            vm((micro, GROUP, width, rows), b),
            vm((width, GROUP * span), b),
            vm((GROUP * span, width), b),
            vm((256, GROUP * span), b),
            vm((256, GROUP * span), b),
            vm((micro, rows, ff), b),
            vm((micro, rows, width), f),
            vm((micro, rows, width), f),
            vm((micro, rows, width), b),
            vm((span, width), b),
            vm((span, width), b),
            vm((2, hw, span), b),
            vm((3, micro, hw, rows), b),
            vm((2, micro, 8, width), f),
            vm((4, micro, rows, width), b),
            vm((4, micro, rows, width), b),
            vm((width, span), b),
            vm((hw, span), b),
            vm((2, micro, hw, rows), b),
            vm((span, hw), b),
            vm((2, hs, hw), b),
            vm((hs, hw), b),
            vm((2 * part_rows, hw), b),
            vm((2 * part_rows, hw), b),
            vm((10, 464, hw), b),
            vm((5, 464, hw), b),
            vm((5, 464, hw), b),
            vm((LINE, span, width), b),
            vm((micro, 2, LINE, rows, width), b),
            dma((4 + micro,)),
            dma((5 * micro,)),
            dma((5 * micro,)),
            dma((2 * micro,)),
            dma((2 * micro,)),
            dma((2, micro, GROUP)),
            dma((micro, LINE)),
            dma((3, 12 * (micro - 1) + 20)),
            dma((micro, GROUP)),
            dma((3 + 3 * micro,)),
            dma((3 + 3 * micro,)),
            dma((26,)),
            dma((26,)),
            dma((2 * micro + 10,)),
            dma((2, ff // 256)),
        ],
        compiler_params=pltpu.CompilerParams(
            collective_id=0, has_side_effects=True, vmem_limit_bytes=60 * 1024 * 1024
        ),
    )(x, cot, starts, lengths, gain1, wqkv, fmap, wmix, gain2, wup, wdown)

    n = lax.axis_size("dp")
    if n > GROUP:
        same_place = [[i + j * GROUP for j in range(n // GROUP)] for i in range(GROUP)]
        qkv, mix, small, up, down = lax.psum((qkv, mix, small, up, down), "dp", axis_index_groups=same_place)

    shapes = []
    for a, step in ((up, 192), (down, 384), (qkv, 768), (mix, 192)):
        shapes += [(step, a.shape[1])] * (a.shape[0] // step)
    outs = [(1, 3, width, hw), (1, hw, width), (1, heads, hs, hs), (1, width), (1, width), (1, width, ff), (1, ff, width)]
    act, ig, qkv, mix, features, g1, g2, up, down = pl.pallas_call(
        widen,
        out_shape=[out(act.shape), out(ig.shape)] + [out(o, f) for o in outs],
        in_specs=[ANY] * 7,
        out_specs=[ANY] * 9,
        scratch_shapes=[dma((len(shapes) + 3,)), dma((len(shapes) + 5,))]
        + [vm(o, b) for o in shapes]
        + [vm(o, f) for o in shapes]
        + [vm(small.shape, b), vm(outs[2], f), vm(outs[3], f), vm(outs[4], f), vm(act.shape, b), vm(ig.shape, b)],
        compiler_params=pltpu.CompilerParams(vmem_limit_bytes=60 * 1024 * 1024),
    )(act, ig, qkv, mix, small, up, down)
    return act, ig, g1, qkv, features, mix, g2, up, down


def solution(mesh):
    in_specs = (
        P(None, ("dp", "mp"), None),
        P(None, ("dp", "mp"), None),
        P(None, "dp", None),
        P(None, "dp", None),
        P("section", None),
        P("section", None, None, "mp"),
        P("section", "mp", None, None),
        P("section", "mp", None),
        P("section", None),
        P("section", None, "mp"),
        P("section", "mp", None),
    )
    out_specs = (
        P("section", None, ("dp", "mp"), None),
        P("section", None, ("dp", "mp"), None),
        P("section", None),
        P("section", None, None, "mp"),
        P("section", "mp", None, None),
        P("section", "mp", None),
        P("section", None),
        P("section", None, "mp"),
        P("section", "mp", None),
    )
    return jax.shard_map(
        on_device, mesh=mesh, in_specs=in_specs, out_specs=out_specs, check_vma=False
    )
```
